32 devices in a mesh: dp: 8 (over z, x), fsdp: 4 (over y, core).
Axes of the slice: x: 2, y: 2, z: 4, core: 2. Of those that a mesh axis runs over, the one named last changes fastest.
Arguments:
- tokens: bfloat16 [16384, 1024], P(('dp', 'fsdp')), may hold values from -6 to 6
- mask_positions: int32 [32, 80], P(('dp', 'fsdp')), may hold values from 0 to 511, as said below
- mask_counts: int32 [32], P(('dp', 'fsdp')), may hold values from 1 to 80, as said below
- replace_ids: int32 [32, 80], P(('dp', 'fsdp')), may hold values from 0 to 29
- cotangent: bfloat16 [16384, 1024], P(('dp', 'fsdp')), may hold values from -6 to 6
- replace_table: bfloat16 [30, 1024], replicated, may hold values from -6 to 6
- w_qkv: bfloat16 [1024, 3072], P('fsdp'), may hold values from -0.25 to 0.25
- b_qv: bfloat16 [2048], P('fsdp'), may hold values from -3 to 3
- w_out: bfloat16 [1024, 1024], P('fsdp'), may hold values from -0.75 to 0.75
- b_out: bfloat16 [1024], P('fsdp'), may hold values from -3 to 3
- norm1_gain: bfloat16 [1024], P('fsdp'), may hold values from 0.5 to 1.5
- norm1_bias: bfloat16 [1024], P('fsdp'), may hold values from -3 to 3
- w_up: bfloat16 [1024, 4096], P('fsdp'), may hold values from -0.1875 to 0.1875
- b_up: bfloat16 [4096], P('fsdp'), may hold values from -3 to 3
- w_down: bfloat16 [4096, 1024], P('fsdp'), may hold values from -0.09375 to 0.09375
- b_down: bfloat16 [1024], P('fsdp'), may hold values from -3 to 3
- norm2_gain: bfloat16 [1024], P('fsdp'), may hold values from 0.5 to 1.5
- norm2_bias: bfloat16 [1024], P('fsdp'), may hold values from -3 to 3
Outputs:
- final: bfloat16 [16384, 1024], P(('dp', 'fsdp'))
- token_grad: float32 [16384, 1024], P(('dp', 'fsdp'))
- table_grad: float32 [30, 1024], replicated
- w_qkv_grad: float32 [1024, 3072], P('fsdp')
- b_qv_grad: float32 [2048], P('fsdp')
- w_out_grad: float32 [1024, 1024], P('fsdp')
- b_out_grad: float32 [1024], P('fsdp')
- norm1_gain_grad: float32 [1024], P('fsdp')
- norm1_bias_grad: float32 [1024], P('fsdp')
- w_up_grad: float32 [1024, 4096], P('fsdp')
- b_up_grad: float32 [4096], P('fsdp')
- w_down_grad: float32 [4096, 1024], P('fsdp')
- b_down_grad: float32 [1024], P('fsdp')
- norm2_gain_grad: float32 [1024], P('fsdp')
- norm2_bias_grad: float32 [1024], P('fsdp')
The draws below stay inside these ranges and needn't reach their ends.
Inputs may be any that keep to these rules, and one draw needn't show every extreme that they name: `mask_positions`: the 80 positions of one sequence are all different. `mask_counts`: some sequence uses all 80 slots.
All inputs are finite; a program needn't handle non-finite values.
Results may differ from the reference program's by a relative error of at most 0.035.
Values may be sent and summed in bfloat16 or wider, within the bound.
A program may use at most 168 MiB of HBM per device.

```python
import math
import jax
import jax.numpy as jnp
from jax import lax

D = 1024
HEADS = 16
FF = 4096
VOCAB = 30
LENGTH = 512
MASKS = 80
SEQS = 32
TOKENS = 16384


def draw_mask_positions(key, part):
    key = jax.random.fold_in(key, 11)
    keys = jax.random.split(key, SEQS)
    return jax.vmap(lambda single: jax.random.permutation(single, LENGTH)[:MASKS])(keys).astype(jnp.int32)


def draw_mask_counts(key, part):
    key = jax.random.fold_in(key, 23)
    first, second = jax.random.split(key)
    counts = jax.random.randint(first, (SEQS,), 1, MASKS + 1)
    fullest = jax.random.randint(second, (), 0, SEQS)
    return counts.at[fullest].set(MASKS).astype(jnp.int32)


def with_ends(values, stream_key, least, high):
    index_at = [jax.random.randint(jax.random.fold_in(stream_key, axis), (), 0, length) for axis, length in enumerate(values.shape)]
    longest = values.shape.index(max(values.shape))
    beside = index_at[:longest] + [(index_at[longest] + 1) % values.shape[longest]] + index_at[longest + 1:]
    return values.at[tuple(index_at)].set(least).at[tuple(beside)].set(high)


def block_scale(rng, extent, pieces, low, top_value):
    factor_of = 1.0
    for position, shards_of in pieces:
        heights = jax.random.uniform(jax.random.fold_in(jax.random.fold_in(rng, 6), position), (shards_of,), jnp.float32, low / len(pieces), top_value / len(pieces))
        factor_of = factor_of * jnp.repeat(jnp.exp(heights), extent[position] // shards_of).reshape((-1,) + (1,) * (len(extent) - 1 - position))
    return factor_of


def normal_values(stream_key, shape, scale, limit, cuts=(), kind=jnp.bfloat16):
    array = scale * jax.random.normal(stream_key, shape, jnp.float32)
    if cuts:
        array = array * block_scale(stream_key, shape, cuts, -0.22, 0.18)
    return jnp.clip(array, -limit, limit).astype(kind)


def setup_inputs(seed: int = 0) -> dict:
    arg_keys = jax.random.split(jax.random.key(seed), 19)
    tokens = normal_values(arg_keys[0], (TOKENS, D), 1.0, 6.0, ((0, 32),))
    mask_positions = draw_mask_positions(jax.random.fold_in(arg_keys[18], 71), 0)
    mask_counts = draw_mask_counts(jax.random.fold_in(arg_keys[18], 71), 0)
    replace_ids = with_ends(jax.random.randint(arg_keys[3], (SEQS, MASKS), 0, VOCAB), jax.random.fold_in(arg_keys[3], 1), 0, VOCAB - 1).astype(jnp.int32)
    cotangent = normal_values(arg_keys[4], (TOKENS, D), 1.0, 6.0, ((0, 32),))
    replace_table = normal_values(arg_keys[5], (VOCAB, D), 1.0, 6.0)
    w_qkv = normal_values(arg_keys[6], (D, 3 * D), (D // 2) ** -0.5, 0.25, ((0, 4),))
    b_qv = normal_values(arg_keys[7], (2 * D,), 0.5, 3.0, ((0, 4),))
    w_out = normal_values(arg_keys[8], (D, D), (D // 16) ** -0.5, 0.75, ((0, 4),))
    b_out = normal_values(arg_keys[9], (D,), 0.5, 3.0, ((0, 4),))
    norm1_gain = jnp.clip(0.5 + 1.0 * jax.random.uniform(arg_keys[10], (D,), jnp.float32) ** block_scale(arg_keys[10], (D,), ((0, 4),), -0.2, 0.2), 0.5, 1.5).astype(jnp.bfloat16)
    norm1_bias = normal_values(arg_keys[11], (D,), 0.5, 3.0, ((0, 4),))
    w_up = normal_values(arg_keys[12], (D, FF), D ** -0.5, 0.1875, ((0, 4),))
    b_up = normal_values(arg_keys[13], (FF,), 0.5, 3.0, ((0, 4),))
    w_down = normal_values(arg_keys[14], (FF, D), FF ** -0.5, 0.09375, ((0, 4),))
    b_down = normal_values(arg_keys[15], (D,), 0.5, 3.0, ((0, 4),))
    norm2_gain = jnp.clip(0.5 + 1.0 * jax.random.uniform(arg_keys[16], (D,), jnp.float32) ** block_scale(arg_keys[16], (D,), ((0, 4),), -0.2, 0.2), 0.5, 1.5).astype(jnp.bfloat16)
    norm2_bias = normal_values(arg_keys[17], (D,), 0.5, 3.0, ((0, 4),))
    return dict(tokens=tokens, mask_positions=mask_positions, mask_counts=mask_counts, replace_ids=replace_ids, cotangent=cotangent, replace_table=replace_table, w_qkv=w_qkv, b_qv=b_qv, w_out=w_out, b_out=b_out, norm1_gain=norm1_gain, norm1_bias=norm1_bias, w_up=w_up, b_up=b_up, w_down=w_down, b_down=b_down, norm2_gain=norm2_gain, norm2_bias=norm2_bias)


@jax.custom_vjp
def low(v):
    return lax.optimization_barrier(v.astype(jnp.bfloat16)).astype(jnp.float32)

@jax.custom_vjp
def reduced_backward(v):
    return v

def low_keep(v):
    return (low(v), None)

def low_pass(kept, grad):
    return (grad,)

def back_keep(v):
    return (v, None)

def back_low(kept, grad):
    return (low(grad),)
low.defvjp(low_keep, low_pass)
reduced_backward.defvjp(back_keep, back_low)
EPSILON = 1e-05

def product(left, right):
    return jnp.dot(left, right, precision=lax.Precision.HIGHEST, preferred_element_type=jnp.float32)

def normalize(values, gain, shift):
    mean = lax.optimization_barrier(jnp.mean(values, axis=-1, keepdims=True))
    centred = values - mean
    spread = lax.optimization_barrier(jnp.mean(centred * centred, axis=-1, keepdims=True))
    return centred * lax.rsqrt(spread + EPSILON) * gain + shift

def encoder_layer(rows, params):
    w_qkv, b_qv, w_out, b_out, gain_one, bias_one, w_up, b_up, w_down, b_down, gain_two, bias_two = params
    width = rows.shape[-1]
    head_dim = width // HEADS
    scale = 1.0 / math.sqrt(head_dim)
    joined = product(low(rows), w_qkv)
    query = reduced_backward(low((joined[..., :width] + b_qv[:width]) * scale))
    keyed = reduced_backward(low(joined[..., width:2 * width]))
    weighted_values = reduced_backward(low(joined[..., 2 * width:] + b_qv[width:]))
    shape = rows.shape[:-1] + (HEADS, head_dim)
    query = query.reshape(shape)
    keyed = keyed.reshape(shape)
    weighted_values = weighted_values.reshape(shape)
    scores = reduced_backward(jnp.einsum('gqhe,gkhe->ghqk', query, keyed, precision=lax.Precision.HIGHEST))
    probs = low(jax.nn.softmax(scores, axis=-1))
    mixed = jnp.einsum('ghqk,gkhe->gqhe', probs, weighted_values, precision=lax.Precision.HIGHEST).reshape(rows.shape)
    mixed = reduced_backward(low(mixed))
    branch = reduced_backward(product(mixed, w_out) + b_out)
    hidden = normalize(rows + branch, gain_one, bias_one)
    inner = reduced_backward(product(low(hidden), w_up) + b_up)
    active = low(jax.nn.gelu(inner, approximate=False))
    output = reduced_backward(product(active, w_down) + b_down)
    return normalize(hidden + output, gain_two, bias_two)

def apply_masks(rows, positions, counts, ids, table):
    slots = jnp.arange(positions.shape[-1]).astype(jnp.int32)
    used = (slots[None, :] < counts[:, None]).astype(jnp.float32)
    places = jnp.arange(rows.shape[1]).astype(jnp.int32)
    position_onehot = (positions[:, :, None] == places[None, None, :]).astype(jnp.float32) * used[:, :, None]
    entries = jnp.arange(table.shape[0]).astype(jnp.int32)
    vocab_hot = (ids[:, :, None] == entries[None, None, :]).astype(jnp.float32)
    chosen = jnp.einsum('gmv,vd->gmd', vocab_hot, table, precision=lax.Precision.HIGHEST)
    placed = jnp.einsum('gml,gmd->gld', position_onehot, chosen, precision=lax.Precision.HIGHEST)
    hit = lax.optimization_barrier(jnp.sum(position_onehot, axis=1))
    return rows * (1.0 - hit[:, :, None]) + placed

def reference(tokens, mask_positions, mask_counts, replace_ids, cotangent, replace_table, w_qkv, b_qv, w_out, b_out, norm1_gain, norm1_bias, w_up, b_up, w_down, b_down, norm2_gain, norm2_bias):
    params = tuple((w.astype(jnp.float32) for w in (w_qkv, b_qv, w_out, b_out, norm1_gain, norm1_bias, w_up, b_up, w_down, b_down, norm2_gain, norm2_bias)))
    table = replace_table.astype(jnp.float32)
    group = math.gcd(SEQS, max(1, 4096 // LENGTH))
    blocks = SEQS // group
    width = tokens.shape[1]
    inputs = (tokens.reshape(blocks, group, LENGTH, width), mask_positions.reshape(blocks, group, -1), mask_counts.reshape(blocks, group), replace_ids.reshape(blocks, group, -1), cotangent.reshape(blocks, group, LENGTH, width))

    def run(totals, block):
        rows, positions, counts, ids, upstream = block

        def forward(rows32, table32, attention_weight):
            start = apply_masks(rows32, positions, counts, ids, table32)
            middle = encoder_layer(start, attention_weight)
            return encoder_layer(middle, attention_weight)
        result, pull = jax.vjp(forward, rows.astype(jnp.float32), table, params)
        d_rows, d_table, d_params = pull(upstream.astype(jnp.float32))
        totals = jax.tree.map(jnp.add, totals, (d_table, d_params))
        return (totals, (result.astype(jnp.bfloat16), d_rows))
    start = jax.tree.map(jnp.zeros_like, (table, params))
    (d_table, grads), (final, d_rows) = lax.scan(run, start, inputs)
    return (final.reshape(-1, width), d_rows.reshape(-1, width), d_table, grads[0], grads[1], grads[2], grads[3], grads[4], grads[5], grads[6], grads[7], grads[8], grads[9], grads[10], grads[11])
```

```python
import functools
import math

import jax
import jax.numpy as jnp
from jax import lax
from jax.experimental import pallas as pl
from jax.experimental.pallas import tpu as pltpu
from jax.sharding import PartitionSpec as P

HEADS = 16
EPSILON = 1e-05
BF = jnp.bfloat16
F32 = jnp.float32
MESH = pl.DeviceIdType.MESH


def log2(n):
    return n.bit_length() - 1

def entry_barrier(partners):
    barrier = pltpu.get_barrier_semaphore()
    for partner in partners:
        pl.semaphore_signal(barrier, inc=1, device_id=partner, device_id_type=MESH)
    pl.semaphore_wait(barrier, len(partners))

def bit_of(value, bit):
    return lax.rem(value // (1 << bit), 2)

def flip(value, bit):
    return value + (1 - 2 * bit_of(value, bit)) * (1 << bit)

def gather_kernel(ndp, nf, shapes, *refs):
    n = len(shapes)
    ins, small, outs, small_out = refs[:n], refs[n], refs[n + 1:2 * n + 1], refs[2 * n + 1]
    send, recv, local = refs[2 * n + 2:]
    dp, me = lax.axis_index("dp"), lax.axis_index("fsdp")
    fbits = log2(nf)
    sibling = (dp, flip(me, 0))
    outer = [(dp, flip(me, b)) for b in range(1, fbits)]
    near = [(flip(dp, 0), me), (flip(dp, 1), me)]
    others = [(dp, lax.rem(me + d, nf)) for d in range(1, nf)]
    entry_barrier(others + near)
    code = lax.rem(dp, 4)
    counter = [0]
    started = []
    arrived = []

    def push(src, dst, partner):
        k = counter[0]
        counter[0] += 1
        copy = pltpu.make_async_remote_copy(src, dst, send.at[k], recv.at[k], device_id=partner, device_id_type=MESH)
        copy.start()
        started.append(copy)
        arrived.append(False)
        return k

    def arrive(k):
        started[k].wait_recv()
        arrived[k] = True

    small_copies = []
    for d in range(1, nf):
        small_copies.append(push(small, small_out.at[me], (dp, lax.rem(me + d, nf))))
    own_small = pltpu.make_async_copy(small, small_out.at[me], local.at[n])
    own_small.start()
    own = [own_small]
    for i in range(n):
        r, c = shapes[i]
        copy = pltpu.make_async_copy(ins[i], outs[i].at[pl.ds(pl.multiple_of(me * r, r), r)], local.at[i])
        copy.start()
        own.append(copy)

    def place(i, f, k, half):
        r, c = shapes[i]
        q, w = r // 4, c // 2
        return outs[i].at[pl.ds(pl.multiple_of(f * r + k * q, 16), q), pl.ds(half * w, w)]

    items = [(i, h) for i in range(n) for h in range(2)]
    waits = {}

    def stage(t, s):
        i, half = items[t]
        r, c = shapes[i]
        q, w = r // 4, c // 2
        p1, p2 = (0, 1) if half == 0 else (1, 0)
        if s == 0:
            src = ins[i].at[pl.ds(pl.multiple_of(code * q, 16), q), pl.ds(half * w, w)]
            if fbits > 1:
                waits[t, "y", 1] = [(me, push(src, place(i, me, code, half), outer[0]))]
            whole = ins[i].at[:, pl.ds(half * w, w)]
            push(whole, outs[i].at[pl.ds(pl.multiple_of(me * r, r), r), pl.ds(half * w, w)], sibling)
            return
        if s < fbits - 1 + 1 and s >= 1:
            got = []
            for f, copy in waits.pop((t, "y", s)):
                arrive(copy)
                got.append(flip(f, s))
            known.setdefault(t, []).extend(got)
            if s < fbits - 1:
                nxt = []
                src = ins[i].at[pl.ds(pl.multiple_of(code * q, 16), q), pl.ds(half * w, w)]
                nxt.append((me, push(src, place(i, me, code, half), outer[s])))
                for f in known[t]:
                    nxt.append((f, push(place(i, f, code, half), place(i, f, code, half), outer[s])))
                waits[t, "y", s + 1] = nxt
            else:
                waits[t, "p1"] = [(f, push(place(i, f, code, half), place(i, f, code, half), near[p1])) for f in known[t]]
                waits[t, "p2a"] = [(f, push(place(i, f, code, half), place(i, f, code, half), near[p2])) for f in known[t]]
            for f in got:
                push(place(i, f, code, half), place(i, f, code, half), sibling)
            return
        if s == fbits:
            k = flip(code, p1)
            out = []
            for f, copy in waits.pop((t, "p1")):
                arrive(copy)
                out.append((f, push(place(i, f, k, half), place(i, f, k, half), near[p2])))
                push(place(i, f, k, half), place(i, f, k, half), sibling)
            waits[t, "p2b"] = out
            return
        if s == fbits + 1:
            k = flip(code, p2)
            for f, copy in waits.pop((t, "p2a")):
                arrive(copy)
                push(place(i, f, k, half), place(i, f, k, half), sibling)
            return
        if s == fbits + 2:
            k = flip(flip(code, p2), p1)
            for f, copy in waits.pop((t, "p2b")):
                arrive(copy)
                push(place(i, f, k, half), place(i, f, k, half), sibling)

    known = {}
    stages = fbits + 3
    ahead = 2
    for step in range(-ahead, len(items) + stages - 1):
        for s in range(stages - 1, -1, -1):
            t = step - s if s else step + ahead
            if 0 <= t < len(items):
                stage(t, s)
    for copy, seen in zip(started, arrived):
        copy.wait_send()
        if not seen:
            copy.wait_recv()
    for copy in own:
        copy.wait()


def gather_weights(ndp, nf, collective_id, shards, small):
    shapes = tuple(s.shape for s in shards)
    fbits = log2(nf)
    per_item = (nf // 2 - 1) * 3 + 1 + (nf // 2 - 1) * 4 + (nf // 2 - 1)
    copies = nf - 1 + 2 * len(shards) * per_item
    any_space = pl.BlockSpec(memory_space=pl.ANY)
    outs = pl.pallas_call(
        functools.partial(gather_kernel, ndp, nf, shapes),
        out_shape=[jax.ShapeDtypeStruct((nf * r, c), jnp.bfloat16) for r, c in shapes]
        + [jax.ShapeDtypeStruct((nf,) + small.shape, small.dtype)],
        in_specs=[any_space] * (len(shards) + 1),
        out_specs=[any_space] * (len(shards) + 1),
        scratch_shapes=[
            pltpu.SemaphoreType.DMA((copies,)),
            pltpu.SemaphoreType.DMA((copies,)),
            pltpu.SemaphoreType.DMA((len(shards) + 1,)),
        ],
        compiler_params=pltpu.CompilerParams(collective_id=collective_id, has_side_effects=True),
        name="gather_weights",
    )(*shards, small)
    return outs[:-1], outs[-1]


def cut_plan(rows, cols, bits):
    plan = []
    for _ in range(bits):
        if rows >= 32:
            rows //= 2
            plan.append((0, rows))
        else:
            cols //= 2
            plan.append((1, cols))
    return plan


def reduce_kernel(ndp, nf, shapes, chunks, *refs):
    n = len(shapes)
    ins, outs = refs[:n], refs[n : 2 * n]
    held, from_core = refs[2 * n : 2 * n + 2]
    rest = refs[2 * n + 2 :]
    fbits, dbits = log2(nf), log2(ndp)
    from_outer, rest = rest[: fbits - 1], rest[fbits - 1 :]
    from_near, rest = rest[:dbits], rest[dbits:]
    done, send, recv, local, store = rest
    dp, me = lax.axis_index("dp"), lax.axis_index("fsdp")
    core = lax.rem(me, 2)
    sibling = (dp, flip(me, 0))
    outer = [(dp, flip(me, b)) for b in range(1, fbits)]
    near = [(flip(dp, b), me) for b in range(dbits)]
    entry_barrier([sibling] + outer + near)
    half = nf // 2
    started = []
    state = {}

    def push(src, dst, partner):
        k = len(started)
        copy = pltpu.make_async_remote_copy(
            src, dst, send.at[k], recv.at[k], device_id=partner, device_id_type=MESH
        )
        copy.start()
        started.append([copy, False])
        return k

    def arrive(k):
        started[k][0].wait_recv()
        started[k][1] = True

    def window(j, block, at):
        (r0, rr), (c0, cc) = at
        return held.at[j, block, pl.ds(r0, rr), pl.ds(c0, cc)]

    def stage(j, s):
        i, r0, c0, rn, cn = chunks[j]
        plan = cut_plan(rn, cn, dbits)
        block_rows = shapes[i][0] // nf
        if s == 0:
            loads, sends = [], []
            for b in range(half):
                mine = ins[i].at[pl.ds(pl.multiple_of((2 * b + core) * block_rows + r0, 16), rn), pl.ds(c0, cn)]
                theirs = ins[i].at[pl.ds(pl.multiple_of((2 * b + 1 - core) * block_rows + r0, 16), rn), pl.ds(c0, cn)]
                copy = pltpu.make_async_copy(mine, held.at[j, b, pl.ds(0, rn), pl.ds(0, cn)], local.at[j * half + b])
                copy.start()
                loads.append(copy)
                sends.append(push(theirs, from_core.at[j, b, pl.ds(0, rn), pl.ds(0, cn)], sibling))
            state[j] = (loads, sends)
            return
        if s == 1:
            loads, sends = state[j]
            for b in range(half):
                loads[b].wait()
                arrive(sends[b])
            held[j, :, :rn, :cn] += from_core[j, :, :rn, :cn]
            state[j] = (0, half)
        elif s < fbits + 1:
            bit = fbits - (s - 1)
            k, lo, size = state[j]
            arrive(k)
            held[j, pl.ds(lo, size), :rn, :cn] += from_outer[bit - 1][j, :, :rn, :cn]
            state[j] = (lo, size)
        if 1 <= s < fbits:
            bit = fbits - s
            lo, size = state[j]
            size //= 2
            mine = bit_of(me, bit)
            keep, give = lo + mine * size, lo + (1 - mine) * size
            k = push(
                held.at[j, pl.ds(give, size), pl.ds(0, rn), pl.ds(0, cn)],
                from_outer[bit - 1].at[j, :, pl.ds(0, rn), pl.ds(0, cn)],
                outer[bit - 1],
            )
            state[j] = (k, keep, size)
            return
        first = fbits
        if first <= s <= first + dbits:
            b = s - first
            if b == 0:
                lo, _ = state[j]
                at = ((0, rn), (0, cn))
            else:
                k, lo, at, history = state[j]
                arrive(k)
                (ra, rr), (ca, cc) = at
                total = held[j, lo, pl.ds(ra, rr), pl.ds(ca, cc)] + from_near[b - 1][j, :rr, :cc]
                if b == dbits:
                    done[j, pl.ds(ra, rr), pl.ds(ca, cc)] = total
                else:
                    held[j, lo, pl.ds(ra, rr), pl.ds(ca, cc)] = total
            if b < dbits:
                (ra, rr), (ca, cc) = at
                axis, size = plan[b]
                mine = bit_of(dp, b)
                if axis == 0:
                    keep = ((al(ra + mine * size, 16), size), (ca, cc))
                    give = ((al(ra + (1 - mine) * size, 16), size), (ca, cc))
                else:
                    keep = ((ra, rr), (al(ca + mine * size, 128), size))
                    give = ((ra, rr), (al(ca + (1 - mine) * size, 128), size))
                k = push(
                    window(j, lo, give), from_near[b].at[j, pl.ds(0, keep[0][1]), pl.ds(0, keep[1][1])], near[b]
                )
                history = [] if b == 0 else state[j][3]
                state[j] = (k, lo, keep, history + [at])
                return
            _, _, at, history = state[j]
        if s == first + dbits:
            at, history = state[j][2], state[j][3]
        else:
            b = dbits - (s - first - dbits)
            k, at, history = state[j]
            arrive(k)
            at, history = history[-1], history[:-1]
        if history:
            b = len(history) - 1
            (ra, rr), (ca, cc) = at
            piece = done.at[j, pl.ds(ra, rr), pl.ds(ca, cc)]
            k = push(piece, piece, near[b])
            state[j] = (k, at, history)
        else:
            copy = pltpu.make_async_copy(done.at[j, pl.ds(0, rn), pl.ds(0, cn)], outs[i].at[pl.ds(r0, rn), pl.ds(c0, cn)], store.at[j])
            copy.start()
            stores.append(copy)

    stores = []
    stages = fbits + 2 * dbits + 1
    ahead = 2
    for step in range(-ahead, len(chunks) + stages - 1):
        for s in range(stages - 1, -1, -1):
            j = step - s if s else step + ahead
            if 0 <= j < len(chunks):
                stage(j, s)
    for copy, seen in started:
        copy.wait_send()
        if not seen:
            copy.wait_recv()
    for copy in stores:
        copy.wait()


def al(value, by):
    return value if isinstance(value, int) else pl.multiple_of(value, by)


def reduce_grads(ndp, nf, collective_id, grads):
    shapes = tuple(g.shape for g in grads)
    fbits, dbits = log2(nf), log2(ndp)
    chunks = tuple(
        (i, r0, c0, min(128, r // nf), min(1024, c))
        for i, (r, c) in enumerate(shapes)
        for c0 in range(0, c, min(1024, c))
        for r0 in range(0, r // nf, min(128, r // nf))
    )
    n, half = len(chunks), nf // 2
    rn, cn = max(c[3] for c in chunks), max(c[4] for c in chunks)
    sizes = [(0, 0)] * dbits
    for _, _, _, rr, cc in chunks:
        for b, (axis, size) in enumerate(cut_plan(rr, cc, dbits)):
            rr, cc = (size, cc) if axis == 0 else (rr, size)
            sizes[b] = max(sizes[b][0], rr), max(sizes[b][1], cc)
    copies = n * (half + fbits - 1 + 2 * dbits)
    any_space = pl.BlockSpec(memory_space=pl.ANY)
    return pl.pallas_call(
        functools.partial(reduce_kernel, ndp, nf, shapes, chunks),
        out_shape=[jax.ShapeDtypeStruct((r // nf, c), jnp.bfloat16) for r, c in shapes],
        in_specs=[any_space] * len(grads),
        out_specs=[any_space] * len(grads),
        scratch_shapes=[
            pltpu.VMEM((n, half, rn, cn), jnp.bfloat16),
            pltpu.VMEM((n, half, rn, cn), jnp.bfloat16),
        ]
        + [pltpu.VMEM((n, 1 << (b - 1), rn, cn), jnp.bfloat16) for b in range(1, fbits)]
        + [pltpu.VMEM((n,) + size, jnp.bfloat16) for size in sizes]
        + [
            pltpu.VMEM((n, rn, cn), jnp.bfloat16),
            pltpu.SemaphoreType.DMA((copies,)),
            pltpu.SemaphoreType.DMA((copies,)),
            pltpu.SemaphoreType.DMA((n * half,)),
            pltpu.SemaphoreType.DMA((n,)),
        ],
        compiler_params=pltpu.CompilerParams(
            collective_id=collective_id, has_side_effects=True, vmem_limit_bytes=56 * 1024 * 1024
        ),
        name="reduce_grads",
    )(*grads)


def dot(left, right):
    return jnp.dot(left, right, preferred_element_type=F32)


def back_dot(left, right):
    return lax.dot_general(left, right, (((1,), (1,)), ((), ())), preferred_element_type=F32)


def outer_dot(left, right):
    return lax.dot_general(left, right, (((0,), (0,)), ((), ())), preferred_element_type=F32)


def norm_forward(t, gain, shift):
    mean = jnp.mean(t, axis=-1, keepdims=True)
    centred = t - mean
    spread = jnp.mean(centred * centred, axis=-1, keepdims=True)
    inverse = lax.rsqrt(spread + EPSILON)
    unit = centred * inverse
    return unit * gain + shift, unit, inverse


def norm_back(g, unit, inverse, gain):
    d_gain = jnp.sum(g * unit, axis=0)
    d_shift = jnp.sum(g, axis=0)
    gg = g * gain
    m1 = jnp.mean(gg, axis=-1, keepdims=True)
    m2 = jnp.mean(gg * unit, axis=-1, keepdims=True)
    return (gg - m1 - unit * m2) * inverse, d_gain, d_shift


def attention(q, k, v, length):
    heads = lambda t: t.reshape(length, HEADS, -1)
    scores = jnp.einsum("qhe,khe->hqk", heads(q), heads(k), preferred_element_type=F32)
    probs = jax.nn.softmax(scores, axis=-1).astype(BF)
    mixed = jnp.einsum("hqk,khe->qhe", probs, heads(v), preferred_element_type=F32)
    return mixed.reshape(length, -1).astype(BF), probs


def attention_back(q, k, v, probs, mixed, d_mixed, length):
    heads = lambda t: t.reshape(length, HEADS, -1)
    qh, kh, vh, doh = heads(q), heads(k), heads(v), heads(d_mixed)
    d_probs = jnp.einsum("qhe,khe->hqk", doh, vh, preferred_element_type=F32)
    inner = jnp.einsum("qhe,qhe->hq", doh.astype(F32), heads(mixed).astype(F32))[:, :, None]
    d_scores = (probs.astype(F32) * (d_probs - inner)).astype(BF)
    dq = jnp.einsum("hqk,khe->qhe", d_scores, kh, preferred_element_type=F32).astype(BF)
    dk = jnp.einsum("hqk,qhe->khe", d_scores, qh, preferred_element_type=F32).astype(BF)
    dv = jnp.einsum("hqk,qhe->khe", probs, doh, preferred_element_type=F32).astype(BF)
    flat = lambda t: t.reshape(length, -1)
    return flat(dq), flat(dk), flat(dv)


def forward(rows, w, length):
    width = rows.shape[1]
    scale = 1.0 / math.sqrt(width // HEADS)
    low = rows.astype(BF)
    joined = dot(low, w["qkv"])
    q = ((joined[:, :width] + w["b_qv"][:width]) * scale).astype(BF)
    k = joined[:, width : 2 * width].astype(BF)
    v = (joined[:, 2 * width :] + w["b_qv"][width:]).astype(BF)
    mixed, probs = attention(q, k, v, length)
    branch = dot(mixed, w["out"]) + w["b_out"]
    hidden, unit1, inv1 = norm_forward(rows + branch, w["gain1"], w["bias1"])
    hidden_low = hidden.astype(BF)
    u = dot(hidden_low, w["up"]) + w["b_up"]
    below = 0.5 * (1.0 + lax.erf(u * math.sqrt(0.5)))
    active = (u * below).astype(BF)
    slope = (below + u * (math.sqrt(0.5 / math.pi) * jnp.exp(-0.5 * u * u))).astype(BF)
    f = dot(active, w["down"]) + w["b_down"]
    result, unit2, inv2 = norm_forward(hidden + f, w["gain2"], w["bias2"])
    return result, dict(
        low=low, q=q, k=k, v=v, mixed=mixed, probs=probs, unit1=unit1, inv1=inv1,
        hidden=hidden_low, active=active, slope=slope, unit2=unit2, inv2=inv2,
    )


def backward(g, kept, w, length):
    width = g.shape[1]
    scale = 1.0 / math.sqrt(width // HEADS)
    total = lambda t: jnp.sum(t.astype(F32), axis=0)
    d_hf, d_gain2, d_bias2 = norm_back(g, kept["unit2"], kept["inv2"], w["gain2"])
    df = d_hf.astype(BF)
    du = (back_dot(df, w["down"]) * kept["slope"].astype(F32)).astype(BF)
    gh = d_hf + back_dot(du, w["up"])
    d_xz, d_gain1, d_bias1 = norm_back(gh, kept["unit1"], kept["inv1"], w["gain1"])
    dz = d_xz.astype(BF)
    d_mixed = back_dot(dz, w["out"]).astype(BF)
    dq, dk, dv = attention_back(kept["q"], kept["k"], kept["v"], kept["probs"], kept["mixed"], d_mixed, length)
    dq = dq * BF(scale)
    d_joined = jnp.concatenate([dq, dk, dv], axis=1)
    d_rows = d_xz + back_dot(d_joined, w["qkv"])
    vectors = (
        jnp.concatenate([total(dq), total(dv)]), total(dz), d_gain1, d_bias1,
        total(du), total(df), d_gain2, d_bias2,
    )
    return d_rows, dict(df=df, du=du, dz=dz, d_joined=d_joined), vectors


def shards(ndp, nf, tokens, mask_positions, mask_counts, replace_ids, cotangent, replace_table,
           w_qkv, b_qv, w_out, b_out, norm1_gain, norm1_bias, w_up, b_up, w_down, b_down, norm2_gain, norm2_bias):
    length, width = tokens.shape
    slots = mask_positions.shape[1]
    vectors = (b_qv, b_out, norm1_gain, norm1_bias, b_up, b_down, norm2_gain, norm2_bias)
    lengths = [t.shape[0] for t in vectors]
    count = sum(lengths)
    lanes = -(-count // 2048) * 128
    packed = jnp.pad(jnp.concatenate(vectors), (0, 16 * lanes - count)).reshape(16, lanes)
    (qkv, out, up, down), small = gather_weights(ndp, nf, 0, [w_qkv, w_out, w_up, w_down], packed)
    small = small.reshape(nf, 16 * lanes)
    names = ("b_qv", "b_out", "gain1", "bias1", "b_up", "b_down", "gain2", "bias2")
    w = dict(qkv=qkv, out=out, up=up, down=down)
    at = 0
    for name, size in zip(names, lengths):
        w[name] = small[:, at : at + size].reshape(-1).astype(F32)
        at += size

    used = (jnp.arange(slots, dtype=jnp.int32) < mask_counts[0]).astype(F32)
    places = jnp.arange(length, dtype=jnp.int32)
    position_hot = (mask_positions[0][:, None] == places[None, :]).astype(F32) * used[:, None]
    entries = jnp.arange(replace_table.shape[0], dtype=jnp.int32)
    vocab_hot = (replace_ids[0][:, None] == entries[None, :]).astype(BF)
    row_hot = outer_dot(position_hot.astype(BF), vocab_hot).astype(BF)
    keep = 1.0 - jnp.sum(position_hot, axis=0)[:, None]
    start = tokens.astype(F32) * keep + dot(row_hot, replace_table)

    middle, kept_one = forward(start, w, length)
    final, kept_two = forward(middle, w, length)
    d_middle, two, vectors_two = backward(cotangent.astype(F32), kept_two, w, length)
    d_start, one, vectors_one = backward(d_middle, kept_one, w, length)
    token_grad = d_start * keep

    def weight(left, right):
        both = lambda a, b: jnp.concatenate([a, b], axis=0)
        return outer_dot(both(kept_one[left], kept_two[left]), both(one[right], two[right])).astype(BF)

    (g_down,) = reduce_grads(ndp, nf, 1, [weight("active", "df")])
    (g_up,) = reduce_grads(ndp, nf, 2, [weight("hidden", "du")])
    high = d_start.astype(BF)
    rest = d_start - high.astype(F32)
    mid = rest.astype(BF)
    d_table = outer_dot(row_hot, high) + outer_dot(row_hot, mid)
    table_rows = -(-replace_table.shape[0] // 16) * 16
    d_table = jnp.pad(d_table, ((0, table_rows - d_table.shape[0]), (0, 0))).astype(BF)
    vec = [a + b for a, b in zip(vectors_one, vectors_two)]
    pieces = jnp.concatenate([t.reshape(nf, -1) for t in vec], axis=1)
    vec_rows = 64 - table_rows
    pieces = jnp.pad(pieces, ((0, 0), (0, vec_rows * width - count))).astype(BF).reshape(nf, vec_rows, width)
    extra = jnp.concatenate([pieces, jnp.broadcast_to(d_table[None], (nf,) + d_table.shape)], axis=1).reshape(-1, width)
    g_out, g_qkv, g_extra = reduce_grads(ndp, nf, 3, [weight("mixed", "dz"), weight("low", "d_joined"), extra])
    table_grad = g_extra[vec_rows : vec_rows + replace_table.shape[0]].astype(F32)
    flat = g_extra[:vec_rows].reshape(-1).astype(F32)
    v = []
    at = 0
    for size in lengths:
        v.append(flat[at : at + size])
        at += size
    up32 = lambda t: t.astype(F32)
    return (
        final.astype(BF), token_grad, table_grad, up32(g_qkv), v[0], up32(g_out), v[1], v[2], v[3],
        up32(g_up), v[4], up32(g_down), v[5], v[6], v[7],
    )


def solution(mesh):
    both = P(("dp", "fsdp"))
    rows = P("fsdp")
    in_specs = (both,) * 5 + (P(),) + (rows,) * 12
    out_specs = (both, both, P()) + (rows,) * 12
    body = functools.partial(shards, mesh.shape["dp"], mesh.shape["fsdp"])
    return jax.shard_map(body, mesh=mesh, in_specs=in_specs, out_specs=out_specs, check_vma=False)
```

```python
import functools
import math

import jax
import jax.numpy as jnp
from jax import lax
from jax.experimental import pallas as pl
from jax.experimental.pallas import tpu as pltpu
from jax.sharding import PartitionSpec as P

HEADS = 16
EPSILON = 1e-05
BF = jnp.bfloat16
F32 = jnp.float32
MESH = pl.DeviceIdType.MESH


def log2(n):
    return n.bit_length() - 1

def entry_barrier(partners):
    barrier = pltpu.get_barrier_semaphore()
    for partner in partners:
        pl.semaphore_signal(barrier, inc=1, device_id=partner, device_id_type=MESH)
    pl.semaphore_wait(barrier, len(partners))

def bit_of(value, bit):
    return lax.rem(value // (1 << bit), 2)

def flip(value, bit):
    return value + (1 - 2 * bit_of(value, bit)) * (1 << bit)

CUTS = 4


SKEW = 2
def gather_kernel(ndp, nf, shapes, *refs):
    n = len(shapes)
    ins, small, outs, small_out = refs[:n], refs[n], refs[n + 1:2 * n + 1], refs[2 * n + 1]
    staged = refs[2 * n + 2 : 3 * n + 2]
    send, recv, local = refs[3 * n + 2 :]
    dp, me = lax.axis_index("dp"), lax.axis_index("fsdp")
    fbits = log2(nf)
    sibling = (dp, flip(me, 0))
    outer = [(dp, flip(me, b)) for b in range(1, fbits)]
    near = [(flip(dp, 0), me), (flip(dp, 1), me)]
    others = [(dp, lax.rem(me + d, nf)) for d in range(1, nf)]
    entry_barrier(others + near)
    code = lax.rem(dp, 4)
    counter = [0]
    started = []
    arrived = []

    def push(src, dst, partner):
        k = counter[0]
        counter[0] += 1
        copy = pltpu.make_async_remote_copy(src, dst, send.at[k], recv.at[k], device_id=partner, device_id_type=MESH)
        copy.start()
        started.append(copy)
        arrived.append(False)
        return k

    def arrive(k):
        started[k].wait_recv()
        arrived[k] = True

    small_copies = []
    for d in range(1, nf):
        small_copies.append(push(small, small_out.at[me], (dp, lax.rem(me + d, nf))))
    own_small = pltpu.make_async_copy(small, small_out.at[me], local.at[n])
    own_small.start()
    own = [own_small]
    loads = []
    for i in range(n):
        r, c = shapes[i]
        copy = pltpu.make_async_copy(ins[i], staged[i], local.at[i])
        copy.start()
        loads.append(copy)

    def place(i, f, k, half):
        r, c = shapes[i]
        q, w = r // 4, c // CUTS
        return outs[i].at[pl.ds(pl.multiple_of(f * r + k * q, 16), q), pl.ds(half * w, w)]

    items = [(i, h) for i in range(n) for h in range(CUTS)]
    waits = {}

    def stage(t, s):
        i, half = items[t]
        r, c = shapes[i]
        q, w = r // 4, c // CUTS
        p1, p2 = (0, 1) if half % 2 == 0 else (1, 0)
        if s == 0:
            src = ins[i].at[pl.ds(pl.multiple_of(code * q, 16), q), pl.ds(half * w, w)]
            if fbits > 1:
                waits[t, "y", 1] = [(me, push(src, place(i, me, code, half), outer[0]))]
            whole = ins[i].at[:, pl.ds(half * w, w)]
            push(whole, outs[i].at[pl.ds(pl.multiple_of(me * r, r), r), pl.ds(half * w, w)], sibling)
            return
        if s < fbits - 1 + 1 and s >= 1:
            got = []
            for f, copy in waits.pop((t, "y", s)):
                arrive(copy)
                got.append(flip(f, s))
            known.setdefault(t, []).extend(got)
            if s < fbits - 1:
                nxt = []
                src = ins[i].at[pl.ds(pl.multiple_of(code * q, 16), q), pl.ds(half * w, w)]
                nxt.append((me, push(src, place(i, me, code, half), outer[s])))
                for f in known[t]:
                    nxt.append((f, push(place(i, f, code, half), place(i, f, code, half), outer[s])))
                waits[t, "y", s + 1] = nxt
            else:
                waits[t, "p1"] = [(f, push(place(i, f, code, half), place(i, f, code, half), near[p1])) for f in known[t]]
                waits[t, "p2a"] = [(f, push(place(i, f, code, half), place(i, f, code, half), near[p2])) for f in known[t]]
            for f in got:
                push(place(i, f, code, half), place(i, f, code, half), sibling)
            return
        if s == fbits:
            k = flip(code, p1)
            out = []
            for f, copy in waits.pop((t, "p1")):
                arrive(copy)
                out.append((f, push(place(i, f, k, half), place(i, f, k, half), near[p2])))
                push(place(i, f, k, half), place(i, f, k, half), sibling)
            waits[t, "p2b"] = out
            return
        if s == fbits + 1:
            k = flip(code, p2)
            for f, copy in waits.pop((t, "p2a")):
                arrive(copy)
                push(place(i, f, k, half), place(i, f, k, half), sibling)
            return
        if s == fbits + 2:
            k = flip(flip(code, p2), p1)
            for f, copy in waits.pop((t, "p2b")):
                arrive(copy)
                push(place(i, f, k, half), place(i, f, k, half), sibling)

    known = {}
    stages = fbits + 3
    ahead = 2
    for step in range(-ahead, len(items) + SKEW * (stages - 1)):
        if step == 0:
            for i in range(n):
                r = shapes[i][0]
                loads[i].wait()
                copy = pltpu.make_async_copy(staged[i], outs[i].at[pl.ds(pl.multiple_of(me * r, r), r)], local.at[i])
                copy.start()
                own.append(copy)
        for s in range(stages - 1, -1, -1):
            t = step - SKEW * s if s else step + ahead
            if 0 <= t < len(items):
                stage(t, s)
    for copy, seen in zip(started, arrived):
        copy.wait_send()
        if not seen:
            copy.wait_recv()
    for copy in own:
        copy.wait()


def gather_weights(ndp, nf, collective_id, shards, small):
    shapes = tuple(s.shape for s in shards)
    fbits = log2(nf)
    per_item = (nf // 2 - 1) * 3 + 1 + (nf // 2 - 1) * 4 + (nf // 2 - 1)
    copies = nf - 1 + CUTS * len(shards) * per_item
    any_space = pl.BlockSpec(memory_space=pl.ANY)
    outs = pl.pallas_call(
        functools.partial(gather_kernel, ndp, nf, shapes),
        out_shape=[jax.ShapeDtypeStruct((nf * r, c), jnp.bfloat16) for r, c in shapes]
        + [jax.ShapeDtypeStruct((nf,) + small.shape, small.dtype)],
        in_specs=[any_space] * (len(shards) + 1),
        out_specs=[any_space] * (len(shards) + 1),
        scratch_shapes=[pltpu.VMEM(shape, jnp.bfloat16) for shape in shapes]
        + [
            pltpu.SemaphoreType.DMA((copies,)),
            pltpu.SemaphoreType.DMA((copies,)),
            pltpu.SemaphoreType.DMA((len(shards) + 1,)),
        ],
        compiler_params=pltpu.CompilerParams(
            collective_id=collective_id, has_side_effects=True, vmem_limit_bytes=32 * 1024 * 1024
        ),
        name="gather_weights",
    )(*shards, small)
    return outs[:-1], outs[-1]


LAG = 2
ROWS = 512
def cut_plan(rows, cols, bits):
    plan = []
    for _ in range(bits):
        if rows >= 32:
            rows //= 2
            plan.append((0, rows))
        else:
            cols //= 2
            plan.append((1, cols))
    return plan


def reduce_kernel(ndp, nf, shapes, chunks, *refs):
    n = len(shapes)
    ins, outs = refs[:n], refs[n : 2 * n]
    held, from_core = refs[2 * n : 2 * n + 2]
    rest = refs[2 * n + 2 :]
    fbits, dbits = log2(nf), log2(ndp)
    from_outer, rest = rest[: fbits - 1], rest[fbits - 1 :]
    from_near, rest = rest[:dbits], rest[dbits:]
    done, send, recv, local, store = rest
    dp, me = lax.axis_index("dp"), lax.axis_index("fsdp")
    core = lax.rem(me, 2)
    sibling = (dp, flip(me, 0))
    outer = [(dp, flip(me, b)) for b in range(1, fbits)]
    near = [(flip(dp, b), me) for b in range(dbits)]
    entry_barrier([sibling] + outer + near)
    half = nf // 2
    started = []
    state = {}

    def push(src, dst, partner):
        k = len(started)
        copy = pltpu.make_async_remote_copy(
            src, dst, send.at[k], recv.at[k], device_id=partner, device_id_type=MESH
        )
        copy.start()
        started.append([copy, False])
        return k

    def arrive(k):
        started[k][0].wait_recv()
        started[k][1] = True

    def window(j, block, at):
        (r0, rr), (c0, cc) = at
        return held.at[j, block, pl.ds(r0, rr), pl.ds(c0, cc)]

    def stage(j, s):
        i, r0, c0, rn, cn = chunks[j]
        plan = cut_plan(rn, cn, dbits)
        block_rows = shapes[i][0] // nf
        if s == 0:
            loads, sends = [], []
            for b in range(half):
                mine = ins[i].at[pl.ds(pl.multiple_of((2 * b + core) * block_rows + r0, 16), rn), pl.ds(c0, cn)]
                theirs = ins[i].at[pl.ds(pl.multiple_of((2 * b + 1 - core) * block_rows + r0, 16), rn), pl.ds(c0, cn)]
                copy = pltpu.make_async_copy(mine, held.at[j, b, pl.ds(0, rn), pl.ds(0, cn)], local.at[j * half + b])
                copy.start()
                loads.append(copy)
                sends.append(push(theirs, from_core.at[j, b, pl.ds(0, rn), pl.ds(0, cn)], sibling))
            state[j] = (loads, sends)
            return
        if s == 1:
            loads, sends = state[j]
            for b in range(half):
                loads[b].wait()
                arrive(sends[b])
            held[j, :, :rn, :cn] += from_core[j, :, :rn, :cn]
            state[j] = (0, half)
        elif s < fbits + 1:
            bit = fbits - (s - 1)
            k, lo, size = state[j]
            arrive(k)
            held[j, pl.ds(lo, size), :rn, :cn] += from_outer[bit - 1][j, :, :rn, :cn]
            state[j] = (lo, size)
        if 1 <= s < fbits:
            bit = fbits - s
            lo, size = state[j]
            size //= 2
            mine = bit_of(me, bit)
            keep, give = lo + mine * size, lo + (1 - mine) * size
            k = push(
                held.at[j, pl.ds(give, size), pl.ds(0, rn), pl.ds(0, cn)],
                from_outer[bit - 1].at[j, :, pl.ds(0, rn), pl.ds(0, cn)],
                outer[bit - 1],
            )
            state[j] = (k, keep, size)
            return
        first = fbits
        if first <= s <= first + dbits:
            b = s - first
            if b == 0:
                lo, _ = state[j]
                at = ((0, rn), (0, cn))
            else:
                k, lo, at, history = state[j]
                arrive(k)
                (ra, rr), (ca, cc) = at
                total = held[j, lo, pl.ds(ra, rr), pl.ds(ca, cc)] + from_near[b - 1][j, :rr, :cc]
                if b == dbits:
                    done[j, pl.ds(ra, rr), pl.ds(ca, cc)] = total
                else:
                    held[j, lo, pl.ds(ra, rr), pl.ds(ca, cc)] = total
            if b < dbits:
                (ra, rr), (ca, cc) = at
                axis, size = plan[b]
                mine = bit_of(dp, b)
                if axis == 0:
                    keep = ((al(ra + mine * size, 16), size), (ca, cc))
                    give = ((al(ra + (1 - mine) * size, 16), size), (ca, cc))
                else:
                    keep = ((ra, rr), (al(ca + mine * size, 128), size))
                    give = ((ra, rr), (al(ca + (1 - mine) * size, 128), size))
                k = push(
                    window(j, lo, give), from_near[b].at[j, pl.ds(0, keep[0][1]), pl.ds(0, keep[1][1])], near[b]
                )
                history = [] if b == 0 else state[j][3]
                state[j] = (k, lo, keep, history + [at])
                return
            _, _, at, history = state[j]
        if s == first + dbits:
            at, history = state[j][2], state[j][3]
        else:
            b = dbits - (s - first - dbits)
            k, at, history = state[j]
            arrive(k)
            at, history = history[-1], history[:-1]
        if history:
            b = len(history) - 1
            (ra, rr), (ca, cc) = at
            piece = done.at[j, pl.ds(ra, rr), pl.ds(ca, cc)]
            k = push(piece, piece, near[b])
            state[j] = (k, at, history)
        else:
            copy = pltpu.make_async_copy(done.at[j, pl.ds(0, rn), pl.ds(0, cn)], outs[i].at[pl.ds(r0, rn), pl.ds(c0, cn)], store.at[j])
            copy.start()
            stores.append(copy)

    stores = []
    stages = fbits + 2 * dbits + 1
    for step in range(len(chunks) + LAG * (stages - 1)):
        for s in range(stages - 1, -1, -1):
            j = step - LAG * s
            if 0 <= j < len(chunks):
                stage(j, s)
    for copy, seen in started:
        copy.wait_send()
        if not seen:
            copy.wait_recv()
    for copy in stores:
        copy.wait()


def al(value, by):
    return value if isinstance(value, int) else pl.multiple_of(value, by)


def reduce_grads(ndp, nf, collective_id, grads):
    shapes = tuple(g.shape for g in grads)
    fbits, dbits = log2(nf), log2(ndp)
    chunks = tuple(
        (i, r0, c0, min(ROWS // nf, r // nf), min(1024, c))
        for i, (r, c) in enumerate(shapes)
        for c0 in range(0, c, min(1024, c))
        for r0 in range(0, r // nf, min(ROWS // nf, r // nf))
    )
    n, half = len(chunks), nf // 2
    rn, cn = max(c[3] for c in chunks), max(c[4] for c in chunks)
    sizes = [(0, 0)] * dbits
    for _, _, _, rr, cc in chunks:
        for b, (axis, size) in enumerate(cut_plan(rr, cc, dbits)):
            rr, cc = (size, cc) if axis == 0 else (rr, size)
            sizes[b] = max(sizes[b][0], rr), max(sizes[b][1], cc)
    copies = n * (half + fbits - 1 + 2 * dbits)
    any_space = pl.BlockSpec(memory_space=pl.ANY)
    return pl.pallas_call(
        functools.partial(reduce_kernel, ndp, nf, shapes, chunks),
        out_shape=[jax.ShapeDtypeStruct((r // nf, c), jnp.bfloat16) for r, c in shapes],
        in_specs=[any_space] * len(grads),
        out_specs=[any_space] * len(grads),
        scratch_shapes=[
            pltpu.VMEM((n, half, rn, cn), jnp.bfloat16),
            pltpu.VMEM((n, half, rn, cn), jnp.bfloat16),
        ]
        + [pltpu.VMEM((n, 1 << (b - 1), rn, cn), jnp.bfloat16) for b in range(1, fbits)]
        + [pltpu.VMEM((n,) + size, jnp.bfloat16) for size in sizes]
        + [
            pltpu.VMEM((n, rn, cn), jnp.bfloat16),
            pltpu.SemaphoreType.DMA((copies,)),
            pltpu.SemaphoreType.DMA((copies,)),
            pltpu.SemaphoreType.DMA((n * half,)),
            pltpu.SemaphoreType.DMA((n,)),
        ],
        compiler_params=pltpu.CompilerParams(
            collective_id=collective_id, has_side_effects=True, vmem_limit_bytes=56 * 1024 * 1024
        ),
        name="reduce_grads",
    )(*grads)


def nt(left, right):
    return lax.dot_general(left, right, (((1,), (1,)), ((), ())), preferred_element_type=F32)


def nn(left, right):
    return jnp.dot(left, right, preferred_element_type=F32)


def attend_kernel(q_ref, k_ref, v_ref, o_ref, probs_ref):
    q, k, v = q_ref[...], k_ref[...], v_ref[...]
    dim = q.shape[1] // 2
    first = lax.broadcasted_iota(jnp.int32, q.shape, 1) < dim
    parts = []
    for h in range(2):
        one = jnp.where(first if h == 0 else ~first, q, jnp.zeros_like(q))
        scores = nt(one, k)
        powers = jnp.exp(scores - jnp.max(scores, axis=1, keepdims=True))
        probs = (powers * (1.0 / jnp.sum(powers, axis=1, keepdims=True))).astype(BF)
        probs_ref[h] = probs
        parts.append(nn(probs, v))
    o_ref[...] = jnp.where(first, parts[0], parts[1]).astype(BF)


def attention(q, k, v):
    length, width = q.shape
    pair = 2 * (width // HEADS)
    cols = pl.BlockSpec((length, pair), lambda p: (0, p))
    return pl.pallas_call(
        attend_kernel,
        grid=(HEADS // 2,),
        in_specs=[cols] * 3,
        out_specs=[cols, pl.BlockSpec((2, length, length), lambda p: (p, 0, 0))],
        out_shape=[
            jax.ShapeDtypeStruct((length, width), BF),
            jax.ShapeDtypeStruct((HEADS, length, length), BF),
        ],
        compiler_params=pltpu.CompilerParams(vmem_limit_bytes=40 * 1024 * 1024),
        name="attend",
    )(q, k, v)


def attend_back_math(q, k, v, o, do, probs, scale):
    dim = q.shape[1] // 2
    first = lax.broadcasted_iota(jnp.int32, q.shape, 1) < dim
    product = do.astype(F32) * o.astype(F32)
    q_t, do_t = q.T, do.T
    dqs, dks, dvs = [], [], []
    for h in range(2):
        mine = first if h == 0 else ~first
        inner = jnp.sum(jnp.where(mine, product, 0.0), axis=1, keepdims=True)
        p = probs(h)
        d_probs = nt(jnp.where(mine, do, jnp.zeros_like(do)), v)
        d_scores = (p.astype(F32) * (d_probs - inner)).astype(BF)
        dqs.append(nn(d_scores, k))
        dks.append(nn(q_t[h * dim : (h + 1) * dim], d_scores))
        dvs.append(nn(do_t[h * dim : (h + 1) * dim], p))
    dq = jnp.where(first, dqs[0], dqs[1]).astype(BF) * BF(scale)
    return dq, jnp.concatenate(dks, axis=0).T.astype(BF), jnp.concatenate(dvs, axis=0).T.astype(BF)


def attend_back_kernel(scale, q_ref, k_ref, v_ref, o_ref, do_ref, probs_ref, dq_ref, dk_ref, dv_ref):
    dq_ref[...], dk_ref[...], dv_ref[...] = attend_back_math(
        q_ref[...], k_ref[...], v_ref[...], o_ref[...], do_ref[...], lambda h: probs_ref[h], scale
    )


def attention_back(q, k, v, o, do, probs):
    length, width = q.shape
    pair = 2 * (width // HEADS)
    scale = 1.0 / math.sqrt(width // HEADS)
    cols = pl.BlockSpec((length, pair), lambda p: (0, p))
    return pl.pallas_call(
        functools.partial(attend_back_kernel, scale),
        grid=(HEADS // 2,),
        in_specs=[cols] * 5 + [pl.BlockSpec((2, length, length), lambda p: (p, 0, 0))],
        out_specs=[cols] * 3,
        out_shape=[jax.ShapeDtypeStruct((length, width), BF)] * 3,
        compiler_params=pltpu.CompilerParams(vmem_limit_bytes=40 * 1024 * 1024),
        name="attend_back",
    )(q, k, v, o, do, probs)


def dot(left, right):
    return jnp.dot(left, right, preferred_element_type=F32)


def back_dot(left, right):
    return lax.dot_general(left, right, (((1,), (1,)), ((), ())), preferred_element_type=F32)


def outer_dot(left, right):
    return lax.dot_general(left, right, (((0,), (0,)), ((), ())), preferred_element_type=F32)


def norm_forward(t, gain, shift):
    mean = jnp.mean(t, axis=-1, keepdims=True)
    centred = t - mean
    spread = jnp.mean(centred * centred, axis=-1, keepdims=True)
    inverse = lax.rsqrt(spread + EPSILON)
    unit = centred * inverse
    return unit * gain + shift, unit, inverse


def norm_back(g, unit, inverse, gain):
    d_gain = jnp.sum(g * unit, axis=0)
    d_shift = jnp.sum(g, axis=0)
    gg = g * gain
    m1 = jnp.mean(gg, axis=-1, keepdims=True)
    m2 = jnp.mean(gg * unit, axis=-1, keepdims=True)
    return (gg - m1 - unit * m2) * inverse, d_gain, d_shift


def forward(rows, w, length):
    width = rows.shape[1]
    scale = 1.0 / math.sqrt(width // HEADS)
    low = rows.astype(BF)
    joined = dot(low, w["qkv"])
    q = ((joined[:, :width] + w["b_qv"][:width]) * scale).astype(BF)
    k = joined[:, width : 2 * width].astype(BF)
    v = (joined[:, 2 * width :] + w["b_qv"][width:]).astype(BF)
    mixed, probs = attention(q, k, v)
    branch = dot(mixed, w["out"]) + w["b_out"]
    hidden, unit1, inv1 = norm_forward(rows + branch, w["gain1"], w["bias1"])
    hidden_low = hidden.astype(BF)
    u = dot(hidden_low, w["up"]) + w["b_up"]
    below = 0.5 * (1.0 + lax.erf(u * math.sqrt(0.5)))
    active = (u * below).astype(BF)
    slope = (below + u * (math.sqrt(0.5 / math.pi) * jnp.exp(-0.5 * u * u))).astype(BF)
    f = dot(active, w["down"]) + w["b_down"]
    result, unit2, inv2 = norm_forward(hidden + f, w["gain2"], w["bias2"])
    return result, dict(
        low=low, q=q, k=k, v=v, mixed=mixed, probs=probs, unit1=unit1, inv1=inv1,
        hidden=hidden_low, active=active, slope=slope, unit2=unit2, inv2=inv2,
    )


def backward(g, kept, w, length):
    width = g.shape[1]
    scale = 1.0 / math.sqrt(width // HEADS)
    total = lambda t: jnp.sum(t.astype(F32), axis=0)
    d_hf, d_gain2, d_bias2 = norm_back(g, kept["unit2"], kept["inv2"], w["gain2"])
    df = d_hf.astype(BF)
    du = (back_dot(df, w["down"]) * kept["slope"].astype(F32)).astype(BF)
    gh = d_hf + back_dot(du, w["up"])
    d_xz, d_gain1, d_bias1 = norm_back(gh, kept["unit1"], kept["inv1"], w["gain1"])
    dz = d_xz.astype(BF)
    d_mixed = back_dot(dz, w["out"]).astype(BF)
    dq, dk, dv = attention_back(kept["q"], kept["k"], kept["v"], kept["mixed"], d_mixed, kept["probs"])
    d_joined = jnp.concatenate([dq, dk, dv], axis=1)
    d_rows = d_xz + back_dot(d_joined, w["qkv"])
    vectors = (
        jnp.concatenate([total(dq), total(dv)]), total(dz), d_gain1, d_bias1,
        total(du), total(df), d_gain2, d_bias2,
    )
    return d_rows, dict(df=df, du=du, dz=dz, d_joined=d_joined), vectors


def shards(ndp, nf, tokens, mask_positions, mask_counts, replace_ids, cotangent, replace_table,
           w_qkv, b_qv, w_out, b_out, norm1_gain, norm1_bias, w_up, b_up, w_down, b_down, norm2_gain, norm2_bias):
    length, width = tokens.shape
    slots = mask_positions.shape[1]
    vectors = (b_qv, b_out, norm1_gain, norm1_bias, b_up, b_down, norm2_gain, norm2_bias)
    lengths = [t.shape[0] for t in vectors]
    count = sum(lengths)
    lanes = -(-count // 2048) * 128
    packed = jnp.pad(jnp.concatenate(vectors), (0, 16 * lanes - count)).reshape(16, lanes)
    (qkv, out, up, down), small = gather_weights(ndp, nf, 0, [w_qkv, w_out, w_up, w_down], packed)
    small = small.reshape(nf, 16 * lanes)
    names = ("b_qv", "b_out", "gain1", "bias1", "b_up", "b_down", "gain2", "bias2")
    w = dict(qkv=qkv, out=out, up=up, down=down)
    at = 0
    for name, size in zip(names, lengths):
        w[name] = small[:, at : at + size].reshape(-1).astype(F32)
        at += size

    used = (jnp.arange(slots, dtype=jnp.int32) < mask_counts[0]).astype(F32)
    places = jnp.arange(length, dtype=jnp.int32)
    position_hot = (mask_positions[0][:, None] == places[None, :]).astype(F32) * used[:, None]
    entries = jnp.arange(replace_table.shape[0], dtype=jnp.int32)
    vocab_hot = (replace_ids[0][:, None] == entries[None, :]).astype(BF)
    row_hot = outer_dot(position_hot.astype(BF), vocab_hot).astype(BF)
    keep = 1.0 - jnp.sum(position_hot, axis=0)[:, None]
    start = tokens.astype(F32) * keep + dot(row_hot, replace_table)

    middle, kept_one = forward(start, w, length)
    final, kept_two = forward(middle, w, length)
    d_middle, two, vectors_two = backward(cotangent.astype(F32), kept_two, w, length)
    d_start, one, vectors_one = backward(d_middle, kept_one, w, length)
    token_grad = d_start * keep

    def weight(left, right):
        both = lambda a, b: jnp.concatenate([a, b], axis=0)
        return outer_dot(both(kept_one[left], kept_two[left]), both(one[right], two[right])).astype(BF)

    high = d_start.astype(BF)
    rest = d_start - high.astype(F32)
    mid = rest.astype(BF)
    d_table = outer_dot(row_hot, high) + outer_dot(row_hot, mid)
    table_rows = -(-replace_table.shape[0] // 16) * 16
    d_table = jnp.pad(d_table, ((0, table_rows - d_table.shape[0]), (0, 0))).astype(BF)
    vec = [a + b for a, b in zip(vectors_one, vectors_two)]
    pieces = jnp.concatenate([t.reshape(nf, -1) for t in vec], axis=1)
    vec_rows = 64 - table_rows
    pieces = jnp.pad(pieces, ((0, 0), (0, vec_rows * width - count))).astype(BF).reshape(nf, vec_rows, width)
    extra = jnp.concatenate([pieces, jnp.broadcast_to(d_table[None], (nf,) + d_table.shape)], axis=1).reshape(-1, width)
    g_down, g_up, g_out, g_qkv, g_extra = reduce_grads(
        ndp, nf, 1, [weight("active", "df"), weight("hidden", "du"), weight("mixed", "dz"), weight("low", "d_joined"), extra]
    )
    table_grad = g_extra[vec_rows : vec_rows + replace_table.shape[0]].astype(F32)
    flat = g_extra[:vec_rows].reshape(-1).astype(F32)
    v = []
    at = 0
    for size in lengths:
        v.append(flat[at : at + size])
        at += size
    up32 = lambda t: t.astype(F32)
    return (
        final.astype(BF), token_grad, table_grad, up32(g_qkv), v[0], up32(g_out), v[1], v[2], v[3],
        up32(g_up), v[4], up32(g_down), v[5], v[6], v[7],
    )


def solution(mesh):
    both = P(("dp", "fsdp"))
    rows = P("fsdp")
    in_specs = (both,) * 5 + (P(),) + (rows,) * 12
    out_specs = (both, both, P()) + (rows,) * 12
    body = functools.partial(shards, mesh.shape["dp"], mesh.shape["fsdp"])
    return jax.shard_map(body, mesh=mesh, in_specs=in_specs, out_specs=out_specs, check_vma=False)
```

```python
import functools
import math

import jax
import jax.numpy as jnp
from jax import lax
from jax.experimental import pallas as pl
from jax.experimental.pallas import tpu as pltpu
from jax.sharding import PartitionSpec as P

HEADS = 16
EPSILON = 1e-05
BF = jnp.bfloat16
F32 = jnp.float32
MESH = pl.DeviceIdType.MESH


def log2(n):
    return n.bit_length() - 1

def entry_barrier(partners):
    barrier = pltpu.get_barrier_semaphore()
    for partner in partners:
        pl.semaphore_signal(barrier, inc=1, device_id=partner, device_id_type=MESH)
    pl.semaphore_wait(barrier, len(partners))

def bit_of(value, bit):
    return lax.rem(value // (1 << bit), 2)

def flip(value, bit):
    return value + (1 - 2 * bit_of(value, bit)) * (1 << bit)

CUTS = 4


SKEW = 2
def gather_kernel(ndp, nf, shapes, *refs):
    n = len(shapes)
    ins, small, outs, small_out = refs[:n], refs[n], refs[n + 1:2 * n + 1], refs[2 * n + 1]
    staged = refs[2 * n + 2 : 3 * n + 2]
    send, recv, local = refs[3 * n + 2 :]
    dp, me = lax.axis_index("dp"), lax.axis_index("fsdp")
    fbits = log2(nf)
    sibling = (dp, flip(me, 0))
    outer = [(dp, flip(me, b)) for b in range(1, fbits)]
    near = [(flip(dp, 0), me), (flip(dp, 1), me)]
    others = [(dp, lax.rem(me + d, nf)) for d in range(1, nf)]
    entry_barrier(others + near)
    code = lax.rem(dp, 4)
    counter = [0]
    started = []
    arrived = []

    def push(src, dst, partner):
        k = counter[0]
        counter[0] += 1
        copy = pltpu.make_async_remote_copy(src, dst, send.at[k], recv.at[k], device_id=partner, device_id_type=MESH)
        copy.start()
        started.append(copy)
        arrived.append(False)
        return k

    def arrive(k):
        started[k].wait_recv()
        arrived[k] = True

    small_copies = []
    for d in range(1, nf):
        small_copies.append(push(small, small_out.at[me], (dp, lax.rem(me + d, nf))))
    own_small = pltpu.make_async_copy(small, small_out.at[me], local.at[n])
    own_small.start()
    own = [own_small]
    loads = []
    for i in range(n):
        r, c = shapes[i]
        copy = pltpu.make_async_copy(ins[i], staged[i], local.at[i])
        copy.start()
        loads.append(copy)

    def place(i, f, k, half):
        r, c = shapes[i]
        q, w = r // 4, c // CUTS
        return outs[i].at[pl.ds(pl.multiple_of(f * r + k * q, 16), q), pl.ds(half * w, w)]

    items = [(i, h) for i in range(n) for h in range(CUTS)]
    waits = {}

    def stage(t, s):
        i, half = items[t]
        r, c = shapes[i]
        q, w = r // 4, c // CUTS
        p1, p2 = (0, 1) if half % 2 == 0 else (1, 0)
        if s == 0:
            src = ins[i].at[pl.ds(pl.multiple_of(code * q, 16), q), pl.ds(half * w, w)]
            if fbits > 1:
                waits[t, "y", 1] = [(me, push(src, place(i, me, code, half), outer[0]))]
            whole = ins[i].at[:, pl.ds(half * w, w)]
            push(whole, outs[i].at[pl.ds(pl.multiple_of(me * r, r), r), pl.ds(half * w, w)], sibling)
            return
        if s < fbits - 1 + 1 and s >= 1:
            got = []
            for f, copy in waits.pop((t, "y", s)):
                arrive(copy)
                got.append(flip(f, s))
            known.setdefault(t, []).extend(got)
            if s < fbits - 1:
                nxt = []
                src = ins[i].at[pl.ds(pl.multiple_of(code * q, 16), q), pl.ds(half * w, w)]
                nxt.append((me, push(src, place(i, me, code, half), outer[s])))
                for f in known[t]:
                    nxt.append((f, push(place(i, f, code, half), place(i, f, code, half), outer[s])))
                waits[t, "y", s + 1] = nxt
            else:
                waits[t, "p1"] = [(f, push(place(i, f, code, half), place(i, f, code, half), near[p1])) for f in known[t]]
                waits[t, "p2a"] = [(f, push(place(i, f, code, half), place(i, f, code, half), near[p2])) for f in known[t]]
            for f in got:
                push(place(i, f, code, half), place(i, f, code, half), sibling)
            return
        if s == fbits:
            k = flip(code, p1)
            out = []
            for f, copy in waits.pop((t, "p1")):
                arrive(copy)
                out.append((f, push(place(i, f, k, half), place(i, f, k, half), near[p2])))
                push(place(i, f, k, half), place(i, f, k, half), sibling)
            waits[t, "p2b"] = out
            return
        if s == fbits + 1:
            k = flip(code, p2)
            for f, copy in waits.pop((t, "p2a")):
                arrive(copy)
                push(place(i, f, k, half), place(i, f, k, half), sibling)
            return
        if s == fbits + 2:
            k = flip(flip(code, p2), p1)
            for f, copy in waits.pop((t, "p2b")):
                arrive(copy)
                push(place(i, f, k, half), place(i, f, k, half), sibling)

    known = {}
    stages = fbits + 3
    ahead = 2
    for step in range(-ahead, len(items) + SKEW * (stages - 1)):
        if step == 0:
            for i in range(n):
                r = shapes[i][0]
                loads[i].wait()
                copy = pltpu.make_async_copy(staged[i], outs[i].at[pl.ds(pl.multiple_of(me * r, r), r)], local.at[i])
                copy.start()
                own.append(copy)
        for s in range(stages - 1, -1, -1):
            t = step - SKEW * s if s else step + ahead
            if 0 <= t < len(items):
                stage(t, s)
    for copy, seen in zip(started, arrived):
        copy.wait_send()
        if not seen:
            copy.wait_recv()
    for copy in own:
        copy.wait()


def gather_weights(ndp, nf, collective_id, shards, small):
    shapes = tuple(s.shape for s in shards)
    fbits = log2(nf)
    per_item = (nf // 2 - 1) * 3 + 1 + (nf // 2 - 1) * 4 + (nf // 2 - 1)
    copies = nf - 1 + CUTS * len(shards) * per_item
    any_space = pl.BlockSpec(memory_space=pl.ANY)
    outs = pl.pallas_call(
        functools.partial(gather_kernel, ndp, nf, shapes),
        out_shape=[jax.ShapeDtypeStruct((nf * r, c), jnp.bfloat16) for r, c in shapes]
        + [jax.ShapeDtypeStruct((nf,) + small.shape, small.dtype)],
        in_specs=[any_space] * (len(shards) + 1),
        out_specs=[any_space] * (len(shards) + 1),
        scratch_shapes=[pltpu.VMEM(shape, jnp.bfloat16) for shape in shapes]
        + [
            pltpu.SemaphoreType.DMA((copies,)),
            pltpu.SemaphoreType.DMA((copies,)),
            pltpu.SemaphoreType.DMA((len(shards) + 1,)),
        ],
        compiler_params=pltpu.CompilerParams(
            collective_id=collective_id, has_side_effects=True, vmem_limit_bytes=32 * 1024 * 1024
        ),
        name="gather_weights",
    )(*shards, small)
    return outs[:-1], outs[-1]


LAG = 2
ROWS = 512


LAG = 2
CHUNK_ROWS = 512
CORE_SLOTS = 4
HELD_SLOTS = 14
KINDS = (0,)


def al(value, by):
    return value if isinstance(value, int) else pl.multiple_of(value, by)


def stage_orders(ndp, nf):
    outer = [("outer", b) for b in range(log2(nf) - 1, 0, -1)]
    near = [("near", b) for b in range(log2(ndp))]
    return (
        outer + near,
        near[:1] + outer + near[1:],
        outer + near[1:2] + near[:1] + near[2:],
    )


def chunk_list(ndp, nf, shapes, kinds):
    chunks = []
    for i, (r, c) in enumerate(shapes):
        rn, cn = min(CHUNK_ROWS // nf, r // nf), min(1024, c)
        for c0 in range(0, c, cn):
            for r0 in range(0, r // nf, rn):
                chunks.append((i, r0, c0, rn, cn, kinds[len(chunks) % len(kinds)]))
    return tuple(chunks)


def halvings(order, half, rn, cn):
    left, blocks = [], half
    for kind, _ in order:
        if kind == "outer":
            blocks //= 2
            axis = 0
        elif rn >= 32:
            rn //= 2
            axis = 1
        else:
            cn //= 2
            axis = 2
        left.append((blocks, rn, cn, axis))
    return left


def engine_scratch(ndp, nf, chunks):
    orders, half = stage_orders(ndp, nf), nf // 2
    rn, cn = max(c[3] for c in chunks), max(c[4] for c in chunks)
    scratch = [
        pltpu.VMEM((HELD_SLOTS, half, rn, cn), jnp.bfloat16),
        pltpu.VMEM((CORE_SLOTS, half, rn, cn), jnp.bfloat16),
        pltpu.VMEM((len(chunks), rn, cn), jnp.bfloat16),
    ]
    for kind, order in enumerate(orders):
        mine = [c for c in chunks if c[5] == kind]
        if mine:
            sizes = [halvings(order, half, c[3], c[4]) for c in mine]
            for s in range(len(order)):
                most = tuple(max(size[s][a] for size in sizes) for a in range(3))
                scratch.append(pltpu.VMEM((2 * LAG,) + most, jnp.bfloat16))
    copies = len(chunks) * (half + len(orders[0]) + log2(ndp))
    return scratch + [
        pltpu.SemaphoreType.DMA((copies,)),
        pltpu.SemaphoreType.DMA((copies,)),
        pltpu.SemaphoreType.DMA((len(chunks) * half,)),
        pltpu.SemaphoreType.DMA((len(chunks),)),
    ]


class Engine:
    def __init__(self, ndp, nf, chunks, refs, source, target):
        self.nf, self.chunks, self.source, self.target = nf, chunks, source, target
        self.orders, self.half = stage_orders(ndp, nf), nf // 2
        self.dbits = log2(ndp)
        self.held, self.from_core, self.done = refs[:3]
        self.landing = {}
        at = 3
        for kind in range(len(self.orders)):
            if any(c[5] == kind for c in chunks):
                for s in range(len(self.orders[0])):
                    self.landing[kind, s] = refs[at]
                    at += 1
        self.send, self.recv, self.local, self.store = refs[at:]
        self.dp, self.me = lax.axis_index("dp"), lax.axis_index("fsdp")
        self.core = lax.rem(self.me, 2)
        self.sibling = (self.dp, flip(self.me, 0))
        self.partner = {("outer", b): (self.dp, flip(self.me, b)) for b in range(1, log2(nf))}
        self.partner.update({("near", b): (flip(self.dp, b), self.me) for b in range(self.dbits)})
        self.started, self.state, self.stores, self.used = [], {}, [], {}
        self.sends = {}
        counts = {}
        self.index = []
        for c in chunks:
            self.index.append(counts.get(c[5], 0) % (2 * LAG))
            counts[c[5]] = counts.get(c[5], 0) + 1
        self.stages = 2 + len(self.orders[0]) + self.dbits
        self.steps = len(chunks) + LAG * (self.stages - 1)
        entry_barrier([self.sibling] + list(self.partner.values()))

    def push(self, src, dst, partner, holder=None):
        k = len(self.started)
        copy = pltpu.make_async_remote_copy(
            src, dst, self.send.at[k], self.recv.at[k], device_id=partner, device_id_type=MESH
        )
        copy.start()
        self.started.append([copy, False, False])
        if holder is not None:
            self.sends.setdefault(holder, []).append(k)
        return k

    def arrive(self, k):
        self.started[k][0].wait_recv()
        self.started[k][1] = True

    def sent(self, holder):
        for k in self.sends.pop(holder, []):
            self.started[k][0].wait_send()
            self.started[k][2] = True

    def block_row(self, j, b, other):
        i, r0 = self.chunks[j][:2]
        core = 1 - self.core if other else self.core
        return (2 * b + core, r0)

    def slot(self, j):
        return j % HELD_SLOTS

    def room(self, j):
        self.sent(("held", self.slot(j)))

    def stage(self, j, s):
        i, r0, c0, rn, cn, kind = self.chunks[j]
        order = self.orders[kind]
        held, slot = self.held, self.slot(j)
        last = len(order)
        if s == 0:
            self.room(j)
            self.state[j] = self.source(self, j)
            return
        if s == 1:
            loads, sends = self.state[j]
            for copy in loads:
                copy.wait()
            for k in sends:
                self.arrive(k)
            held[slot, :, :rn, :cn] += self.from_core[j % CORE_SLOTS, :, :rn, :cn]
            now, history = ((0, self.half), (0, rn), (0, cn)), []
        elif s <= last + 1:
            k, now, history = self.state[j]
            self.arrive(k)
            (b0, bn), (ra, rr), (ca, cc) = now
            arrived = self.landing[kind, s - 2][self.index[j], :bn, :rr, :cc]
            total = held[slot, pl.ds(b0, bn), pl.ds(ra, rr), pl.ds(ca, cc)] + arrived
            if s == last + 1:
                self.done[j, pl.ds(ra, rr), pl.ds(ca, cc)] = total[0]
            else:
                held[slot, pl.ds(b0, bn), pl.ds(ra, rr), pl.ds(ca, cc)] = total
        if s <= last:
            name, bit = order[s - 1]
            axis = halvings(order, self.half, rn, cn)[s - 1][3]
            mine = bit_of(self.me if name == "outer" else self.dp, bit)
            start, size = now[axis]
            size //= 2
            by = (1, 16, 128)[axis]
            keep, give = list(now), list(now)
            keep[axis] = (al(start + mine * size, by), size)
            give[axis] = (al(start + (1 - mine) * size, by), size)
            src = held.at[(slot,) + tuple(pl.ds(*g) for g in give)]
            dst = self.landing[kind, s - 1].at[(self.index[j],) + tuple(pl.ds(0, g[1]) for g in give)]
            k = self.push(src, dst, self.partner[name, bit], ("held", slot))
            if name == "near":
                history = history + [(bit, now[1:])]
            self.state[j] = (k, tuple(keep), history)
            return
        if s > last + 1:
            k, _, history = self.state[j]
            self.arrive(k)
            at, history = history[-1][1], history[:-1]
        else:
            at = now[1:]
        if history:
            piece = self.done.at[(j,) + tuple(pl.ds(*a) for a in at)]
            k = self.push(piece, piece, self.partner["near", history[-1][0]])
            self.state[j] = (k, None, history)
        else:
            copy = pltpu.make_async_copy(
                self.done.at[j, pl.ds(0, rn), pl.ds(0, cn)], self.target(j), self.store.at[j]
            )
            copy.start()
            self.stores.append(copy)

    def step(self, t):
        for s in range(self.stages - 1, -1, -1):
            j = t - LAG * s
            if 0 <= j < len(self.chunks):
                self.stage(j, s)

    def finish(self):
        for copy, seen, left in self.started:
            if not left:
                copy.wait_send()
            if not seen:
                copy.wait_recv()
        for copy in self.stores:
            copy.wait()


def nt(left, right):
    return lax.dot_general(left, right, (((1,), (1,)), ((), ())), preferred_element_type=F32)


def nn(left, right):
    return jnp.dot(left, right, preferred_element_type=F32)


def attend_kernel(q_ref, k_ref, v_ref, o_ref, probs_ref):
    q, k, v = q_ref[...], k_ref[...], v_ref[...]
    dim = q.shape[1] // 2
    first = lax.broadcasted_iota(jnp.int32, q.shape, 1) < dim
    parts = []
    for h in range(2):
        one = jnp.where(first if h == 0 else ~first, q, jnp.zeros_like(q))
        scores = nt(one, k)
        powers = jnp.exp(scores - jnp.max(scores, axis=1, keepdims=True))
        probs = (powers * (1.0 / jnp.sum(powers, axis=1, keepdims=True))).astype(BF)
        probs_ref[h] = probs
        parts.append(nn(probs, v))
    o_ref[...] = jnp.where(first, parts[0], parts[1]).astype(BF)


def attention(q, k, v):
    length, width = q.shape
    pair = 2 * (width // HEADS)
    cols = pl.BlockSpec((length, pair), lambda p: (0, p))
    return pl.pallas_call(
        attend_kernel,
        grid=(HEADS // 2,),
        in_specs=[cols] * 3,
        out_specs=[cols, pl.BlockSpec((2, length, length), lambda p: (p, 0, 0))],
        out_shape=[
            jax.ShapeDtypeStruct((length, width), BF),
            jax.ShapeDtypeStruct((HEADS, length, length), BF),
        ],
        compiler_params=pltpu.CompilerParams(vmem_limit_bytes=40 * 1024 * 1024),
        name="attend",
    )(q, k, v)


def attend_back_math(q, k, v, o, do, probs, scale):
    dim = q.shape[1] // 2
    first = lax.broadcasted_iota(jnp.int32, q.shape, 1) < dim
    product = do.astype(F32) * o.astype(F32)
    q_t, do_t = q.T, do.T
    dqs, dks, dvs = [], [], []
    for h in range(2):
        mine = first if h == 0 else ~first
        inner = jnp.sum(jnp.where(mine, product, 0.0), axis=1, keepdims=True)
        p = probs(h)
        d_probs = nt(jnp.where(mine, do, jnp.zeros_like(do)), v)
        d_scores = (p.astype(F32) * (d_probs - inner)).astype(BF)
        dqs.append(nn(d_scores, k))
        dks.append(nn(q_t[h * dim : (h + 1) * dim], d_scores))
        dvs.append(nn(do_t[h * dim : (h + 1) * dim], p))
    dq = jnp.where(first, dqs[0], dqs[1]).astype(BF) * BF(scale)
    return dq, jnp.concatenate(dks, axis=0).T.astype(BF), jnp.concatenate(dvs, axis=0).T.astype(BF)


def attend_back_kernel(scale, q_ref, k_ref, v_ref, o_ref, do_ref, probs_ref, dq_ref, dk_ref, dv_ref):
    dq_ref[...], dk_ref[...], dv_ref[...] = attend_back_math(
        q_ref[...], k_ref[...], v_ref[...], o_ref[...], do_ref[...], lambda h: probs_ref[h], scale
    )


def attention_back(q, k, v, o, do, probs):
    length, width = q.shape
    pair = 2 * (width // HEADS)
    scale = 1.0 / math.sqrt(width // HEADS)
    cols = pl.BlockSpec((length, pair), lambda p: (0, p))
    return pl.pallas_call(
        functools.partial(attend_back_kernel, scale),
        grid=(HEADS // 2,),
        in_specs=[cols] * 5 + [pl.BlockSpec((2, length, length), lambda p: (p, 0, 0))],
        out_specs=[cols] * 3,
        out_shape=[jax.ShapeDtypeStruct((length, width), BF)] * 3,
        compiler_params=pltpu.CompilerParams(vmem_limit_bytes=40 * 1024 * 1024),
        name="attend_back",
    )(q, k, v, o, do, probs)


TILE = 256
STAGED = 3


def tiles(count, body):
    lax.fori_loop(0, count, lambda n, c: (body(pl.multiple_of(n * TILE, TILE)), c)[1], 0)


class Loads:
    def __init__(self, sem, ring, items):
        self.sem, self.ring, self.items, self.next, self.copies = sem, ring, items, 0, {}

    def start(self):
        if self.next < len(self.items):
            k = self.next
            self.next += 1
            group = []
            for n, (src, dst) in enumerate(self.items[k](k % self.ring)):
                copy = pltpu.make_async_copy(src, dst, self.sem.at[k % self.ring, n])
                copy.start()
                group.append(copy)
            self.copies[k] = group

    def wait(self, k):
        for copy in self.copies.pop(k):
            copy.wait()
        return k % self.ring


def tail_kernel(ndp, nf, shapes, chunks, scale, *refs):
    (
        w_down, w_up, w_out, w_qkv, slope, d_hf, unit, df1, df2, du2, dz2, dqkv2,
        a1, a2, h1, h2, o1, o2, x1, x2, q, k, v, o, probs, sums_in, gain, inverse, entry_hot,
    ) = refs[:29]
    outs, g0 = refs[29:34], refs[34]
    (
        r_down, r_up, r_out, r_qkv, r_qkv2, lhs, turned, staged, gh, unit_v, weight, slope_v, pair_v,
        do, probs_v, sums, w_sem, s_sem, p_sem, l_sem, m_sem,
    ) = refs[35:56]
    tokens, width = df1.shape
    part = min(1024, width)
    ff = w_down.shape[0]
    parts = ff // part
    wide = part // TILE
    pair = pair_v.shape[3]
    pairs = width // pair
    n_mid = 3

    misc = []
    def load(src, dst):
        copy = pltpu.make_async_copy(src, dst, m_sem.at[len(misc)])
        copy.start()
        misc.append(copy)
        return copy

    need_df = [load(df1, r_down.at[0]), load(df2, r_down.at[1])]
    need_hf = [load(d_hf, gh), load(unit, unit_v)]
    need_sums = load(sums_in, sums)
    need_du2 = load(du2, r_up.at[1])
    need_dz2 = load(dz2, r_out.at[1])
    need_dqkv2 = load(dqkv2, r_qkv2)

    columns = lambda t: pl.ds(t * part, part)
    weights = Loads(w_sem, 2, (
        [lambda s, t=t: [(w_down.at[columns(t)], weight.at[s])] for t in range(parts)]
        + [lambda s, t=t: [(w_up.at[:, columns(t)], weight.at[s])] for t in range(parts)]
        + [lambda s: [(w_out, weight.at[s])]]
        + [lambda s, t=t: [(w_qkv.at[:, columns(t)], weight.at[s])] for t in range(n_mid)]
    ))
    slopes = Loads(s_sem, 2, [lambda s, t=t: [(slope.at[:, columns(t)], slope_v.at[s])] for t in range(parts)])
    heads = Loads(p_sem, 2, [
        lambda s, p=p: [(t.at[:, pl.ds(p * pair, pair)], pair_v.at[s, n]) for n, t in enumerate((q, k, v, o))]
        + [(probs.at[pl.ds(2 * p, 2)], probs_v.at[s])]
        for p in range(pairs)
    ])
    lefts = ((a1, a2), (h1, h2), (o1, o2), (x1, x2))

    def left_item(j):
        i, r0, _, rn, _, _ = chunks[j]

        def item(s):
            block = shapes[i][0] // nf
            core = lax.rem(lax.axis_index("fsdp"), 2)
            out = []
            for app in range(2):
                for n in range(nf):
                    f = 2 * n + core if n < nf // 2 else 2 * (n - nf // 2) + 1 - core
                    features = pl.ds(pl.multiple_of(f * block + r0, rn), rn)
                    if rn % 128 == 0:
                        out.append((lefts[i][app].at[:, features], lhs.at[s, app, n]))
                    else:
                        out.append((lefts[i][app].at[features], lhs.at[s, app, n]))
            return out

        return item

    rows_of = [j for j in range(len(chunks)) if chunks[j][0] < 4]
    left = Loads(l_sem, 2, [left_item(j) for j in rows_of])
    rights = (
        lambda app, at: r_down[app, :, at],
        lambda app, at: r_up[app, :, at],
        lambda app, at: r_out[app, :, at],
        lambda app, at: r_qkv[:, at] if app == 0 else r_qkv2[:, at],
    )

    def source(engine, j):
        i, r0, c0, rn, cn, _ = chunks[j]
        slot, s = engine.slot(j), j % STAGED
        engine.sent(("staged", s))
        half = nf // 2
        if i < 4:
            buffer = left.wait(j)
            for app in range(2):
                for n in range(nf):
                    block = lhs[buffer, app, n]
                    turned[pl.ds(n * rn, rn), pl.ds(app * tokens, tokens)] = block.T if rn % 128 == 0 else block
            left.start()

            def tile(at):
                right = pl.ds(c0 + at, TILE)
                total = nn(turned[:, :tokens], rights[i](0, right)) + nn(turned[:, tokens:], rights[i](1, right))
                total = total.astype(BF).reshape(nf, rn, TILE)
                engine.held[slot, :, :, pl.ds(at, TILE)] = total[:half]
                staged[s, :, :, pl.ds(at, TILE)] = total[half:]

            tiles(cn // TILE, tile)
        else:
            block = sums[pl.ds(r0, rn), :].astype(BF)
            for b in range(half):
                engine.held[slot, b, :rn] = block
                staged[s, b, :rn] = block
        src = staged.at[s, :, pl.ds(0, rn), pl.ds(0, cn)]
        dst = engine.from_core.at[j % CORE_SLOTS, :, pl.ds(0, rn), pl.ds(0, cn)]
        return [], [engine.push(src, dst, engine.sibling, ("staged", s))]

    def target(j):
        i, r0, c0, rn, cn, _ = chunks[j]
        return outs[i].at[pl.ds(r0, rn), pl.ds(c0, cn)]

    def task_du(t):
        def run():
            s = weights.wait(t)
            slopes.wait(t)

            def tile(at):
                d = nt(r_down[0], weight[s, pl.ds(at, TILE), :])
                du = (d * slope_v[t % 2, :, pl.ds(at, TILE)].astype(F32)).astype(BF)
                r_up[0, :, pl.ds(t * part + at, TILE)] = du
                sums[5 + t : 6 + t, pl.ds(at, TILE)] += jnp.sum(du.astype(F32), axis=0, keepdims=True)

            tiles(wide, tile)
            weights.start()
            slopes.start()
        return run

    def task_gh(t):
        def run():
            if t == 0:
                for copy in need_hf:
                    copy.wait()
            s = weights.wait(parts + t)

            def tile(at):
                gh[:, pl.ds(at, TILE)] += nt(r_up[0, :, t * part : (t + 1) * part], weight[s, pl.ds(at, TILE), :])

            tiles(wide, tile)
            weights.start()
        return run

    def task_norm():
        def tile(at):
            rows = pl.ds(at, TILE)
            g, u = gh[rows, :], unit_v[rows, :].astype(F32)
            gg = g * gain[...]
            m1 = jnp.mean(gg, axis=1, keepdims=True)
            m2 = jnp.mean(gg * u, axis=1, keepdims=True)
            d = (gg - m1 - u * m2) * inverse[rows, :]
            gh[rows, :] = d
            dz = d.astype(BF)
            r_out[0, rows, :] = dz
            total = lambda t: jnp.sum(t, axis=0, keepdims=True)
            sums[2:3, :] += total(dz.astype(F32))
            sums[3:4, :] += total(g * u)
            sums[4:5, :] += total(g)

        tiles(tokens // TILE, tile)
        need_dz2.wait()

    def task_do():
        s = weights.wait(2 * parts)

        def tile(at):
            do[:, pl.ds(at, TILE)] = nt(r_out[0], weight[s, pl.ds(at, TILE), :]).astype(BF)

        tiles(width // TILE, tile)
        weights.start()

    def task_heads(p):
        def run():
            s = heads.wait(p)
            at = slice(p * pair, (p + 1) * pair)
            dq, dk, dv = attend_back_math(
                pair_v[s, 0], pair_v[s, 1], pair_v[s, 2], pair_v[s, 3], do[:, at], lambda h: probs_v[s, h], scale
            )
            r_qkv[:, at] = dq
            r_qkv[:, width + p * pair : width + (p + 1) * pair] = dk
            r_qkv[:, 2 * width + p * pair : 2 * width + (p + 1) * pair] = dv
            total = lambda t: jnp.sum(t.astype(F32), axis=0, keepdims=True)
            sums[0:1, at] += total(dq)
            sums[1:2, at] += total(dv)
            heads.start()
        return run

    def task_back(t):
        def run():
            s = weights.wait(2 * parts + 1 + t)

            def tile(at):
                gh[:, pl.ds(at, TILE)] += nt(r_qkv[:, t * part : (t + 1) * part], weight[s, pl.ds(at, TILE), :])

            tiles(wide, tile)
            weights.start()
        return run

    def task_table():
        def tile(at):
            g = gh[:, pl.ds(at, TILE)]
            high = g.astype(BF)
            rest = (g - high.astype(F32)).astype(BF)
            sums[16:48, pl.ds(at, TILE)] += nn(entry_hot[...], high) + nn(entry_hot[...], rest)

        tiles(width // TILE, tile)
        load(gh, g0)

    for _ in range(2):
        weights.start()
        slopes.start()
        left.start()
        heads.start()
    engine = Engine(ndp, nf, chunks, refs[56:], source, target)
    for copy in need_df:
        copy.wait()
    need_sums.wait()
    counts = [sum(c[0] == i for c in chunks) for i in range(5)]
    first = [sum(counts[:i]) for i in range(5)]
    early = [task_du(t) for t in range(parts)] + [task_gh(t) for t in range(parts)]
    middle = [task_norm, task_do] + [task_heads(p) for p in range(pairs)]
    late = [task_back(t) for t in range(n_mid)] + [task_table]
    plan = {}

    def spread(tasks, begin, end):
        for n, task in enumerate(tasks):
            plan.setdefault(begin + n * (end - begin) // len(tasks), []).append(task)

    spread(early, 0, first[1])
    spread(middle, first[1], first[3] - 1)
    spread(late, first[3], first[4])
    for t in range(engine.steps):
        if t == first[1]:
            need_du2.wait()
        if t == first[3]:
            need_dqkv2.wait()
        engine.step(t)
        for task in plan.get(t, ()):
            task()
    engine.finish()
    misc[-1].wait()


def tail(ndp, nf, collective_id, scale, big, gain, inverse, entry_hot):
    w_down, w_up, w_out, w_qkv = big[:4]
    df1 = big[7]
    tokens, width = df1.shape
    ff = w_down.shape[0]
    extra = big[25].shape[0]
    shapes = (w_down.shape, w_up.shape, w_out.shape, w_qkv.shape, (nf * extra, width))
    chunks = chunk_list(ndp, nf, shapes, KINDS)
    half = nf // 2
    part = min(1024, width)
    pair = 2 * (width // HEADS)
    rn = chunks[0][3]
    if rn % 128:
        big = big[:12] + [t.T for t in big[12:20]] + big[20:]
    any_space = pl.BlockSpec(memory_space=pl.ANY)
    vmem = pl.BlockSpec(memory_space=pltpu.VMEM)
    return pl.pallas_call(
        functools.partial(tail_kernel, ndp, nf, shapes, chunks, scale),
        out_shape=[jax.ShapeDtypeStruct((r // nf, c), BF) for r, c in shapes]
        + [jax.ShapeDtypeStruct((tokens, width), F32)],
        in_specs=[any_space] * len(big) + [vmem] * 3,
        out_specs=[any_space] * 6,
        scratch_shapes=[
            pltpu.VMEM((2, tokens, width), BF),
            pltpu.VMEM((2, tokens, ff), BF),
            pltpu.VMEM((2, tokens, width), BF),
            pltpu.VMEM((tokens, 3 * width), BF),
            pltpu.VMEM((tokens, 3 * width), BF),
            pltpu.VMEM((2, 2, nf, tokens, rn) if rn % 128 == 0 else (2, 2, nf, rn, tokens), BF),
            pltpu.VMEM((nf * rn, 2 * tokens), BF),
            pltpu.VMEM((STAGED, half, rn, part), BF),
            pltpu.VMEM((tokens, width), F32),
            pltpu.VMEM((tokens, width), BF),
            pltpu.VMEM((2, part, width), BF),
            pltpu.VMEM((2, tokens, part), BF),
            pltpu.VMEM((2, 4, tokens, pair), BF),
            pltpu.VMEM((tokens, width), BF),
            pltpu.VMEM((2, 2, tokens, tokens), BF),
            pltpu.VMEM((extra, width), F32),
            pltpu.SemaphoreType.DMA((2, 1)),
            pltpu.SemaphoreType.DMA((2, 1)),
            pltpu.SemaphoreType.DMA((2, 5)),
            pltpu.SemaphoreType.DMA((2, 2 * nf)),
            pltpu.SemaphoreType.DMA((16,)),
        ]
        + engine_scratch(ndp, nf, chunks),
        compiler_params=pltpu.CompilerParams(
            collective_id=collective_id, has_side_effects=True, vmem_limit_bytes=61 * 1024 * 1024
        ),
        name="tail",
    )(*big, gain, inverse, entry_hot)


def dot(left, right):
    return jnp.dot(left, right, preferred_element_type=F32)


def back_dot(left, right):
    return lax.dot_general(left, right, (((1,), (1,)), ((), ())), preferred_element_type=F32)


def outer_dot(left, right):
    return lax.dot_general(left, right, (((0,), (0,)), ((), ())), preferred_element_type=F32)


def norm_forward(t, gain, shift):
    mean = jnp.mean(t, axis=-1, keepdims=True)
    centred = t - mean
    spread = jnp.mean(centred * centred, axis=-1, keepdims=True)
    inverse = lax.rsqrt(spread + EPSILON)
    unit = centred * inverse
    return unit * gain + shift, unit, inverse


def norm_back(g, unit, inverse, gain):
    d_gain = jnp.sum(g * unit, axis=0)
    d_shift = jnp.sum(g, axis=0)
    gg = g * gain
    m1 = jnp.mean(gg, axis=-1, keepdims=True)
    m2 = jnp.mean(gg * unit, axis=-1, keepdims=True)
    return (gg - m1 - unit * m2) * inverse, d_gain, d_shift


def forward(rows, w, length):
    width = rows.shape[1]
    scale = 1.0 / math.sqrt(width // HEADS)
    low = rows.astype(BF)
    joined = dot(low, w["qkv"])
    q = ((joined[:, :width] + w["b_qv"][:width]) * scale).astype(BF)
    k = joined[:, width : 2 * width].astype(BF)
    v = (joined[:, 2 * width :] + w["b_qv"][width:]).astype(BF)
    mixed, probs = attention(q, k, v)
    branch = dot(mixed, w["out"]) + w["b_out"]
    hidden, unit1, inv1 = norm_forward(rows + branch, w["gain1"], w["bias1"])
    hidden_low = hidden.astype(BF)
    u = dot(hidden_low, w["up"]) + w["b_up"]
    below = 0.5 * (1.0 + lax.erf(u * math.sqrt(0.5)))
    active = (u * below).astype(BF)
    slope = (below + u * (math.sqrt(0.5 / math.pi) * jnp.exp(-0.5 * u * u))).astype(BF)
    f = dot(active, w["down"]) + w["b_down"]
    result, unit2, inv2 = norm_forward(hidden + f, w["gain2"], w["bias2"])
    return result, dict(
        low=low, q=q, k=k, v=v, mixed=mixed, probs=probs, unit1=unit1, inv1=inv1,
        hidden=hidden_low, active=active, slope=slope, unit2=unit2, inv2=inv2,
    )


def backward(g, kept, w, length):
    width = g.shape[1]
    scale = 1.0 / math.sqrt(width // HEADS)
    total = lambda t: jnp.sum(t.astype(F32), axis=0)
    d_hf, d_gain2, d_bias2 = norm_back(g, kept["unit2"], kept["inv2"], w["gain2"])
    df = d_hf.astype(BF)
    du = (back_dot(df, w["down"]) * kept["slope"].astype(F32)).astype(BF)
    gh = d_hf + back_dot(du, w["up"])
    d_xz, d_gain1, d_bias1 = norm_back(gh, kept["unit1"], kept["inv1"], w["gain1"])
    dz = d_xz.astype(BF)
    d_mixed = back_dot(dz, w["out"]).astype(BF)
    dq, dk, dv = attention_back(kept["q"], kept["k"], kept["v"], kept["mixed"], d_mixed, kept["probs"])
    d_joined = jnp.concatenate([dq, dk, dv], axis=1)
    d_rows = d_xz + back_dot(d_joined, w["qkv"])
    sums = [total(dq), total(dv), total(dz), d_gain1, d_bias1, *total(du).reshape(-1, width), total(df), d_gain2, d_bias2]
    return d_rows, dict(df=df, du=du, dz=dz, d_joined=d_joined), sums


def shards(ndp, nf, tokens, mask_positions, mask_counts, replace_ids, cotangent, replace_table,
           w_qkv, b_qv, w_out, b_out, norm1_gain, norm1_bias, w_up, b_up, w_down, b_down, norm2_gain, norm2_bias):
    length, width = tokens.shape
    slots = mask_positions.shape[1]
    vectors = (b_qv, b_out, norm1_gain, norm1_bias, b_up, b_down, norm2_gain, norm2_bias)
    lengths = [t.shape[0] for t in vectors]
    count = sum(lengths)
    lanes = -(-count // 2048) * 128
    packed = jnp.pad(jnp.concatenate(vectors), (0, 16 * lanes - count)).reshape(16, lanes)
    (qkv, out, up, down), small = gather_weights(ndp, nf, 0, [w_qkv, w_out, w_up, w_down], packed)
    small = small.reshape(nf, 16 * lanes)
    names = ("b_qv", "b_out", "gain1", "bias1", "b_up", "b_down", "gain2", "bias2")
    w = dict(qkv=qkv, out=out, up=up, down=down)
    at = 0
    for name, size in zip(names, lengths):
        w[name] = small[:, at : at + size].reshape(-1).astype(F32)
        at += size

    used = (jnp.arange(slots, dtype=jnp.int32) < mask_counts[0]).astype(F32)
    places = jnp.arange(length, dtype=jnp.int32)
    position_hot = (mask_positions[0][:, None] == places[None, :]).astype(F32) * used[:, None]
    entries = jnp.arange(replace_table.shape[0], dtype=jnp.int32)
    vocab_hot = (replace_ids[0][:, None] == entries[None, :]).astype(BF)
    row_hot = outer_dot(position_hot.astype(BF), vocab_hot).astype(BF)
    keep = 1.0 - jnp.sum(position_hot, axis=0)[:, None]
    start = tokens.astype(F32) * keep + dot(row_hot, replace_table)

    middle, kept_one = forward(start, w, length)
    final, kept_two = forward(middle, w, length)
    d_middle, two, sums = backward(cotangent.astype(F32), kept_two, w, length)

    one = kept_one
    d_hf, d_gain2, d_bias2 = norm_back(d_middle, one["unit2"], one["inv2"], w["gain2"])
    df = d_hf.astype(BF)
    sums[-3:] = [sums[-3] + jnp.sum(df.astype(F32), axis=0), sums[-2] + d_gain2, sums[-1] + d_bias2]
    sums = jnp.pad(jnp.stack(sums), ((0, 64 - len(sums)), (0, 0)))
    entries = replace_table.shape[0]
    entry_hot = jnp.pad(row_hot.T, ((0, 32 - entries), (0, 0)))
    big = [
        w["down"], w["up"], w["out"], w["qkv"], one["slope"], d_hf, one["unit1"].astype(BF),
        df, two["df"], two["du"], two["dz"], two["d_joined"],
        one["active"], kept_two["active"], one["hidden"], kept_two["hidden"], one["mixed"], kept_two["mixed"],
        one["low"], kept_two["low"], one["q"], one["k"], one["v"], one["mixed"], one["probs"], sums,
    ]
    scale = 1.0 / math.sqrt(width // HEADS)
    g_down, g_up, g_out, g_qkv, extra, d_start = tail(
        ndp, nf, 1, scale, big, w["gain1"].reshape(1, width), one["inv1"], entry_hot
    )
    token_grad = d_start * keep
    up32 = lambda t: t.astype(F32)
    extra = up32(extra)
    table_grad = extra[16 : 16 + entries]
    place = lax.axis_index("fsdp")
    mine = lambda t: lax.dynamic_slice_in_dim(t, place * (t.shape[0] // nf), t.shape[0] // nf)
    grown = w_up.shape[1] // width
    v = [mine(extra[:2].reshape(-1))] + [mine(extra[n]) for n in (2, 3, 4)]
    v += [mine(extra[5 : 5 + grown].reshape(-1))] + [mine(extra[n + grown]) for n in (5, 6, 7)]
    return (
        final.astype(BF), token_grad, table_grad, up32(g_qkv), v[0], up32(g_out), v[1], v[2], v[3],
        up32(g_up), v[4], up32(g_down), v[5], v[6], v[7],
    )


def solution(mesh):
    both = P(("dp", "fsdp"))
    rows = P("fsdp")
    in_specs = (both,) * 5 + (P(),) + (rows,) * 12
    out_specs = (both, both, P()) + (rows,) * 12
    body = functools.partial(shards, mesh.shape["dp"], mesh.shape["fsdp"])
    return jax.shard_map(body, mesh=mesh, in_specs=in_specs, out_specs=out_specs, check_vma=False)
```

```python
import functools
import math

import jax
import jax.numpy as jnp
from jax import lax
from jax.experimental import pallas as pl
from jax.experimental.pallas import tpu as pltpu
from jax.sharding import PartitionSpec as P

HEADS = 16
EPSILON = 1e-05
BF = jnp.bfloat16
F32 = jnp.float32
MESH = pl.DeviceIdType.MESH


def log2(n):
    return n.bit_length() - 1

def entry_barrier(partners):
    barrier = pltpu.get_barrier_semaphore()
    for partner in partners:
        pl.semaphore_signal(barrier, inc=1, device_id=partner, device_id_type=MESH)
    pl.semaphore_wait(barrier, len(partners))

def bit_of(value, bit):
    return lax.rem(value // (1 << bit), 2)

def flip(value, bit):
    return value + (1 - 2 * bit_of(value, bit)) * (1 << bit)

CHUNK_ROWS = 512
CHUNK_COLUMNS = 512
KINDS = (0, 2, 0, 2, 1, 0)


def al(value, by):
    return value if isinstance(value, int) else pl.multiple_of(value, by)


def stage_orders(ndp, nf):
    outer = [("outer", b) for b in range(log2(nf) - 1, 0, -1)]
    near = [("near", b) for b in range(log2(ndp))]
    return (
        outer + near,
        near[:1] + outer + near[1:],
        outer + near[1:2] + near[:1] + near[2:],
    )


def chunk_list(ndp, nf, shapes, kinds):
    chunks = []
    for i, (r, c) in enumerate(shapes):
        rn = min(CHUNK_ROWS // nf, r // nf)
        cn = min(max(CHUNK_COLUMNS, (128 * 16 * ndp) // rn), c)
        for r0 in range(0, r // nf, rn):
            for c0 in range(0, c, cn):
                chunks.append((i, r0, c0, rn, cn, kinds[len(chunks) % len(kinds)]))
    return tuple(chunks)


def lag_of(chunks):
    return 3 if chunks[0][4] <= 512 else 2


def halvings(order, half, rn, cn):
    left, blocks = [], half
    for kind, _ in order:
        if kind == "outer":
            blocks //= 2
            axis = 0
        elif rn >= 32:
            rn //= 2
            axis = 1
        else:
            cn //= 2
            axis = 2
        left.append((blocks, rn, cn, axis))
    return left


def engine_scratch(ndp, nf, chunks):
    orders, half = stage_orders(ndp, nf), nf // 2
    rn, cn = max(c[3] for c in chunks), max(c[4] for c in chunks)
    lag = lag_of(chunks)
    scratch = [
        pltpu.VMEM((lag * (len(orders[0]) + 1), half, rn, cn), jnp.bfloat16),
        pltpu.VMEM((2 * lag, half, rn, cn), jnp.bfloat16),
        pltpu.VMEM((len(chunks), rn, cn), jnp.bfloat16),
    ]
    for kind, order in enumerate(orders):
        mine = [c for c in chunks if c[5] == kind]
        if mine:
            sizes = [halvings(order, half, c[3], c[4]) for c in mine]
            for s in range(len(order)):
                most = tuple(max(size[s][a] for size in sizes) for a in range(3))
                scratch.append(pltpu.VMEM((2 * lag,) + most, jnp.bfloat16))
    copies = len(chunks) * (half + len(orders[0]) + log2(ndp))
    return scratch + [
        pltpu.SemaphoreType.DMA((copies,)),
        pltpu.SemaphoreType.DMA((copies,)),
        pltpu.SemaphoreType.DMA((len(chunks) * half,)),
        pltpu.SemaphoreType.DMA((len(chunks),)),
    ]


class Engine:
    def __init__(self, ndp, nf, chunks, refs, source, target):
        self.nf, self.chunks, self.source, self.target = nf, chunks, source, target
        self.orders, self.half = stage_orders(ndp, nf), nf // 2
        self.dbits, self.lag = log2(ndp), lag_of(chunks)
        self.held_slots, self.core_slots = self.lag * (len(self.orders[0]) + 1), 2 * self.lag
        self.held, self.from_core, self.done = refs[:3]
        self.landing = {}
        at = 3
        for kind in range(len(self.orders)):
            if any(c[5] == kind for c in chunks):
                for s in range(len(self.orders[0])):
                    self.landing[kind, s] = refs[at]
                    at += 1
        self.send, self.recv, self.local, self.store = refs[at:]
        self.dp, self.me = lax.axis_index("dp"), lax.axis_index("fsdp")
        self.core = lax.rem(self.me, 2)
        self.sibling = (self.dp, flip(self.me, 0))
        self.partner = {("outer", b): (self.dp, flip(self.me, b)) for b in range(1, log2(nf))}
        self.partner.update({("near", b): (flip(self.dp, b), self.me) for b in range(self.dbits)})
        self.started, self.state, self.stores, self.used = [], {}, [], {}
        self.sends = {}
        counts = {}
        self.index = []
        for c in chunks:
            self.index.append(counts.get(c[5], 0) % (2 * self.lag))
            counts[c[5]] = counts.get(c[5], 0) + 1
        self.stages = 2 + len(self.orders[0]) + self.dbits
        self.steps = len(chunks) + self.lag * (self.stages - 1)
        entry_barrier([self.sibling] + list(self.partner.values()))

    def push(self, src, dst, partner, holder=None):
        k = len(self.started)
        copy = pltpu.make_async_remote_copy(
            src, dst, self.send.at[k], self.recv.at[k], device_id=partner, device_id_type=MESH
        )
        copy.start()
        self.started.append([copy, False, False])
        if holder is not None:
            self.sends.setdefault(holder, []).append(k)
        return k

    def arrive(self, k):
        self.started[k][0].wait_recv()
        self.started[k][1] = True

    def sent(self, holder):
        for k in self.sends.pop(holder, []):
            self.started[k][0].wait_send()
            self.started[k][2] = True

    def block_row(self, j, b, other):
        i, r0 = self.chunks[j][:2]
        core = 1 - self.core if other else self.core
        return (2 * b + core, r0)

    def slot(self, j):
        return j % self.held_slots

    def room(self, j):
        self.sent(("held", self.slot(j)))

    def stage(self, j, s):
        i, r0, c0, rn, cn, kind = self.chunks[j]
        order = self.orders[kind]
        held, slot = self.held, self.slot(j)
        last = len(order)
        if s == 0:
            self.room(j)
            self.state[j] = self.source(self, j)
            return
        if s == 1:
            loads, sends = self.state[j]
            for copy in loads:
                copy.wait()
            for k in sends:
                self.arrive(k)
            held[slot, :, :rn, :cn] += self.from_core[j % self.core_slots, :, :rn, :cn]
            now, history = ((0, self.half), (0, rn), (0, cn)), []
        elif s <= last + 1:
            k, now, history = self.state[j]
            self.arrive(k)
            (b0, bn), (ra, rr), (ca, cc) = now
            arrived = self.landing[kind, s - 2][self.index[j], :bn, :rr, :cc]
            total = held[slot, pl.ds(b0, bn), pl.ds(ra, rr), pl.ds(ca, cc)] + arrived
            if s == last + 1:
                self.done[j, pl.ds(ra, rr), pl.ds(ca, cc)] = total[0]
            else:
                held[slot, pl.ds(b0, bn), pl.ds(ra, rr), pl.ds(ca, cc)] = total
        if s <= last:
            name, bit = order[s - 1]
            axis = halvings(order, self.half, rn, cn)[s - 1][3]
            mine = bit_of(self.me if name == "outer" else self.dp, bit)
            start, size = now[axis]
            size //= 2
            by = (1, 16, 128)[axis]
            keep, give = list(now), list(now)
            keep[axis] = (al(start + mine * size, by), size)
            give[axis] = (al(start + (1 - mine) * size, by), size)
            src = held.at[(slot,) + tuple(pl.ds(*g) for g in give)]
            dst = self.landing[kind, s - 1].at[(self.index[j],) + tuple(pl.ds(0, g[1]) for g in give)]
            k = self.push(src, dst, self.partner[name, bit], ("held", slot))
            if name == "near":
                history = history + [(bit, now[1:])]
            self.state[j] = (k, tuple(keep), history)
            return
        if s > last + 1:
            k, _, history = self.state[j]
            self.arrive(k)
            at, history = history[-1][1], history[:-1]
        else:
            at = now[1:]
        if history:
            piece = self.done.at[(j,) + tuple(pl.ds(*a) for a in at)]
            k = self.push(piece, piece, self.partner["near", history[-1][0]])
            self.state[j] = (k, None, history)
        else:
            copy = pltpu.make_async_copy(
                self.done.at[j, pl.ds(0, rn), pl.ds(0, cn)], self.target(j), self.store.at[j]
            )
            copy.start()
            self.stores.append(copy)

    def step(self, t):
        for s in range(self.stages - 1, -1, -1):
            j = t - self.lag * s
            if 0 <= j < len(self.chunks):
                self.stage(j, s)

    def finish(self):
        for copy, seen, left in self.started:
            if not left:
                copy.wait_send()
            if not seen:
                copy.wait_recv()
        for copy in self.stores:
            copy.wait()


def nt(left, right):
    return lax.dot_general(left, right, (((1,), (1,)), ((), ())), preferred_element_type=F32)


def nn(left, right):
    return jnp.dot(left, right, preferred_element_type=F32)


def attend_math(q, k, v, probs_ref):
    dim = q.shape[1] // 2
    first = lax.broadcasted_iota(jnp.int32, q.shape, 1) < dim
    parts = []
    for h in range(2):
        one = jnp.where(first if h == 0 else ~first, q, jnp.zeros_like(q))
        scores = nt(one, k)
        powers = jnp.exp(scores - jnp.max(scores, axis=1, keepdims=True))
        probs = (powers * (1.0 / jnp.sum(powers, axis=1, keepdims=True))).astype(BF)
        probs_ref[h] = probs
        parts.append(nn(probs, v))
    return jnp.where(first, parts[0], parts[1]).astype(BF)


def attend_back_math(q, k, v, o, do, probs, scale):
    dim = q.shape[1] // 2
    first = lax.broadcasted_iota(jnp.int32, q.shape, 1) < dim
    product = do.astype(F32) * o.astype(F32)
    q_t, do_t = q.T, do.T
    dqs, dks, dvs = [], [], []
    for h in range(2):
        mine = first if h == 0 else ~first
        inner = jnp.sum(jnp.where(mine, product, 0.0), axis=1, keepdims=True)
        p = probs(h)
        d_probs = nt(jnp.where(mine, do, jnp.zeros_like(do)), v)
        d_scores = (p.astype(F32) * (d_probs - inner)).astype(BF)
        dqs.append(nn(d_scores, k))
        dks.append(nn(q_t[h * dim : (h + 1) * dim], d_scores))
        dvs.append(nn(do_t[h * dim : (h + 1) * dim], p))
    dq = jnp.where(first, dqs[0], dqs[1]).astype(BF) * BF(scale)
    return dq, jnp.concatenate(dks, axis=0).T.astype(BF), jnp.concatenate(dvs, axis=0).T.astype(BF)


def attend_back_kernel(scale, q_ref, k_ref, v_ref, o_ref, do_ref, probs_ref, dq_ref, dk_ref, dv_ref):
    dq_ref[...], dk_ref[...], dv_ref[...] = attend_back_math(
        q_ref[...], k_ref[...], v_ref[...], o_ref[...], do_ref[...], lambda h: probs_ref[h], scale
    )


def attention_back(q, k, v, o, do, probs):
    length, width = q.shape
    pair = 2 * (width // HEADS)
    scale = 1.0 / math.sqrt(width // HEADS)
    cols = pl.BlockSpec((length, pair), lambda p: (0, p))
    return pl.pallas_call(
        functools.partial(attend_back_kernel, scale),
        grid=(HEADS // 2,),
        in_specs=[cols] * 5 + [pl.BlockSpec((2, length, length), lambda p: (p, 0, 0))],
        out_specs=[cols] * 3,
        out_shape=[jax.ShapeDtypeStruct((length, width), BF)] * 3,
        compiler_params=pltpu.CompilerParams(vmem_limit_bytes=40 * 1024 * 1024),
        name="attend_back",
    )(q, k, v, o, do, probs)


TILE = 256
STAGED = 4
CUTS = 4
SKEW = 2


def tiles(count, body):
    lax.fori_loop(0, count, lambda n, c: (body(pl.multiple_of(n * TILE, TILE)), c)[1], 0, unroll=True)


class Loads:
    def __init__(self, sem, ring, items):
        self.sem, self.ring, self.items, self.next, self.copies = sem, ring, items, 0, {}

    def start(self):
        if self.next < len(self.items):
            k = self.next
            self.next += 1
            group = []
            for n, (src, dst) in enumerate(self.items[k](k % self.ring)):
                copy = pltpu.make_async_copy(src, dst, self.sem.at[k % self.ring, n])
                copy.start()
                group.append(copy)
            self.copies[k] = group

    def wait(self, k):
        for copy in self.copies.pop(k):
            copy.wait()
        return k % self.ring


def tail_kernel(ndp, nf, shapes, chunks, scale, *refs):
    (
        w_down, w_up, w_out, w_qkv, slope, d_hf, unit, df1, df2, du2, dz2, dqkv2,
        a1, a2, h1, h2, o1, o2, x1, x2, q, k, v, o, probs, sums_in, gain, inverse, entry_hot,
    ) = refs[:29]
    outs, g0 = refs[29:34], refs[34]
    (
        r_down, r_up, r_out, r_qkv, r_qkv2, lhs, turned, staged, gh, unit_v, weight, slope_v, pair_v,
        do, probs_v, sums, w_sem, s_sem, p_sem, l_sem, m_sem,
    ) = refs[35:56]
    tokens, width = df1.shape
    part = min(1024, width)
    ff = w_down.shape[0]
    parts = ff // part
    wide = part // TILE
    pair = pair_v.shape[3]
    pairs = width // pair
    n_mid = 3

    misc = []
    def load(src, dst):
        copy = pltpu.make_async_copy(src, dst, m_sem.at[len(misc)])
        copy.start()
        misc.append(copy)
        return copy

    need_df = [load(df1, r_down.at[0]), load(df2, r_down.at[1])]
    need_hf = [load(d_hf, gh), load(unit, unit_v)]
    need_sums = load(sums_in, sums)
    need_du2 = load(du2, r_up.at[1])
    need_dz2 = load(dz2, r_out.at[1])
    need_dqkv2 = load(dqkv2, r_qkv2)

    columns = lambda t: pl.ds(t * part, part)
    weights = Loads(w_sem, 2, (
        [lambda s, t=t: [(w_down.at[columns(t)], weight.at[s])] for t in range(parts)]
        + [lambda s, t=t: [(w_up.at[:, columns(t)], weight.at[s])] for t in range(parts)]
        + [lambda s: [(w_out, weight.at[s])]]
        + [lambda s, t=t: [(w_qkv.at[:, columns(t)], weight.at[s])] for t in range(n_mid)]
    ))
    slopes = Loads(s_sem, 2, [lambda s, t=t: [(slope.at[:, columns(t)], slope_v.at[s])] for t in range(parts)])
    heads = Loads(p_sem, 2, [
        lambda s, p=p: [(t.at[:, pl.ds(p * pair, pair)], pair_v.at[s, n]) for n, t in enumerate((q, k, v, o))]
        + [(probs.at[pl.ds(2 * p, 2)], probs_v.at[s])]
        for p in range(pairs)
    ])
    lefts = ((a1, a2), (h1, h2), (o1, o2), (x1, x2))

    def left_item(i, r0, rn):

        def item(s):
            block = shapes[i][0] // nf
            core = lax.rem(lax.axis_index("fsdp"), 2)
            out = []
            for app in range(2):
                for n in range(nf):
                    f = 2 * n + core if n < nf // 2 else 2 * (n - nf // 2) + 1 - core
                    features = pl.ds(pl.multiple_of(f * block + r0, rn), rn)
                    if rn % 128 == 0:
                        out.append((lefts[i][app].at[:, features], lhs.at[s, app, n]))
                    else:
                        out.append((lefts[i][app].at[features], lhs.at[s, app, n]))
            return out

        return item

    groups = list(dict.fromkeys((c[0], c[1], c[3]) for c in chunks if c[0] < 4))
    left = Loads(l_sem, 2, [left_item(*g) for g in groups])
    rights = (
        lambda app, at: r_down[app, :, at],
        lambda app, at: r_up[app, :, at],
        lambda app, at: r_out[app, :, at],
        lambda app, at: r_qkv[:, at] if app == 0 else r_qkv2[:, at],
    )

    def source(engine, j):
        i, r0, c0, rn, cn, _ = chunks[j]
        slot, s = engine.slot(j), j % STAGED
        engine.sent(("staged", s))
        half = nf // 2
        if i < 4:
            if c0 == 0:
                buffer = left.wait(groups.index((i, r0, rn)))
                for app in range(2):
                    for n in range(nf):
                        block = lhs[buffer, app, n]
                        turned[pl.ds(n * rn, rn), pl.ds(app * tokens, tokens)] = block.T if rn % 128 == 0 else block
                left.start()

            def tile(at):
                right = pl.ds(c0 + at, TILE)
                total = nn(turned[:, :tokens], rights[i](0, right)) + nn(turned[:, tokens:], rights[i](1, right))
                total = total.astype(BF).reshape(nf, rn, TILE)
                engine.held[slot, :, :, pl.ds(at, TILE)] = total[:half]
                staged[s, :, :, pl.ds(at, TILE)] = total[half:]

            tiles(cn // TILE, tile)
        else:
            block = sums[pl.ds(r0, rn), pl.ds(c0, cn)].astype(BF)
            for b in range(half):
                engine.held[slot, b, :rn, :cn] = block
                staged[s, b, :rn, :cn] = block
        src = staged.at[s, :, pl.ds(0, rn), pl.ds(0, cn)]
        dst = engine.from_core.at[j % engine.core_slots, :, pl.ds(0, rn), pl.ds(0, cn)]
        return [], [engine.push(src, dst, engine.sibling, ("staged", s))]

    def target(j):
        i, r0, c0, rn, cn, _ = chunks[j]
        return outs[i].at[pl.ds(r0, rn), pl.ds(c0, cn)]

    def task_du(t):
        def run():
            s = weights.wait(t)
            slopes.wait(t)

            def tile(at):
                d = nt(r_down[0], weight[s, pl.ds(at, TILE), :])
                du = (d * slope_v[t % 2, :, pl.ds(at, TILE)].astype(F32)).astype(BF)
                r_up[0, :, pl.ds(t * part + at, TILE)] = du
                sums[5 + t : 6 + t, pl.ds(at, TILE)] += jnp.sum(du.astype(F32), axis=0, keepdims=True)

            tiles(wide, tile)
            weights.start()
            slopes.start()
        return run

    def task_gh(t):
        def run():
            if t == 0:
                for copy in need_hf:
                    copy.wait()
            s = weights.wait(parts + t)

            def tile(at):
                gh[:, pl.ds(at, TILE)] += nt(r_up[0, :, t * part : (t + 1) * part], weight[s, pl.ds(at, TILE), :])

            tiles(wide, tile)
            weights.start()
        return run

    def task_norm():
        def tile(at):
            rows = pl.ds(at, TILE)
            g, u = gh[rows, :], unit_v[rows, :].astype(F32)
            gg = g * gain[...]
            m1 = jnp.mean(gg, axis=1, keepdims=True)
            m2 = jnp.mean(gg * u, axis=1, keepdims=True)
            d = (gg - m1 - u * m2) * inverse[rows, :]
            gh[rows, :] = d
            dz = d.astype(BF)
            r_out[0, rows, :] = dz
            total = lambda t: jnp.sum(t, axis=0, keepdims=True)
            sums[2:3, :] += total(dz.astype(F32))
            sums[3:4, :] += total(g * u)
            sums[4:5, :] += total(g)

        tiles(tokens // TILE, tile)
        need_dz2.wait()

    def task_do():
        s = weights.wait(2 * parts)

        def tile(at):
            do[:, pl.ds(at, TILE)] = nt(r_out[0], weight[s, pl.ds(at, TILE), :]).astype(BF)

        tiles(width // TILE, tile)
        weights.start()

    def task_heads(p):
        def run():
            s = heads.wait(p)
            at = slice(p * pair, (p + 1) * pair)
            dq, dk, dv = attend_back_math(
                pair_v[s, 0], pair_v[s, 1], pair_v[s, 2], pair_v[s, 3], do[:, at], lambda h: probs_v[s, h], scale
            )
            r_qkv[:, at] = dq
            r_qkv[:, width + p * pair : width + (p + 1) * pair] = dk
            r_qkv[:, 2 * width + p * pair : 2 * width + (p + 1) * pair] = dv
            total = lambda t: jnp.sum(t.astype(F32), axis=0, keepdims=True)
            sums[0:1, at] += total(dq)
            sums[1:2, at] += total(dv)
            heads.start()
        return run

    def task_back(t):
        def run():
            s = weights.wait(2 * parts + 1 + t)

            def tile(at):
                gh[:, pl.ds(at, TILE)] += nt(r_qkv[:, t * part : (t + 1) * part], weight[s, pl.ds(at, TILE), :])

            tiles(wide, tile)
            weights.start()
        return run

    def task_table():
        def tile(at):
            g = gh[:, pl.ds(at, TILE)]
            high = g.astype(BF)
            rest = (g - high.astype(F32)).astype(BF)
            sums[16:48, pl.ds(at, TILE)] += nn(entry_hot[...], high) + nn(entry_hot[...], rest)

        tiles(width // TILE, tile)
        load(gh, g0)

    for _ in range(2):
        weights.start()
        slopes.start()
        left.start()
        heads.start()
    engine = Engine(ndp, nf, chunks, refs[56:], source, target)
    for copy in need_df:
        copy.wait()
    need_sums.wait()
    counts = [sum(c[0] == i for c in chunks) for i in range(5)]
    first = [sum(counts[:i]) for i in range(5)]
    early = [task_du(t) for t in range(parts)] + [task_gh(t) for t in range(parts)]
    middle = [task_norm, task_do] + [task_heads(p) for p in range(pairs)]
    late = [task_back(t) for t in range(n_mid)] + [task_table]
    plan = {}

    def spread(tasks, begin, end):
        for n, task in enumerate(tasks):
            plan.setdefault(begin + n * (end - begin) // len(tasks), []).append(task)

    spread(early, 0, first[1])
    spread(middle, first[1], first[3] - 1)
    spread(late, first[3], first[4])
    for t in range(engine.steps):
        if t == first[1]:
            need_du2.wait()
        if t == first[3]:
            need_dqkv2.wait()
        engine.step(t)
        for task in plan.get(t, ()):
            task()
    engine.finish()
    misc[-1].wait()


def tail(ndp, nf, collective_id, scale, big, gain, inverse, entry_hot):
    w_down, w_up, w_out, w_qkv = big[:4]
    df1 = big[7]
    tokens, width = df1.shape
    ff = w_down.shape[0]
    extra = big[25].shape[0]
    shapes = (w_down.shape, w_up.shape, w_out.shape, w_qkv.shape, (nf * extra, width))
    chunks = chunk_list(ndp, nf, shapes, KINDS)
    half = nf // 2
    part = min(1024, width)
    pair = 2 * (width // HEADS)
    rn = chunks[0][3]
    if rn % 128:
        big = big[:12] + [t.T for t in big[12:20]] + big[20:]
    any_space = pl.BlockSpec(memory_space=pl.ANY)
    vmem = pl.BlockSpec(memory_space=pltpu.VMEM)
    return pl.pallas_call(
        functools.partial(tail_kernel, ndp, nf, shapes, chunks, scale),
        out_shape=[jax.ShapeDtypeStruct((r // nf, c), BF) for r, c in shapes]
        + [jax.ShapeDtypeStruct((tokens, width), F32)],
        in_specs=[any_space] * len(big) + [vmem] * 3,
        out_specs=[any_space] * 6,
        scratch_shapes=[
            pltpu.VMEM((2, tokens, width), BF),
            pltpu.VMEM((2, tokens, ff), BF),
            pltpu.VMEM((2, tokens, width), BF),
            pltpu.VMEM((tokens, 3 * width), BF),
            pltpu.VMEM((tokens, 3 * width), BF),
            pltpu.VMEM((2, 2, nf, tokens, rn) if rn % 128 == 0 else (2, 2, nf, rn, tokens), BF),
            pltpu.VMEM((nf * rn, 2 * tokens), BF),
            pltpu.VMEM((STAGED, half, rn, chunks[0][4]), BF),
            pltpu.VMEM((tokens, width), F32),
            pltpu.VMEM((tokens, width), BF),
            pltpu.VMEM((2, part, width), BF),
            pltpu.VMEM((2, tokens, part), BF),
            pltpu.VMEM((2, 4, tokens, pair), BF),
            pltpu.VMEM((tokens, width), BF),
            pltpu.VMEM((2, 2, tokens, tokens), BF),
            pltpu.VMEM((extra, width), F32),
            pltpu.SemaphoreType.DMA((2, 1)),
            pltpu.SemaphoreType.DMA((2, 1)),
            pltpu.SemaphoreType.DMA((2, 5)),
            pltpu.SemaphoreType.DMA((2, 2 * nf)),
            pltpu.SemaphoreType.DMA((16,)),
        ]
        + engine_scratch(ndp, nf, chunks),
        compiler_params=pltpu.CompilerParams(
            collective_id=collective_id, has_side_effects=True, vmem_limit_bytes=61 * 1024 * 1024
        ),
        name="tail",
    )(*big, gain, inverse, entry_hot)


LAYER = ("low", "q", "k", "v", "mixed", "probs", "unit1", "inv1", "hidden", "active", "slope", "unit2", "inv2")


def head_kernel(ndp, nf, shapes, scale, *refs):
    n = len(shapes)
    ins, small, tokens_ref, keep, row_hot, table = refs[:n], refs[n], refs[n + 1], refs[n + 2], refs[n + 3], refs[n + 4]
    refs = refs[n + 5 :]
    full_out, vec_out, final_out = refs[:n], refs[n], refs[n + 1]
    kept = [dict(zip(LAYER, refs[n + 2 + k * len(LAYER) :])) for k in range(2)]
    refs = refs[n + 2 + 2 * len(LAYER) :]
    full, refs = refs[:n], refs[n:]
    (
        small_all, vec, x, low, joined, mixed, hidden, active, slope, probs, unit, inv,
        send, recv, local, save_sem,
    ) = refs
    outs = full
    dp, me = lax.axis_index("dp"), lax.axis_index("fsdp")
    fbits = log2(nf)
    sibling = (dp, flip(me, 0))
    outer = [(dp, flip(me, b)) for b in range(1, fbits)]
    near = [(flip(dp, 0), me), (flip(dp, 1), me)]
    others = [(dp, lax.rem(me + d, nf)) for d in range(1, nf)]
    code = lax.rem(dp, 4)
    started, arrived, final_of = [], [], {i: [] for i in range(n)}
    own = []
    for i in range(n):
        r, c = shapes[i]
        copy = pltpu.make_async_copy(ins[i], full[i].at[pl.ds(pl.multiple_of(me * r, r), r)], local.at[i])
        copy.start()
        own.append(copy)
    own_small = pltpu.make_async_copy(small, small_all.at[me], local.at[n])
    own_small.start()
    entry_barrier(others + near)

    def push(src, dst, partner):
        k = len(started)
        copy = pltpu.make_async_remote_copy(src, dst, send.at[k], recv.at[k], device_id=partner, device_id_type=MESH)
        copy.start()
        started.append(copy)
        arrived.append(False)
        return k

    def arrive(k):
        if not arrived[k]:
            started[k].wait_recv()
            arrived[k] = True

    small_copies = [push(small, small_all.at[me], other) for other in others]

    def place(i, f, k, half):
        r, c = shapes[i]
        q, w = r // 4, c // CUTS
        return full[i].at[pl.ds(pl.multiple_of(f * r + k * q, 16), q), pl.ds(half * w, w)]

    items = [(i, h) for i in range(n) for h in range(CUTS)]
    waits, known = {}, {}

    def share(i, where):
        final_of[i].append(push(where, where, sibling))

    def stage(t, s):
        i, half = items[t]
        r, c = shapes[i]
        q, w = r // 4, c // CUTS
        p1, p2 = (0, 1) if half % 2 == 0 else (1, 0)
        src = ins[i].at[pl.ds(pl.multiple_of(code * q, 16), q), pl.ds(half * w, w)]
        at = lambda f, k: place(i, f, k, half)
        if s == 0:
            if fbits > 1:
                waits[t, "y", 1] = [(me, push(src, at(me, code), outer[0]))]
            whole = full[i].at[pl.ds(pl.multiple_of(me * r, r), r), pl.ds(half * w, w)]
            final_of[i].append(push(ins[i].at[:, pl.ds(half * w, w)], whole, sibling))
        elif s < fbits:
            got = []
            for f, copy in waits.pop((t, "y", s)):
                arrive(copy)
                got.append(flip(f, s))
            known.setdefault(t, []).extend(got)
            if s < fbits - 1:
                waits[t, "y", s + 1] = [(me, push(src, at(me, code), outer[s]))] + [
                    (f, push(at(f, code), at(f, code), outer[s])) for f in known[t]
                ]
            else:
                waits[t, "p1"] = [(f, push(at(f, code), at(f, code), near[p1])) for f in known[t]]
                waits[t, "p2a"] = [(f, push(at(f, code), at(f, code), near[p2])) for f in known[t]]
            for f in got:
                share(i, at(f, code))
        elif s == fbits:
            k = flip(code, p1)
            waits[t, "p2b"] = []
            for f, copy in waits.pop((t, "p1")):
                arrive(copy)
                waits[t, "p2b"].append((f, push(at(f, k), at(f, k), near[p2])))
                share(i, at(f, k))
        else:
            k = flip(code, p2) if s == fbits + 1 else flip(flip(code, p2), p1)
            for f, copy in waits.pop((t, "p2a" if s == fbits + 1 else "p2b")):
                arrive(copy)
                share(i, at(f, k))

    saves, pending = [], {}

    def save(name, src, dst):
        copy = pltpu.make_async_copy(src, dst, save_sem.at[len(saves)])
        copy.start()
        saves.append(copy)
        pending.setdefault(name, []).append(copy)

    def free(name):
        for copy in pending.pop(name, []):
            copy.wait()

    ready = set()

    def need(i):
        if i not in ready:
            ready.add(i)
            own[i].wait()
            for k in final_of[i]:
                arrive(k)
            save("full", full[i], full_out[i])

    tokens, width = x.shape
    part = min(1024, width)
    parts = shapes[2][1] // part
    pairs = HEADS // 2
    pair = width // pairs
    mine = width // nf

    def task_start():
        own_small.wait()
        for k in small_copies:
            arrive(k)
        row = 0
        for count in (2, 1, 1, 1, parts, 1, 1, 1):
            for f in range(nf):
                for i in range(count):
                    at = (f * count + i) * mine
                    vec[row + at // width : row + at // width + 1, at % width : at % width + mine] = small_all[
                        f, row + i : row + i + 1, :
                    ].astype(F32)
            row += count
        save("vec", vec, vec_out)

        def tile(at):
            rows = pl.ds(at, TILE)
            x0 = tokens_ref[rows, :].astype(F32) * keep[rows, :] + nn(row_hot[rows, :], table[...])
            x[rows, :] = x0
            low[rows, :] = x0.astype(BF)

        tiles(tokens // TILE, tile)
        save("low", low, kept[0]["low"])

    def task_joined(app, t):
        def run():
            need(0)
            free("qkv"[t])

            def tile(at):
                cols = pl.ds(t * width + at, TILE)
                value = nn(low[...], full[0][:, cols])
                if t == 0:
                    value = (value + vec[0:1, pl.ds(at, TILE)]) * scale
                if t == 2:
                    value = value + vec[1:2, pl.ds(at, TILE)]
                joined[:, cols] = value.astype(BF)

            tiles(width // TILE, tile)
            save("qkv"[t], joined.at[:, pl.ds(t * width, width)], kept[app]["qkv"[t]])
        return run

    def task_heads(app, p):
        def run():
            if p == 0:
                free("mixed")
            free(("probs", p % 2))
            at = lambda t: slice(t * width + p * pair, t * width + (p + 1) * pair)
            mixed[:, at(0)] = attend_math(joined[:, at(0)], joined[:, at(1)], joined[:, at(2)], probs.at[p % 2])
            save(("probs", p % 2), probs.at[p % 2], kept[app]["probs"].at[pl.ds(2 * p, 2)])
            if p == pairs - 1:
                save("mixed", mixed, kept[app]["mixed"])
        return run

    def norm(t, gain, shift):
        mean = jnp.mean(t, axis=1, keepdims=True)
        centred = t - mean
        spread = jnp.mean(centred * centred, axis=1, keepdims=True)
        inverse = lax.rsqrt(spread + EPSILON)
        normal = centred * inverse
        return normal * vec[gain : gain + 1, :] + vec[shift : shift + 1, :], normal.astype(BF), inverse

    def task_out(app):
        def run():
            need(1)
            free("hidden")
            free("unit1")
            free("inv1")

            def tile(at):
                rows = pl.ds(at, TILE)
                t = x[rows, :] + nn(mixed[rows, :], full[1][...]) + vec[2:3, :]
                h, unit[0, rows, :], inv[0, rows, :] = norm(t, 3, 4)
                x[rows, :] = h
                hidden[rows, :] = h.astype(BF)

            tiles(tokens // TILE, tile)
            save("unit1", unit.at[0], kept[app]["unit1"])
            save("inv1", inv.at[0], kept[app]["inv1"])
            save("hidden", hidden, kept[app]["hidden"])
        return run

    def task_up(app, t):
        def run():
            need(2)
            free(("active", t))
            free(("slope", t % 2))

            def tile(at):
                cols = pl.ds(t * part + at, TILE)
                u = nn(hidden[...], full[2][:, cols]) + vec[5 + t : 6 + t, pl.ds(at, TILE)]
                below = 0.5 + 0.5 * lax.erf(u * math.sqrt(0.5))
                active[:, cols] = (u * below).astype(BF)
                bell = math.sqrt(0.5 / math.pi) * jnp.exp(-0.5 * u * u)
                slope[t % 2, :, pl.ds(at, TILE)] = (below + u * bell).astype(BF)

            tiles(part // TILE, tile)
            cols = pl.ds(t * part, part)
            save(("active", t), active.at[:, cols], kept[app]["active"].at[:, cols])
            save(("slope", t % 2), slope.at[t % 2], kept[app]["slope"].at[:, cols])
        return run

    def task_down(app):
        def run():
            need(3)
            free("low")
            free("unit2")
            free("inv2")

            def tile(at):
                rows = pl.ds(at, TILE)
                t = x[rows, :] + nn(active[rows, :], full[3][...]) + vec[5 + parts : 6 + parts, :]
                y, unit[1, rows, :], inv[1, rows, :] = norm(t, 6 + parts, 7 + parts)
                x[rows, :] = y
                low[rows, :] = y.astype(BF)

            tiles(tokens // TILE, tile)
            save("unit2", unit.at[1], kept[app]["unit2"])
            save("inv2", inv.at[1], kept[app]["inv2"])
            save("low", low, final_out if app else kept[1]["low"])
        return run

    first = lambda app: [task_joined(app, t) for t in range(3)] + [task_heads(app, p) for p in range(pairs)] + [task_out(app)]
    second = lambda app: [task_up(app, t) for t in range(parts)]
    stages = fbits + 3
    ahead = 2
    steps = len(items) + SKEW * (stages - 1)
    done_at = lambda i: CUTS * (i + 1) - 1 + SKEW * (stages - 1)
    plan = {}

    def spread(tasks, begin, end):
        for k, task in enumerate(tasks):
            plan.setdefault(min(begin + k * (end - begin) // len(tasks), steps), []).append(task)

    spread([task_start], 0, 1)
    spread(first(0), done_at(0) + 1, done_at(2) + 1)
    spread(second(0), done_at(2) + 1, steps)
    spread([task_down(0)] + first(1) + second(1) + [task_down(1)], steps, steps)
    for step in range(-ahead, steps):
        for s in range(stages - 1, -1, -1):
            t = step - SKEW * s if s else step + ahead
            if 0 <= t < len(items):
                stage(t, s)
        for task in plan.get(step, ()):
            task()
    for task in plan[steps]:
        task()
    for copy in started:
        copy.wait_send()
    for k in range(len(started)):
        arrive(k)
    for name in list(pending):
        free(name)


def head(ndp, nf, collective_id, scale, shards, small, tokens, keep, row_hot, table):
    shapes = tuple(s.shape for s in shards)
    length, width = tokens.shape
    ff = shapes[2][1]
    part = min(1024, width)
    kinds = dict(
        low=((length, width), BF), q=((length, width), BF), k=((length, width), BF), v=((length, width), BF),
        mixed=((length, width), BF), probs=((HEADS, length, length), BF), unit1=((length, width), BF),
        inv1=((length, 1), F32), hidden=((length, width), BF), active=((length, ff), BF), slope=((length, ff), BF),
        unit2=((length, width), BF), inv2=((length, 1), F32),
    )
    full = [(nf * r, c) for r, c in shapes]
    out_shape = [jax.ShapeDtypeStruct(s, BF) for s in full]
    out_shape += [jax.ShapeDtypeStruct((small.shape[0], width), F32), jax.ShapeDtypeStruct((length, width), BF)]
    out_shape += [jax.ShapeDtypeStruct(*kinds[name]) for _ in range(2) for name in LAYER]
    per_item = (nf // 2 - 1) * 8 + 1
    copies = nf - 1 + CUTS * len(shards) * per_item
    any_space = pl.BlockSpec(memory_space=pl.ANY)
    vmem = pl.BlockSpec(memory_space=pltpu.VMEM)
    outs = pl.pallas_call(
        functools.partial(head_kernel, ndp, nf, shapes, scale),
        out_shape=out_shape,
        in_specs=[any_space] * (len(shards) + 1) + [vmem] * 4,
        out_specs=[any_space] * len(out_shape),
        scratch_shapes=[pltpu.VMEM(s, BF) for s in full]
        + [
            pltpu.VMEM((nf,) + small.shape, BF),
            pltpu.VMEM((small.shape[0], width), F32),
            pltpu.VMEM((length, width), F32),
            pltpu.VMEM((length, width), BF),
            pltpu.VMEM((length, 3 * width), BF),
            pltpu.VMEM((length, width), BF),
            pltpu.VMEM((length, width), BF),
            pltpu.VMEM((length, ff), BF),
            pltpu.VMEM((2, length, part), BF),
            pltpu.VMEM((2, 2, length, length), BF),
            pltpu.VMEM((2, length, width), BF),
            pltpu.VMEM((2, length, 1), F32),
            pltpu.SemaphoreType.DMA((copies,)),
            pltpu.SemaphoreType.DMA((copies,)),
            pltpu.SemaphoreType.DMA((len(shards) + 1,)),
            pltpu.SemaphoreType.DMA((96,)),
        ],
        compiler_params=pltpu.CompilerParams(
            collective_id=collective_id, has_side_effects=True, vmem_limit_bytes=61 * 1024 * 1024
        ),
        name="head",
    )(*shards, small, tokens, keep, row_hot, table)
    n = len(shards)
    kept = [dict(zip(LAYER, outs[n + 2 + k * len(LAYER) :])) for k in range(2)]
    return outs[:n], outs[n], outs[n + 1], kept


def dot(left, right):
    return jnp.dot(left, right, preferred_element_type=F32)


def back_dot(left, right):
    return lax.dot_general(left, right, (((1,), (1,)), ((), ())), preferred_element_type=F32)


def outer_dot(left, right):
    return lax.dot_general(left, right, (((0,), (0,)), ((), ())), preferred_element_type=F32)


def norm_back(g, unit, inverse, gain):
    d_gain = jnp.sum(g * unit, axis=0)
    d_shift = jnp.sum(g, axis=0)
    gg = g * gain
    m1 = jnp.mean(gg, axis=-1, keepdims=True)
    m2 = jnp.mean(gg * unit, axis=-1, keepdims=True)
    return (gg - m1 - unit * m2) * inverse, d_gain, d_shift


def backward(g, kept, w, length):
    width = g.shape[1]
    scale = 1.0 / math.sqrt(width // HEADS)
    total = lambda t: jnp.sum(t.astype(F32), axis=0)
    d_hf, d_gain2, d_bias2 = norm_back(g, kept["unit2"], kept["inv2"], w["gain2"])
    df = d_hf.astype(BF)
    du = (back_dot(df, w["down"]) * kept["slope"].astype(F32)).astype(BF)
    gh = d_hf + back_dot(du, w["up"])
    d_xz, d_gain1, d_bias1 = norm_back(gh, kept["unit1"], kept["inv1"], w["gain1"])
    dz = d_xz.astype(BF)
    d_mixed = back_dot(dz, w["out"]).astype(BF)
    dq, dk, dv = attention_back(kept["q"], kept["k"], kept["v"], kept["mixed"], d_mixed, kept["probs"])
    d_joined = jnp.concatenate([dq, dk, dv], axis=1)
    d_rows = d_xz + back_dot(d_joined, w["qkv"])
    sums = [total(dq), total(dv), total(dz), d_gain1, d_bias1, *total(du).reshape(-1, width), total(df), d_gain2, d_bias2]
    return d_rows, dict(df=df, du=du, dz=dz, d_joined=d_joined), sums


def shards(ndp, nf, tokens, mask_positions, mask_counts, replace_ids, cotangent, replace_table,
           w_qkv, b_qv, w_out, b_out, norm1_gain, norm1_bias, w_up, b_up, w_down, b_down, norm2_gain, norm2_bias):
    length, width = tokens.shape
    slots = mask_positions.shape[1]
    used = (jnp.arange(slots, dtype=jnp.int32) < mask_counts[0]).astype(F32)
    places = jnp.arange(length, dtype=jnp.int32)
    position_hot = (mask_positions[0][:, None] == places[None, :]).astype(F32) * used[:, None]
    entries = jnp.arange(replace_table.shape[0], dtype=jnp.int32)
    vocab_hot = (replace_ids[0][:, None] == entries[None, :]).astype(BF)
    row_hot = outer_dot(position_hot.astype(BF), vocab_hot).astype(BF)
    keep = 1.0 - jnp.sum(position_hot, axis=0)[:, None]
    entries = replace_table.shape[0]
    mine = width // nf
    small = jnp.zeros((16, mine), BF)
    at = 0
    for vector in (b_qv, b_out, norm1_gain, norm1_bias, b_up, b_down, norm2_gain, norm2_bias):
        rows = vector.shape[0] // mine
        small = small + jnp.pad(vector.reshape(rows, mine), ((at, 16 - at - rows), (0, 0)))
        at += rows
    scale = 1.0 / math.sqrt(width // HEADS)
    (qkv, out, up, down), vec, final, (kept_one, kept_two) = head(
        ndp, nf, 0, scale, [w_qkv, w_out, w_up, w_down], small, tokens, keep,
        jnp.pad(row_hot, ((0, 0), (0, 32 - entries))), jnp.pad(replace_table, ((0, 32 - entries), (0, 0))),
    )
    grown = w_up.shape[1] // width
    w = dict(qkv=qkv, out=out, up=up, down=down, gain1=vec[3], gain2=vec[6 + grown])

    d_middle, two, sums = backward(cotangent.astype(F32), kept_two, w, length)

    one = kept_one
    d_hf, d_gain2, d_bias2 = norm_back(d_middle, one["unit2"], one["inv2"], w["gain2"])
    df = d_hf.astype(BF)
    sums[-3:] = [sums[-3] + jnp.sum(df.astype(F32), axis=0), sums[-2] + d_gain2, sums[-1] + d_bias2]
    sums = jnp.pad(jnp.stack(sums), ((0, 64 - len(sums)), (0, 0)))
    entry_hot = jnp.pad(row_hot.T, ((0, 32 - entries), (0, 0)))
    big = [
        w["down"], w["up"], w["out"], w["qkv"], one["slope"], d_hf, one["unit1"],
        df, two["df"], two["du"], two["dz"], two["d_joined"],
        one["active"], kept_two["active"], one["hidden"], kept_two["hidden"], one["mixed"], kept_two["mixed"],
        one["low"], kept_two["low"], one["q"], one["k"], one["v"], one["mixed"], one["probs"], sums,
    ]
    g_down, g_up, g_out, g_qkv, extra, d_start = tail(
        ndp, nf, 1, scale, big, w["gain1"].reshape(1, width), one["inv1"], entry_hot
    )
    token_grad = d_start * keep
    up32 = lambda t: t.astype(F32)
    extra = up32(extra)
    table_grad = extra[16 : 16 + entries]
    place = lax.axis_index("fsdp")
    mine = lambda t: lax.dynamic_slice_in_dim(t, place * (t.shape[0] // nf), t.shape[0] // nf)
    v = [mine(extra[:2].reshape(-1))] + [mine(extra[n]) for n in (2, 3, 4)]
    v += [mine(extra[5 : 5 + grown].reshape(-1))] + [mine(extra[n + grown]) for n in (5, 6, 7)]
    return (
        final, token_grad, table_grad, up32(g_qkv), v[0], up32(g_out), v[1], v[2], v[3],
        up32(g_up), v[4], up32(g_down), v[5], v[6], v[7],
    )


def solution(mesh):
    both = P(("dp", "fsdp"))
    rows = P("fsdp")
    in_specs = (both,) * 5 + (P(),) + (rows,) * 12
    out_specs = (both, both, P()) + (rows,) * 12
    body = functools.partial(shards, mesh.shape["dp"], mesh.shape["fsdp"])
    return jax.shard_map(body, mesh=mesh, in_specs=in_specs, out_specs=out_specs, check_vma=False)
```

```python
import functools
import math

import jax
import jax.numpy as jnp
from jax import lax
from jax.experimental import pallas as pl
from jax.experimental.pallas import tpu as pltpu
from jax.sharding import PartitionSpec as P

HEADS = 16
EPSILON = 1e-05
BF = jnp.bfloat16
F32 = jnp.float32
MESH = pl.DeviceIdType.MESH


def log2(n):
    return n.bit_length() - 1

def entry_barrier(partners):
    barrier = pltpu.get_barrier_semaphore()
    for partner in partners:
        pl.semaphore_signal(barrier, inc=1, device_id=partner, device_id_type=MESH)
    pl.semaphore_wait(barrier, len(partners))

def bit_of(value, bit):
    return lax.rem(value // (1 << bit), 2)

def flip(value, bit):
    return value + (1 - 2 * bit_of(value, bit)) * (1 << bit)

CHUNK_ROWS = 512
CHUNK_COLUMNS = 512
KINDS = (0, 2, 0, 2, 1, 0)


def al(value, by):
    return value if isinstance(value, int) else pl.multiple_of(value, by)


def stage_orders(ndp, nf):
    outer = [("outer", b) for b in range(log2(nf) - 1, 0, -1)]
    near = [("near", b) for b in range(log2(ndp))]
    return (
        outer + near,
        near[:1] + outer + near[1:],
        outer + near[1:2] + near[:1] + near[2:],
    )


def chunk_list(ndp, nf, shapes, kinds):
    chunks = []
    for i, (r, c) in enumerate(shapes):
        rn = min(CHUNK_ROWS // nf, r // nf)
        cn = min(max(CHUNK_COLUMNS, (128 * 16 * ndp) // rn), c)
        for r0 in range(0, r // nf, rn):
            for c0 in range(0, c, cn):
                chunks.append((i, r0, c0, rn, cn, kinds[len(chunks) % len(kinds)]))
    return tuple(chunks)


def lag_of(chunks):
    return 3 if chunks[0][4] <= 512 else 2


def halvings(order, half, rn, cn):
    left, blocks = [], half
    for kind, _ in order:
        if kind == "outer":
            blocks //= 2
            axis = 0
        elif rn >= 32:
            rn //= 2
            axis = 1
        else:
            cn //= 2
            axis = 2
        left.append((blocks, rn, cn, axis))
    return left


def engine_scratch(ndp, nf, chunks):
    orders, half = stage_orders(ndp, nf), nf // 2
    rn, cn = max(c[3] for c in chunks), max(c[4] for c in chunks)
    lag = lag_of(chunks)
    scratch = [
        pltpu.VMEM((lag * (len(orders[0]) + 1), half, rn, cn), jnp.bfloat16),
        pltpu.VMEM((2 * lag, half, rn, cn), jnp.bfloat16),
        pltpu.VMEM((len(chunks), rn, cn), jnp.bfloat16),
    ]
    for kind, order in enumerate(orders):
        mine = [c for c in chunks if c[5] == kind]
        if mine:
            sizes = [halvings(order, half, c[3], c[4]) for c in mine]
            for s in range(len(order)):
                most = tuple(max(size[s][a] for size in sizes) for a in range(3))
                scratch.append(pltpu.VMEM((2 * lag,) + most, jnp.bfloat16))
    copies = len(chunks) * (half + len(orders[0]) + log2(ndp))
    return scratch + [
        pltpu.SemaphoreType.DMA((copies,)),
        pltpu.SemaphoreType.DMA((copies,)),
        pltpu.SemaphoreType.DMA((len(chunks) * half,)),
        pltpu.SemaphoreType.DMA((len(chunks),)),
    ]


class Engine:
    def __init__(self, ndp, nf, chunks, refs, source, target):
        self.nf, self.chunks, self.source, self.target = nf, chunks, source, target
        self.orders, self.half = stage_orders(ndp, nf), nf // 2
        self.dbits, self.lag = log2(ndp), lag_of(chunks)
        self.held_slots, self.core_slots = self.lag * (len(self.orders[0]) + 1), 2 * self.lag
        self.held, self.from_core, self.done = refs[:3]
        self.landing = {}
        at = 3
        for kind in range(len(self.orders)):
            if any(c[5] == kind for c in chunks):
                for s in range(len(self.orders[0])):
                    self.landing[kind, s] = refs[at]
                    at += 1
        self.send, self.recv, self.local, self.store = refs[at:]
        self.dp, self.me = lax.axis_index("dp"), lax.axis_index("fsdp")
        self.core = lax.rem(self.me, 2)
        self.sibling = (self.dp, flip(self.me, 0))
        self.partner = {("outer", b): (self.dp, flip(self.me, b)) for b in range(1, log2(nf))}
        self.partner.update({("near", b): (flip(self.dp, b), self.me) for b in range(self.dbits)})
        self.started, self.state, self.stores, self.used = [], {}, [], {}
        self.sends = {}
        counts = {}
        self.index = []
        for c in chunks:
            self.index.append(counts.get(c[5], 0) % (2 * self.lag))
            counts[c[5]] = counts.get(c[5], 0) + 1
        self.stages = 2 + len(self.orders[0]) + self.dbits
        self.steps = len(chunks) + self.lag * (self.stages - 1)
        entry_barrier([self.sibling] + list(self.partner.values()))

    def push(self, src, dst, partner, holder=None):
        k = len(self.started)
        copy = pltpu.make_async_remote_copy(
            src, dst, self.send.at[k], self.recv.at[k], device_id=partner, device_id_type=MESH
        )
        copy.start()
        self.started.append([copy, False, False])
        if holder is not None:
            self.sends.setdefault(holder, []).append(k)
        return k

    def arrive(self, k):
        self.started[k][0].wait_recv()
        self.started[k][1] = True

    def sent(self, holder):
        for k in self.sends.pop(holder, []):
            self.started[k][0].wait_send()
            self.started[k][2] = True

    def block_row(self, j, b, other):
        i, r0 = self.chunks[j][:2]
        core = 1 - self.core if other else self.core
        return (2 * b + core, r0)

    def slot(self, j):
        return j % self.held_slots

    def room(self, j):
        self.sent(("held", self.slot(j)))

    def stage(self, j, s):
        i, r0, c0, rn, cn, kind = self.chunks[j]
        order = self.orders[kind]
        held, slot = self.held, self.slot(j)
        last = len(order)
        if s == 0:
            self.room(j)
            self.state[j] = self.source(self, j)
            return
        if s == 1:
            loads, sends = self.state[j]
            for copy in loads:
                copy.wait()
            for k in sends:
                self.arrive(k)
            held[slot, :, :rn, :cn] += self.from_core[j % self.core_slots, :, :rn, :cn]
            now, history = ((0, self.half), (0, rn), (0, cn)), []
        elif s <= last + 1:
            k, now, history = self.state[j]
            self.arrive(k)
            (b0, bn), (ra, rr), (ca, cc) = now
            arrived = self.landing[kind, s - 2][self.index[j], :bn, :rr, :cc]
            total = held[slot, pl.ds(b0, bn), pl.ds(ra, rr), pl.ds(ca, cc)] + arrived
            if s == last + 1:
                self.done[j, pl.ds(ra, rr), pl.ds(ca, cc)] = total[0]
            else:
                held[slot, pl.ds(b0, bn), pl.ds(ra, rr), pl.ds(ca, cc)] = total
        if s <= last:
            name, bit = order[s - 1]
            axis = halvings(order, self.half, rn, cn)[s - 1][3]
            mine = bit_of(self.me if name == "outer" else self.dp, bit)
            start, size = now[axis]
            size //= 2
            by = (1, 16, 128)[axis]
            keep, give = list(now), list(now)
            keep[axis] = (al(start + mine * size, by), size)
            give[axis] = (al(start + (1 - mine) * size, by), size)
            src = held.at[(slot,) + tuple(pl.ds(*g) for g in give)]
            dst = self.landing[kind, s - 1].at[(self.index[j],) + tuple(pl.ds(0, g[1]) for g in give)]
            k = self.push(src, dst, self.partner[name, bit], ("held", slot))
            if name == "near":
                history = history + [(bit, now[1:])]
            self.state[j] = (k, tuple(keep), history)
            return
        if s > last + 1:
            k, _, history = self.state[j]
            self.arrive(k)
            at, history = history[-1][1], history[:-1]
        else:
            at = now[1:]
        if history:
            piece = self.done.at[(j,) + tuple(pl.ds(*a) for a in at)]
            k = self.push(piece, piece, self.partner["near", history[-1][0]])
            self.state[j] = (k, None, history)
        else:
            copy = pltpu.make_async_copy(
                self.done.at[j, pl.ds(0, rn), pl.ds(0, cn)], self.target(j), self.store.at[j]
            )
            copy.start()
            self.stores.append(copy)

    def step(self, t):
        for s in range(self.stages - 1, -1, -1):
            j = t - self.lag * s
            if 0 <= j < len(self.chunks):
                self.stage(j, s)

    def finish(self):
        for copy, seen, left in self.started:
            if not left:
                copy.wait_send()
            if not seen:
                copy.wait_recv()
        for copy in self.stores:
            copy.wait()


def nt(left, right):
    return lax.dot_general(left, right, (((1,), (1,)), ((), ())), preferred_element_type=F32)


def nn(left, right):
    return jnp.dot(left, right, preferred_element_type=F32)


def attend_math(q, k, v, probs_ref):
    dim = q.shape[1] // 2
    first = lax.broadcasted_iota(jnp.int32, q.shape, 1) < dim
    parts = []
    for h in range(2):
        one = jnp.where(first if h == 0 else ~first, q, jnp.zeros_like(q))
        scores = nt(one, k)
        powers = jnp.exp(scores - jnp.max(scores, axis=1, keepdims=True))
        probs = (powers * (1.0 / jnp.sum(powers, axis=1, keepdims=True))).astype(BF)
        probs_ref[h] = probs
        parts.append(nn(probs, v))
    return jnp.where(first, parts[0], parts[1]).astype(BF)


def attend_back_math(q, k, v, o, do, probs, scale):
    dim = q.shape[1] // 2
    first = lax.broadcasted_iota(jnp.int32, q.shape, 1) < dim
    product = do.astype(F32) * o.astype(F32)
    q_t, do_t = q.T, do.T
    dqs, dks, dvs = [], [], []
    for h in range(2):
        mine = first if h == 0 else ~first
        inner = jnp.sum(jnp.where(mine, product, 0.0), axis=1, keepdims=True)
        p = probs(h)
        d_probs = nt(jnp.where(mine, do, jnp.zeros_like(do)), v)
        d_scores = (p.astype(F32) * (d_probs - inner)).astype(BF)
        dqs.append(nn(d_scores, k))
        dks.append(nn(q_t[h * dim : (h + 1) * dim], d_scores))
        dvs.append(nn(do_t[h * dim : (h + 1) * dim], p))
    dq = jnp.where(first, dqs[0], dqs[1]).astype(BF) * BF(scale)
    return dq, jnp.concatenate(dks, axis=0).T.astype(BF), jnp.concatenate(dvs, axis=0).T.astype(BF)


TILE = 256
STAGED = 4
CUTS = 4
SKEW = 2


def tiles(count, body, unroll=True):
    lax.fori_loop(0, count, lambda n, c: (body(pl.multiple_of(n * TILE, TILE)), c)[1], 0, unroll=unroll)


class Loads:
    def __init__(self, sem, ring, items):
        self.sem, self.ring, self.items, self.next, self.copies = sem, ring, items, 0, {}

    def start(self):
        if self.next < len(self.items):
            k = self.next
            self.next += 1
            group = []
            for n, (src, dst) in enumerate(self.items[k](k % self.ring)):
                copy = pltpu.make_async_copy(src, dst, self.sem.at[k % self.ring, n])
                copy.start()
                group.append(copy)
            self.copies[k] = group

    def wait(self, k):
        for copy in self.copies.pop(k):
            copy.wait()
        return k % self.ring


def tail_kernel(ndp, nf, shapes, chunks, scale, *refs):
    w_down, w_up, w_out, w_qkv, cotangent = refs[:5]
    lefts = tuple((refs[5 + 2 * i], refs[6 + 2 * i]) for i in range(4))
    saved = [dict(zip(SAVED, refs[13 + app * len(SAVED) :])) for app in range(2)]
    refs = refs[13 + 2 * len(SAVED) :]
    inverse = ((refs[0], refs[1]), (refs[2], refs[3]))
    vec, entry_hot = refs[4], refs[5]
    outs, g0 = refs[6:11], refs[11]
    (
        r_down, r_up, r_out, r_qkv, r_qkv2, lhs, turned, staged, gh, unit_v, weight, slope_v, pair_v,
        do, probs_v, sums, w_sem, s_sem, p_sem, l_sem, u_sem, m_sem,
    ) = refs[12:34]
    joined = (r_qkv, r_qkv2)
    tokens, width = gh.shape
    part = min(1024, width)
    ff = w_down.shape[0]
    parts = ff // part
    pair = pair_v.shape[3]
    pairs = width // pair
    n_mid = 3
    turn = 2 * parts + 1 + n_mid

    first_g = pltpu.make_async_copy(cotangent, r_out.at[0], m_sem.at[0])
    first_g.start()
    columns = lambda t: pl.ds(t * part, part)
    weights = Loads(w_sem, 2, (
        [lambda s, t=t: [(w_down.at[columns(t)], weight.at[s])] for t in range(parts)]
        + [lambda s, t=t: [(w_up.at[:, columns(t)], weight.at[s])] for t in range(parts)]
        + [lambda s: [(w_out, weight.at[s])]]
        + [lambda s, t=t: [(w_qkv.at[:, columns(t)], weight.at[s])] for t in range(n_mid)]
    ) * 2)
    slopes = Loads(s_sem, 2, [
        lambda s, t=t, app=app: [(saved[app]["slope"].at[:, columns(t)], slope_v.at[s])]
        for app in (1, 0) for t in range(parts)
    ])
    heads = Loads(p_sem, 2, [
        lambda s, p=p, app=app: [
            (saved[app][name].at[:, pl.ds(p * pair, pair)], pair_v.at[s, n]) for n, name in enumerate(("q", "k", "v", "o"))
        ] + [(saved[app]["probs"].at[pl.ds(2 * p, 2)], probs_v.at[s])]
        for app in (1, 0) for p in range(pairs)
    ])
    units = Loads(u_sem, 2, [
        lambda s, name=name, app=app: [(saved[app][name], unit_v.at[s])] for app in (1, 0) for name in ("unit2", "unit1")
    ])

    def left_item(i, r0, rn):
        def item(s):
            block = shapes[i][0] // nf
            core = lax.rem(lax.axis_index("fsdp"), 2)
            out = []
            for app in range(2):
                for n in range(nf):
                    f = 2 * n + core if n < nf // 2 else 2 * (n - nf // 2) + 1 - core
                    features = pl.ds(pl.multiple_of(f * block + r0, rn), rn)
                    if rn % 128 == 0:
                        out.append((lefts[i][app].at[:, features], lhs.at[s, app, n]))
                    else:
                        out.append((lefts[i][app].at[features], lhs.at[s, app, n]))
            return out

        return item

    groups = list(dict.fromkeys((c[0], c[1], c[3]) for c in chunks if c[0] < 4))
    left = Loads(l_sem, 2, [left_item(*g) for g in groups])
    rights = (
        lambda app, at: r_down[app, :, at],
        lambda app, at: r_up[app, :, at],
        lambda app, at: r_out[app, :, at],
        lambda app, at: joined[app][:, at],
    )

    def source(engine, j):
        i, r0, c0, rn, cn, _ = chunks[j]
        slot, s = engine.slot(j), j % STAGED
        engine.sent(("staged", s))
        half = nf // 2
        if i < 4:
            if c0 == 0:
                buffer = left.wait(groups.index((i, r0, rn)))
                for app in range(2):
                    for n in range(nf):
                        block = lhs[buffer, app, n]
                        turned[pl.ds(n * rn, rn), pl.ds(app * tokens, tokens)] = block.T if rn % 128 == 0 else block
                left.start()

            def tile(at):
                right = pl.ds(c0 + at, TILE)
                total = nn(turned[:, :tokens], rights[i](0, right)) + nn(turned[:, tokens:], rights[i](1, right))
                total = total.astype(BF).reshape(nf, rn, TILE)
                engine.held[slot, :, :, pl.ds(at, TILE)] = total[:half]
                staged[s, :, :, pl.ds(at, TILE)] = total[half:]

            tiles(cn // TILE, tile, 1)
        else:
            block = sums[pl.ds(r0, rn), pl.ds(c0, cn)].astype(BF)
            for b in range(half):
                engine.held[slot, b, :rn, :cn] = block
                staged[s, b, :rn, :cn] = block
        src = staged.at[s, :, pl.ds(0, rn), pl.ds(0, cn)]
        dst = engine.from_core.at[j % engine.core_slots, :, pl.ds(0, rn), pl.ds(0, cn)]
        return [], [engine.push(src, dst, engine.sibling, ("staged", s))]

    def target(j):
        i, r0, c0, rn, cn, _ = chunks[j]
        return outs[i].at[pl.ds(r0, rn), pl.ds(c0, cn)]

    total = lambda t: jnp.sum(t.astype(F32), axis=0, keepdims=True)

    def norm_back(app, n, g_of, low, gain_row, rows_at):
        s = units.wait(2 * (1 - app) + n)

        def tile(at):
            rows = pl.ds(at, TILE)
            g, u = g_of(rows), unit_v[s, rows, :].astype(F32)
            gg = g * vec[gain_row : gain_row + 1, :]
            m1 = jnp.mean(gg, axis=1, keepdims=True)
            m2 = jnp.mean(gg * u, axis=1, keepdims=True)
            d = (gg - m1 - u * m2) * inverse[app][1 - n][rows, :]
            gh[rows, :] = d
            rounded = d.astype(BF)
            low[app, rows, :] = rounded
            for row, value in zip(rows_at, (rounded, g * u, g)):
                sums[row : row + 1, :] += total(value)

        tiles(tokens // TILE, tile)
        units.start()

    def tasks(app):
        base, unroll = turn * (1 - app), True if app else 1

        def du(t):
            s = weights.wait(base + t)
            k = slopes.wait(parts * (1 - app) + t)

            def tile(at):
                d = nt(r_down[app], weight[s, pl.ds(at, TILE), :])
                value = (d * slope_v[k, :, pl.ds(at, TILE)].astype(F32)).astype(BF)
                r_up[app, :, pl.ds(t * part + at, TILE)] = value
                sums[5 + t : 6 + t, pl.ds(at, TILE)] += total(value)

            tiles(part // TILE, tile, unroll)
            weights.start()
            slopes.start()

        def add(t, left_part, index):
            s = weights.wait(index)

            def tile(at):
                gh[:, pl.ds(at, TILE)] += nt(left_part(t), weight[s, pl.ds(at, TILE), :])

            tiles(width // TILE, tile, unroll)
            weights.start()

        def mixed():
            s = weights.wait(base + 2 * parts)

            def tile(at):
                do[:, pl.ds(at, TILE)] = nt(r_out[app], weight[s, pl.ds(at, TILE), :]).astype(BF)

            tiles(width // TILE, tile, unroll)
            weights.start()

        def one_pair(p):
            s = heads.wait(pairs * (1 - app) + p)
            at = lambda t: slice(t * width + p * pair, t * width + (p + 1) * pair)
            dq, dk, dv = attend_back_math(
                pair_v[s, 0], pair_v[s, 1], pair_v[s, 2], pair_v[s, 3], do[:, at(0)], lambda h: probs_v[s, h], scale
            )
            for t, value in enumerate((dq, dk, dv)):
                joined[app][:, at(t)] = value
            sums[0:1, at(0)] += total(dq)
            sums[1:2, at(0)] += total(dv)
            heads.start()

        early = [functools.partial(du, t) for t in range(parts)]
        early += [
            functools.partial(add, t, lambda t: r_up[app, :, t * part : (t + 1) * part], base + parts + t)
            for t in range(parts)
        ]
        middle = [lambda: norm_back(app, 1, lambda rows: gh[rows, :], r_out, 3, (2, 3, 4)), mixed]
        middle += [functools.partial(one_pair, p) for p in range(pairs)]
        late = [
            functools.partial(
                add, t, lambda t: joined[app][:, t * part : (t + 1) * part], base + 2 * parts + 1 + t
            )
            for t in range(n_mid)
        ]
        return early, middle, late

    def task_table():
        def tile(at):
            g = gh[:, pl.ds(at, TILE)]
            high = g.astype(BF)
            rest = (g - high.astype(F32)).astype(BF)
            sums[16:48, pl.ds(at, TILE)] += nn(entry_hot[...], high) + nn(entry_hot[...], rest)

        tiles(width // TILE, tile, 1)
        result.start()

    result = pltpu.make_async_copy(gh, g0, m_sem.at[1])
    for _ in range(2):
        weights.start()
        slopes.start()
        units.start()
        heads.start()
        left.start()
    engine = Engine(ndp, nf, chunks, refs[34:], source, target)
    sums[...] = jnp.zeros_like(sums)
    first_g.wait()
    last_rows = (5 + parts, 6 + parts, 7 + parts)
    norm_back(1, 0, lambda rows: r_out[0, rows, :].astype(F32), r_down, 6 + parts, last_rows)
    for group in tasks(1):
        for task in group:
            task()
    norm_back(0, 0, lambda rows: gh[rows, :], r_down, 6 + parts, last_rows)
    counts = [sum(c[0] == i for c in chunks) for i in range(5)]
    first = [sum(counts[:i]) for i in range(5)]
    early, middle, late = tasks(0)
    plan = {}

    def spread(group, begin, end):
        for n, task in enumerate(group):
            plan.setdefault(begin + n * (end - begin) // len(group), []).append(task)

    spread(early, 0, first[1])
    spread(middle, first[1], first[3] - 1)
    spread(late + [task_table], first[3], first[4])
    for t in range(engine.steps):
        engine.step(t)
        for task in plan.get(t, ()):
            task()
    engine.finish()
    result.wait()


SAVED = ("slope", "unit2", "unit1", "q", "k", "v", "o", "probs")


def tail(ndp, nf, collective_id, scale, full, cotangent, kept, vec, entry_hot):
    w_down, w_up, w_out, w_qkv = full
    tokens, width = cotangent.shape
    ff, extra = w_down.shape[0], 64
    shapes = (w_down.shape, w_up.shape, w_out.shape, w_qkv.shape, (nf * extra, width))
    chunks = chunk_list(ndp, nf, shapes, KINDS)
    half = nf // 2
    part = min(1024, width)
    pair = 2 * (width // HEADS)
    rn = chunks[0][3]
    lefts = [kept[app][name] for name in ("active", "hidden", "mixed", "low") for app in range(2)]
    if rn % 128:
        lefts = [t.T for t in lefts]
    big = list(full) + [cotangent] + lefts
    for app in range(2):
        big += [kept[app]["mixed" if name == "o" else name] for name in SAVED]
    little = [kept[app][name] for app in range(2) for name in ("inv1", "inv2")] + [vec, entry_hot]
    any_space = pl.BlockSpec(memory_space=pl.ANY)
    vmem = pl.BlockSpec(memory_space=pltpu.VMEM)
    return pl.pallas_call(
        functools.partial(tail_kernel, ndp, nf, shapes, chunks, scale),
        out_shape=[jax.ShapeDtypeStruct((r // nf, c), BF) for r, c in shapes]
        + [jax.ShapeDtypeStruct((tokens, width), F32)],
        in_specs=[any_space] * len(big) + [vmem] * len(little),
        out_specs=[any_space] * 6,
        scratch_shapes=[
            pltpu.VMEM((2, tokens, width), BF),
            pltpu.VMEM((2, tokens, ff), BF),
            pltpu.VMEM((2, tokens, width), BF),
            pltpu.VMEM((tokens, 3 * width), BF),
            pltpu.VMEM((tokens, 3 * width), BF),
            pltpu.VMEM((2, 2, nf, tokens, rn) if rn % 128 == 0 else (2, 2, nf, rn, tokens), BF),
            pltpu.VMEM((nf * rn, 2 * tokens), BF),
            pltpu.VMEM((STAGED, half, rn, chunks[0][4]), BF),
            pltpu.VMEM((tokens, width), F32),
            pltpu.VMEM((2, tokens, width), BF),
            pltpu.VMEM((2, part, width), BF),
            pltpu.VMEM((2, tokens, part), BF),
            pltpu.VMEM((2, 4, tokens, pair), BF),
            pltpu.VMEM((tokens, width), BF),
            pltpu.VMEM((2, 2, tokens, tokens), BF),
            pltpu.VMEM((extra, width), F32),
            pltpu.SemaphoreType.DMA((2, 1)),
            pltpu.SemaphoreType.DMA((2, 1)),
            pltpu.SemaphoreType.DMA((2, 5)),
            pltpu.SemaphoreType.DMA((2, 2 * nf)),
            pltpu.SemaphoreType.DMA((2, 1)),
            pltpu.SemaphoreType.DMA((2,)),
        ]
        + engine_scratch(ndp, nf, chunks),
        compiler_params=pltpu.CompilerParams(
            collective_id=collective_id, has_side_effects=True, vmem_limit_bytes=63 * 1024 * 1024
        ),
        name="tail",
    )(*big, *little)


def widen_kernel(*refs):
    keep, g0 = refs[:2]
    ins, token_grad, outs = refs[2:6], refs[6], refs[7:]
    token_grad[...] = g0[...] * keep[...]
    for source, target in zip(ins, outs):
        target[...] = source[...].astype(F32)


def widen(keep, g0, grads):
    arrays = [keep, g0, *grads]
    blocks = [pl.BlockSpec((t.shape[0] // 4, t.shape[1]), lambda n: (n, 0)) for t in arrays]
    return pl.pallas_call(
        widen_kernel,
        grid=(4,),
        in_specs=blocks,
        out_specs=blocks[1:],
        out_shape=[jax.ShapeDtypeStruct(t.shape, F32) for t in arrays[1:]],
        compiler_params=pltpu.CompilerParams(vmem_limit_bytes=60 * 1024 * 1024),
        name="widen",
    )(*arrays)


LAYER = ("low", "q", "k", "v", "mixed", "probs", "unit1", "inv1", "hidden", "active", "slope", "unit2", "inv2")


def head_kernel(ndp, nf, shapes, scale, *refs):
    n = len(shapes)
    ins, small, tokens_ref, keep, row_hot, table = refs[:n], refs[n], refs[n + 1], refs[n + 2], refs[n + 3], refs[n + 4]
    refs = refs[n + 5 :]
    full_out, vec_out, final_out = refs[:n], refs[n], refs[n + 1]
    kept = [dict(zip(LAYER, refs[n + 2 + k * len(LAYER) :])) for k in range(2)]
    refs = refs[n + 2 + 2 * len(LAYER) :]
    full, refs = refs[:n], refs[n:]
    (
        small_all, vec, entries, x, low, joined, mixed, hidden, active, slope, probs, unit, inv,
        send, recv, local, save_sem,
    ) = refs
    outs = full
    dp, me = lax.axis_index("dp"), lax.axis_index("fsdp")
    fbits = log2(nf)
    sibling = (dp, flip(me, 0))
    outer = [(dp, flip(me, b)) for b in range(1, fbits)]
    near = [(flip(dp, 0), me), (flip(dp, 1), me)]
    others = [(dp, lax.rem(me + d, nf)) for d in range(1, nf)]
    code = lax.rem(dp, 4)
    started, arrived, final_of = [], [], {i: [] for i in range(n)}
    own = []
    for i in range(n):
        r, c = shapes[i]
        copy = pltpu.make_async_copy(ins[i], full[i].at[pl.ds(pl.multiple_of(me * r, r), r)], local.at[i])
        copy.start()
        own.append(copy)
    own_small = pltpu.make_async_copy(small, small_all.at[me], local.at[n])
    own_small.start()
    entry_barrier(others + near)

    def push(src, dst, partner):
        k = len(started)
        copy = pltpu.make_async_remote_copy(src, dst, send.at[k], recv.at[k], device_id=partner, device_id_type=MESH)
        copy.start()
        started.append(copy)
        arrived.append(False)
        return k

    def arrive(k):
        if not arrived[k]:
            started[k].wait_recv()
            arrived[k] = True

    small_copies = [push(small, small_all.at[me], other) for other in others]

    def place(i, f, k, half):
        r, c = shapes[i]
        q, w = r // 4, c // CUTS
        return full[i].at[pl.ds(pl.multiple_of(f * r + k * q, 16), q), pl.ds(half * w, w)]

    items = [(i, h) for i in range(n) for h in range(CUTS)]
    waits, known = {}, {}

    def share(i, where):
        final_of[i].append(push(where, where, sibling))

    def stage(t, s):
        i, half = items[t]
        r, c = shapes[i]
        q, w = r // 4, c // CUTS
        p1, p2 = (0, 1) if half % 2 == 0 else (1, 0)
        src = ins[i].at[pl.ds(pl.multiple_of(code * q, 16), q), pl.ds(half * w, w)]
        at = lambda f, k: place(i, f, k, half)
        if s == 0:
            if fbits > 1:
                waits[t, "y", 1] = [(me, push(src, at(me, code), outer[0]))]
            whole = full[i].at[pl.ds(pl.multiple_of(me * r, r), r), pl.ds(half * w, w)]
            final_of[i].append(push(ins[i].at[:, pl.ds(half * w, w)], whole, sibling))
        elif s < fbits:
            got = []
            for f, copy in waits.pop((t, "y", s)):
                arrive(copy)
                got.append(flip(f, s))
            known.setdefault(t, []).extend(got)
            if s < fbits - 1:
                waits[t, "y", s + 1] = [(me, push(src, at(me, code), outer[s]))] + [
                    (f, push(at(f, code), at(f, code), outer[s])) for f in known[t]
                ]
            else:
                waits[t, "p1"] = [(f, push(at(f, code), at(f, code), near[p1])) for f in known[t]]
                waits[t, "p2a"] = [(f, push(at(f, code), at(f, code), near[p2])) for f in known[t]]
            for f in got:
                share(i, at(f, code))
        elif s == fbits:
            k = flip(code, p1)
            waits[t, "p2b"] = []
            for f, copy in waits.pop((t, "p1")):
                arrive(copy)
                waits[t, "p2b"].append((f, push(at(f, k), at(f, k), near[p2])))
                share(i, at(f, k))
        else:
            k = flip(code, p2) if s == fbits + 1 else flip(flip(code, p2), p1)
            for f, copy in waits.pop((t, "p2a" if s == fbits + 1 else "p2b")):
                arrive(copy)
                share(i, at(f, k))

    saves, pending = [], {}

    def save(name, src, dst):
        copy = pltpu.make_async_copy(src, dst, save_sem.at[len(saves)])
        copy.start()
        saves.append(copy)
        pending.setdefault(name, []).append(copy)

    def free(name):
        for copy in pending.pop(name, []):
            copy.wait()

    ready = set()

    def need(i):
        if i not in ready:
            ready.add(i)
            own[i].wait()
            for k in final_of[i]:
                arrive(k)
            save("full", full[i], full_out[i])

    tokens, width = x.shape
    part = min(1024, width)
    parts = shapes[2][1] // part
    pairs = HEADS // 2
    pair = width // pairs
    mine = width // nf

    def task_start():
        own_small.wait()
        for k in small_copies:
            arrive(k)
        row = 0
        for count in (2, 1, 1, 1, parts, 1, 1, 1):
            for f in range(nf):
                for i in range(count):
                    at = (f * count + i) * mine
                    vec[row + at // width : row + at // width + 1, at % width : at % width + mine] = small_all[
                        f, row + i : row + i + 1, :
                    ].astype(F32)
            row += count
        save("vec", vec, vec_out)
        entries[...] = jnp.zeros_like(entries)
        entries[: table.shape[0], :] = table[...]

        def tile(at):
            rows = pl.ds(at, TILE)
            x0 = tokens_ref[rows, :].astype(F32) * keep[rows, :] + nn(row_hot[rows, :], entries[...])
            x[rows, :] = x0
            low[rows, :] = x0.astype(BF)

        tiles(tokens // TILE, tile)
        save("low", low, kept[0]["low"])

    def task_joined(app, t):
        def run():
            need(0)
            free("qkv"[t])

            def tile(at):
                cols = pl.ds(t * width + at, TILE)
                value = nn(low[...], full[0][:, cols])
                if t == 0:
                    value = (value + vec[0:1, pl.ds(at, TILE)]) * scale
                if t == 2:
                    value = value + vec[1:2, pl.ds(at, TILE)]
                joined[:, cols] = value.astype(BF)

            tiles(width // TILE, tile)
            save("qkv"[t], joined.at[:, pl.ds(t * width, width)], kept[app]["qkv"[t]])
        return run

    def task_heads(app, p):
        def run():
            if p == 0:
                free("mixed")
            free(("probs", p % 2))
            at = lambda t: slice(t * width + p * pair, t * width + (p + 1) * pair)
            mixed[:, at(0)] = attend_math(joined[:, at(0)], joined[:, at(1)], joined[:, at(2)], probs.at[p % 2])
            save(("probs", p % 2), probs.at[p % 2], kept[app]["probs"].at[pl.ds(2 * p, 2)])
            if p == pairs - 1:
                save("mixed", mixed, kept[app]["mixed"])
        return run

    def norm(t, gain, shift):
        mean = jnp.mean(t, axis=1, keepdims=True)
        centred = t - mean
        spread = jnp.mean(centred * centred, axis=1, keepdims=True)
        inverse = lax.rsqrt(spread + EPSILON)
        normal = centred * inverse
        return normal * vec[gain : gain + 1, :] + vec[shift : shift + 1, :], normal.astype(BF), inverse

    def task_out(app):
        def run():
            need(1)
            free("hidden")
            free("unit1")
            free("inv1")

            def tile(at):
                rows = pl.ds(at, TILE)
                t = x[rows, :] + nn(mixed[rows, :], full[1][...]) + vec[2:3, :]
                h, unit[0, rows, :], inv[0, rows, :] = norm(t, 3, 4)
                x[rows, :] = h
                hidden[rows, :] = h.astype(BF)

            tiles(tokens // TILE, tile)
            save("unit1", unit.at[0], kept[app]["unit1"])
            save("inv1", inv.at[0], kept[app]["inv1"])
            save("hidden", hidden, kept[app]["hidden"])
        return run

    def task_up(app, t):
        def run():
            need(2)
            free(("active", t))
            free(("slope", t % 2))

            def tile(at):
                cols = pl.ds(t * part + at, TILE)
                u = nn(hidden[...], full[2][:, cols]) + vec[5 + t : 6 + t, pl.ds(at, TILE)]
                below = 0.5 + 0.5 * lax.erf(u * math.sqrt(0.5))
                active[:, cols] = (u * below).astype(BF)
                bell = math.sqrt(0.5 / math.pi) * jnp.exp(-0.5 * u * u)
                slope[t % 2, :, pl.ds(at, TILE)] = (below + u * bell).astype(BF)

            tiles(part // TILE, tile)
            cols = pl.ds(t * part, part)
            save(("active", t), active.at[:, cols], kept[app]["active"].at[:, cols])
            save(("slope", t % 2), slope.at[t % 2], kept[app]["slope"].at[:, cols])
        return run

    def task_down(app):
        def run():
            need(3)
            free("low")
            free("unit2")
            free("inv2")

            def tile(at):
                rows = pl.ds(at, TILE)
                t = x[rows, :] + nn(active[rows, :], full[3][...]) + vec[5 + parts : 6 + parts, :]
                y, unit[1, rows, :], inv[1, rows, :] = norm(t, 6 + parts, 7 + parts)
                x[rows, :] = y
                low[rows, :] = y.astype(BF)

            tiles(tokens // TILE, tile)
            save("unit2", unit.at[1], kept[app]["unit2"])
            save("inv2", inv.at[1], kept[app]["inv2"])
            save("low", low, final_out if app else kept[1]["low"])
        return run

    first = lambda app: [task_joined(app, t) for t in range(3)] + [task_heads(app, p) for p in range(pairs)] + [task_out(app)]
    second = lambda app: [task_up(app, t) for t in range(parts)]
    stages = fbits + 3
    ahead = 2
    steps = len(items) + SKEW * (stages - 1)
    done_at = lambda i: CUTS * (i + 1) - 1 + SKEW * (stages - 1)
    plan = {}

    def spread(tasks, begin, end):
        for k, task in enumerate(tasks):
            plan.setdefault(min(begin + k * (end - begin) // len(tasks), steps), []).append(task)

    spread([task_start], 0, 1)
    spread(first(0), done_at(0) + 1, done_at(2) + 1)
    spread(second(0), done_at(2) + 1, steps)
    spread([task_down(0)] + first(1) + second(1) + [task_down(1)], steps, steps)
    for step in range(-ahead, steps):
        for s in range(stages - 1, -1, -1):
            t = step - SKEW * s if s else step + ahead
            if 0 <= t < len(items):
                stage(t, s)
        for task in plan.get(step, ()):
            task()
    for task in plan[steps]:
        task()
    for copy in started:
        copy.wait_send()
    for k in range(len(started)):
        arrive(k)
    for name in list(pending):
        free(name)


def head(ndp, nf, collective_id, scale, shards, small, tokens, keep, row_hot, table):
    shapes = tuple(s.shape for s in shards)
    length, width = tokens.shape
    ff = shapes[2][1]
    part = min(1024, width)
    kinds = dict(
        low=((length, width), BF), q=((length, width), BF), k=((length, width), BF), v=((length, width), BF),
        mixed=((length, width), BF), probs=((HEADS, length, length), BF), unit1=((length, width), BF),
        inv1=((length, 1), F32), hidden=((length, width), BF), active=((length, ff), BF), slope=((length, ff), BF),
        unit2=((length, width), BF), inv2=((length, 1), F32),
    )
    full = [(nf * r, c) for r, c in shapes]
    out_shape = [jax.ShapeDtypeStruct(s, BF) for s in full]
    out_shape += [jax.ShapeDtypeStruct((small.shape[0], width), F32), jax.ShapeDtypeStruct((length, width), BF)]
    out_shape += [jax.ShapeDtypeStruct(*kinds[name]) for _ in range(2) for name in LAYER]
    per_item = (nf // 2 - 1) * 8 + 1
    copies = nf - 1 + CUTS * len(shards) * per_item
    any_space = pl.BlockSpec(memory_space=pl.ANY)
    vmem = pl.BlockSpec(memory_space=pltpu.VMEM)
    outs = pl.pallas_call(
        functools.partial(head_kernel, ndp, nf, shapes, scale),
        out_shape=out_shape,
        in_specs=[any_space] * (len(shards) + 1) + [vmem] * 4,
        out_specs=[any_space] * len(out_shape),
        scratch_shapes=[pltpu.VMEM(s, BF) for s in full]
        + [
            pltpu.VMEM((nf,) + small.shape, BF),
            pltpu.VMEM((small.shape[0], width), F32),
            pltpu.VMEM((32, width), BF),
            pltpu.VMEM((length, width), F32),
            pltpu.VMEM((length, width), BF),
            pltpu.VMEM((length, 3 * width), BF),
            pltpu.VMEM((length, width), BF),
            pltpu.VMEM((length, width), BF),
            pltpu.VMEM((length, ff), BF),
            pltpu.VMEM((2, length, part), BF),
            pltpu.VMEM((2, 2, length, length), BF),
            pltpu.VMEM((2, length, width), BF),
            pltpu.VMEM((2, length, 1), F32),
            pltpu.SemaphoreType.DMA((copies,)),
            pltpu.SemaphoreType.DMA((copies,)),
            pltpu.SemaphoreType.DMA((len(shards) + 1,)),
            pltpu.SemaphoreType.DMA((96,)),
        ],
        compiler_params=pltpu.CompilerParams(
            collective_id=collective_id, has_side_effects=True, vmem_limit_bytes=61 * 1024 * 1024
        ),
        name="head",
    )(*shards, small, tokens, keep, row_hot, table)
    n = len(shards)
    kept = [dict(zip(LAYER, outs[n + 2 + k * len(LAYER) :])) for k in range(2)]
    return outs[:n], outs[n], outs[n + 1], kept


def shards(ndp, nf, tokens, mask_positions, mask_counts, replace_ids, cotangent, replace_table,
           w_qkv, b_qv, w_out, b_out, norm1_gain, norm1_bias, w_up, b_up, w_down, b_down, norm2_gain, norm2_bias):
    length, width = tokens.shape
    slots = mask_positions.shape[1]
    used = (jnp.arange(slots, dtype=jnp.int32) < mask_counts[0]).astype(F32)
    places = jnp.arange(length, dtype=jnp.int32)
    position_hot = (mask_positions[0][:, None] == places[None, :]).astype(F32) * used[:, None]
    entries = jnp.arange(32, dtype=jnp.int32)
    vocab_hot = (replace_ids[0][:, None] == entries[None, :]).astype(BF)
    row_hot = nn(position_hot.astype(BF).T, vocab_hot).astype(BF)
    keep = 1.0 - jnp.sum(position_hot, axis=0)[:, None]
    entries = replace_table.shape[0]
    mine = width // nf
    small = jnp.zeros((16 * mine,), BF)
    at = 0
    for vector in (b_qv, b_out, norm1_gain, norm1_bias, b_up, b_down, norm2_gain, norm2_bias):
        small = small + jnp.pad(vector, (at, 16 * mine - at - vector.shape[0]))
        at += vector.shape[0]
    small = small.reshape(16, mine)
    scale = 1.0 / math.sqrt(width // HEADS)
    (qkv, out, up, down), vec, final, (kept_one, kept_two) = head(
        ndp, nf, 0, scale, [w_qkv, w_out, w_up, w_down], small, tokens, keep,
        row_hot, replace_table,
    )
    grown = w_up.shape[1] // width
    g_down, g_up, g_out, g_qkv, extra, d_start = tail(
        ndp, nf, 1, scale, (down, up, out, qkv), cotangent, (kept_one, kept_two), vec, row_hot.T
    )
    token_grad, g_down, g_up, g_out, g_qkv = widen(keep, d_start, (g_down, g_up, g_out, g_qkv))
    extra = extra.astype(F32)
    table_grad = extra[16 : 16 + entries]
    place = lax.axis_index("fsdp")
    mine = lambda t: lax.dynamic_slice_in_dim(t, place * (t.shape[0] // nf), t.shape[0] // nf)
    v = [mine(extra[:2].reshape(-1))] + [mine(extra[n]) for n in (2, 3, 4)]
    v += [mine(extra[5 : 5 + grown].reshape(-1))] + [mine(extra[n + grown]) for n in (5, 6, 7)]
    return (
        final, token_grad, table_grad, g_qkv, v[0], g_out, v[1], v[2], v[3],
        g_up, v[4], g_down, v[5], v[6], v[7],
    )


def solution(mesh):
    both = P(("dp", "fsdp"))
    rows = P("fsdp")
    in_specs = (both,) * 5 + (P(),) + (rows,) * 12
    out_specs = (both, both, P()) + (rows,) * 12
    body = functools.partial(shards, mesh.shape["dp"], mesh.shape["fsdp"])
    return jax.shard_map(body, mesh=mesh, in_specs=in_specs, out_specs=out_specs, check_vma=False)
```

```python
import functools
import math

import jax
import jax.numpy as jnp
from jax import lax
from jax.experimental import pallas as pl
from jax.experimental.pallas import tpu as pltpu
from jax.sharding import PartitionSpec as P

HEADS = 16
EPSILON = 1e-05
BF = jnp.bfloat16
F32 = jnp.float32
MESH = pl.DeviceIdType.MESH


def log2(n):
    return n.bit_length() - 1

def entry_barrier(partners):
    barrier = pltpu.get_barrier_semaphore()
    for partner in partners:
        pl.semaphore_signal(barrier, inc=1, device_id=partner, device_id_type=MESH)
    pl.semaphore_wait(barrier, len(partners))

def bit_of(value, bit):
    return lax.rem(value // (1 << bit), 2)

def flip(value, bit):
    return value + (1 - 2 * bit_of(value, bit)) * (1 << bit)

CHUNK_ROWS = 512
CHUNK_COLUMNS = 512
KINDS = (0, 2, 1)


def al(value, by):
    return value if isinstance(value, int) else pl.multiple_of(value, by)


def stage_orders(ndp, nf):
    outer = [("outer", b) for b in range(log2(nf) - 1, 0, -1)]
    near = [("near", b) for b in range(log2(ndp))]
    return (
        outer + near,
        near[:1] + outer + near[1:],
        outer + near[1:2] + near[:1] + near[2:],
    )


def chunk_list(ndp, nf, shapes, kinds):
    chunks = []
    for i, (r, c) in enumerate(shapes):
        rn = min(CHUNK_ROWS // nf, r // nf)
        cn = min(max(CHUNK_COLUMNS, (128 * 16 * ndp) // rn), c)
        for r0 in range(0, r // nf, rn):
            for c0 in range(0, c, cn):
                chunks.append((i, r0, c0, rn, cn, kinds[len(chunks) % len(kinds)]))
    return tuple(chunks)


def lag_of(chunks):
    return 3 if chunks[0][4] <= 512 else 2


def halvings(order, half, rn, cn):
    left, blocks = [], half
    for kind, _ in order:
        if kind == "outer":
            blocks //= 2
            axis = 0
        elif rn >= 32:
            rn //= 2
            axis = 1
        else:
            cn //= 2
            axis = 2
        left.append((blocks, rn, cn, axis))
    return left


def engine_scratch(ndp, nf, chunks):
    orders, half = stage_orders(ndp, nf), nf // 2
    rn, cn = max(c[3] for c in chunks), max(c[4] for c in chunks)
    lag = lag_of(chunks)
    scratch = [
        pltpu.VMEM((lag * (len(orders[0]) + 1), half, rn, cn), jnp.bfloat16),
        pltpu.VMEM((2 * lag, half, rn, cn), jnp.bfloat16),
        pltpu.VMEM((len(chunks), rn, cn), jnp.bfloat16),
    ]
    for kind, order in enumerate(orders):
        mine = [c for c in chunks if c[5] == kind]
        if mine:
            sizes = [halvings(order, half, c[3], c[4]) for c in mine]
            for s in range(len(order)):
                most = tuple(max(size[s][a] for size in sizes) for a in range(3))
                scratch.append(pltpu.VMEM((2 * lag,) + most, jnp.bfloat16))
    copies = len(chunks) * (half + len(orders[0]) + log2(ndp))
    return scratch + [
        pltpu.SemaphoreType.DMA((copies,)),
        pltpu.SemaphoreType.DMA((copies,)),
        pltpu.SemaphoreType.DMA((len(chunks) * half,)),
        pltpu.SemaphoreType.DMA((len(chunks),)),
    ]


class Engine:
    def __init__(self, ndp, nf, chunks, refs, source, target):
        self.nf, self.chunks, self.source, self.target = nf, chunks, source, target
        self.orders, self.half = stage_orders(ndp, nf), nf // 2
        self.dbits, self.lag = log2(ndp), lag_of(chunks)
        self.held_slots, self.core_slots = self.lag * (len(self.orders[0]) + 1), 2 * self.lag
        self.held, self.from_core, self.done = refs[:3]
        self.landing = {}
        at = 3
        for kind in range(len(self.orders)):
            if any(c[5] == kind for c in chunks):
                for s in range(len(self.orders[0])):
                    self.landing[kind, s] = refs[at]
                    at += 1
        self.send, self.recv, self.local, self.store = refs[at:]
        self.dp, self.me = lax.axis_index("dp"), lax.axis_index("fsdp")
        self.core = lax.rem(self.me, 2)
        self.sibling = (self.dp, flip(self.me, 0))
        self.partner = {("outer", b): (self.dp, flip(self.me, b)) for b in range(1, log2(nf))}
        self.partner.update({("near", b): (flip(self.dp, b), self.me) for b in range(self.dbits)})
        self.started, self.state, self.stores, self.used = [], {}, [], {}
        self.sends = {}
        counts = {}
        self.index = []
        for c in chunks:
            self.index.append(counts.get(c[5], 0) % (2 * self.lag))
            counts[c[5]] = counts.get(c[5], 0) + 1
        self.stages = 2 + len(self.orders[0]) + self.dbits
        self.steps = len(chunks) + self.lag * (self.stages - 1)
        entry_barrier([self.sibling] + list(self.partner.values()))

    def push(self, src, dst, partner, holder=None):
        k = len(self.started)
        copy = pltpu.make_async_remote_copy(
            src, dst, self.send.at[k], self.recv.at[k], device_id=partner, device_id_type=MESH
        )
        copy.start()
        self.started.append([copy, False, False])
        if holder is not None:
            self.sends.setdefault(holder, []).append(k)
        return k

    def arrive(self, k):
        self.started[k][0].wait_recv()
        self.started[k][1] = True

    def sent(self, holder):
        for k in self.sends.pop(holder, []):
            self.started[k][0].wait_send()
            self.started[k][2] = True

    def block_row(self, j, b, other):
        i, r0 = self.chunks[j][:2]
        core = 1 - self.core if other else self.core
        return (2 * b + core, r0)

    def slot(self, j):
        return j % self.held_slots

    def room(self, j):
        self.sent(("held", self.slot(j)))

    def stage(self, j, s):
        i, r0, c0, rn, cn, kind = self.chunks[j]
        order = self.orders[kind]
        held, slot = self.held, self.slot(j)
        last = len(order)
        if s == 0:
            self.room(j)
            self.state[j] = self.source(self, j)
            return
        if s == 1:
            loads, sends = self.state[j]
            for copy in loads:
                copy.wait()
            for k in sends:
                self.arrive(k)
            held[slot, :, :rn, :cn] += self.from_core[j % self.core_slots, :, :rn, :cn]
            now, history = ((0, self.half), (0, rn), (0, cn)), []
        elif s <= last + 1:
            k, now, history = self.state[j]
            self.arrive(k)
            (b0, bn), (ra, rr), (ca, cc) = now
            arrived = self.landing[kind, s - 2][self.index[j], :bn, :rr, :cc]
            total = held[slot, pl.ds(b0, bn), pl.ds(ra, rr), pl.ds(ca, cc)] + arrived
            if s == last + 1:
                self.done[j, pl.ds(ra, rr), pl.ds(ca, cc)] = total[0]
            else:
                held[slot, pl.ds(b0, bn), pl.ds(ra, rr), pl.ds(ca, cc)] = total
        if s <= last:
            name, bit = order[s - 1]
            axis = halvings(order, self.half, rn, cn)[s - 1][3]
            mine = bit_of(self.me if name == "outer" else self.dp, bit)
            start, size = now[axis]
            size //= 2
            by = (1, 16, 128)[axis]
            keep, give = list(now), list(now)
            keep[axis] = (al(start + mine * size, by), size)
            give[axis] = (al(start + (1 - mine) * size, by), size)
            src = held.at[(slot,) + tuple(pl.ds(*g) for g in give)]
            dst = self.landing[kind, s - 1].at[(self.index[j],) + tuple(pl.ds(0, g[1]) for g in give)]
            k = self.push(src, dst, self.partner[name, bit], ("held", slot))
            if name == "near":
                history = history + [(bit, now[1:])]
            self.state[j] = (k, tuple(keep), history)
            return
        if s > last + 1:
            k, _, history = self.state[j]
            self.arrive(k)
            at, history = history[-1][1], history[:-1]
        else:
            at = now[1:]
        if history:
            piece = self.done.at[(j,) + tuple(pl.ds(*a) for a in at)]
            k = self.push(piece, piece, self.partner["near", history[-1][0]])
            self.state[j] = (k, None, history)
        else:
            copy = pltpu.make_async_copy(
                self.done.at[j, pl.ds(0, rn), pl.ds(0, cn)], self.target(j), self.store.at[j]
            )
            copy.start()
            self.stores.append(copy)

    def step(self, t):
        for s in range(self.stages - 1, -1, -1):
            j = t - self.lag * s
            if 0 <= j < len(self.chunks):
                self.stage(j, s)

    def finish(self):
        for copy, seen, left in self.started:
            if not left:
                copy.wait_send()
            if not seen:
                copy.wait_recv()
        for copy in self.stores:
            copy.wait()


def nt(left, right):
    return lax.dot_general(left, right, (((1,), (1,)), ((), ())), preferred_element_type=F32)


def nn(left, right):
    return jnp.dot(left, right, preferred_element_type=F32)


def attend_math(q, k, v, probs_ref):
    dim = q.shape[1] // 2
    first = lax.broadcasted_iota(jnp.int32, q.shape, 1) < dim
    parts = []
    for h in range(2):
        one = jnp.where(first if h == 0 else ~first, q, jnp.zeros_like(q))
        scores = nt(one, k)
        powers = jnp.exp(scores - jnp.max(scores, axis=1, keepdims=True))
        probs = (powers * (1.0 / jnp.sum(powers, axis=1, keepdims=True))).astype(BF)
        probs_ref[h] = probs
        parts.append(nn(probs, v))
    return jnp.where(first, parts[0], parts[1]).astype(BF)


def attend_back_math(q, k, v, o, do, probs, scale):
    dim = q.shape[1] // 2
    first = lax.broadcasted_iota(jnp.int32, q.shape, 1) < dim
    product = do.astype(F32) * o.astype(F32)
    q_t, do_t = q.T, do.T
    dqs, dks, dvs = [], [], []
    for h in range(2):
        mine = first if h == 0 else ~first
        inner = jnp.sum(jnp.where(mine, product, 0.0), axis=1, keepdims=True)
        p = probs(h)
        d_probs = nt(jnp.where(mine, do, jnp.zeros_like(do)), v)
        d_scores = (p.astype(F32) * (d_probs - inner)).astype(BF)
        dqs.append(nn(d_scores, k))
        dks.append(nn(q_t[h * dim : (h + 1) * dim], d_scores))
        dvs.append(nn(do_t[h * dim : (h + 1) * dim], p))
    dq = jnp.where(first, dqs[0], dqs[1]).astype(BF) * BF(scale)
    return dq, jnp.concatenate(dks, axis=0).T.astype(BF), jnp.concatenate(dvs, axis=0).T.astype(BF)


TILE = 256
STAGED = 4
CUTS = 4
SKEW = 2


def tiles(count, body, unroll=True):
    lax.fori_loop(0, count, lambda n, c: (body(pl.multiple_of(n * TILE, TILE)), c)[1], 0, unroll=unroll)


class Loads:
    def __init__(self, sem, ring, items):
        self.sem, self.ring, self.items, self.next, self.copies = sem, ring, items, 0, {}

    def start(self):
        if self.next < len(self.items):
            k = self.next
            self.next += 1
            group = []
            for n, (src, dst) in enumerate(self.items[k](k % self.ring)):
                copy = pltpu.make_async_copy(src, dst, self.sem.at[k % self.ring, n])
                copy.start()
                group.append(copy)
            self.copies[k] = group

    def wait(self, k):
        for copy in self.copies.pop(k):
            copy.wait()
        return k % self.ring


def tail_kernel(ndp, nf, shapes, chunks, scale, *refs):
    w_down, w_up, w_out, w_qkv, cotangent = refs[:5]
    lefts = tuple((refs[5 + 2 * i], refs[6 + 2 * i]) for i in range(4))
    saved = [dict(zip(SAVED, refs[13 + app * len(SAVED) :])) for app in range(2)]
    refs = refs[13 + 2 * len(SAVED) :]
    inverse = ((refs[0], refs[1]), (refs[2], refs[3]))
    vec, entry_hot = refs[4], refs[5]
    outs, g0 = refs[6:11], refs[11]
    (
        r_down, r_up, r_out, r_qkv, r_qkv2, lhs, turned, staged, gh, unit_v, weight, slope_v, pair_v,
        do, probs_v, sums, w_sem, s_sem, p_sem, l_sem, u_sem, m_sem,
    ) = refs[12:34]
    joined = (r_qkv, r_qkv2)
    tokens, width = gh.shape
    part = min(1024, width)
    ff = w_down.shape[0]
    parts = ff // part
    pair = pair_v.shape[3]
    pairs = width // pair
    n_mid = 3
    turn = 2 * parts + 1 + n_mid

    first_g = pltpu.make_async_copy(cotangent, r_out.at[0], m_sem.at[0])
    first_g.start()
    columns = lambda t: pl.ds(t * part, part)
    weights = Loads(w_sem, 2, (
        [lambda s, t=t: [(w_down.at[columns(t)], weight.at[s])] for t in range(parts)]
        + [lambda s, t=t: [(w_up.at[:, columns(t)], weight.at[s])] for t in range(parts)]
        + [lambda s: [(w_out, weight.at[s])]]
        + [lambda s, t=t: [(w_qkv.at[:, columns(t)], weight.at[s])] for t in range(n_mid)]
    ) * 2)
    slopes = Loads(s_sem, 2, [
        lambda s, t=t, app=app: [(saved[app]["slope"].at[:, columns(t)], slope_v.at[s])]
        for app in (1, 0) for t in range(parts)
    ])
    heads = Loads(p_sem, 2, [
        lambda s, p=p, app=app: [
            (saved[app][name].at[:, pl.ds(p * pair, pair)], pair_v.at[s, n]) for n, name in enumerate(("q", "k", "v", "o"))
        ] + [(saved[app]["probs"].at[pl.ds(2 * p, 2)], probs_v.at[s])]
        for app in (1, 0) for p in range(pairs)
    ])
    units = Loads(u_sem, 2, [
        lambda s, name=name, app=app: [(saved[app][name], unit_v.at[s])] for app in (1, 0) for name in ("unit2", "unit1")
    ])

    def left_item(i, r0, rn):
        def item(s):
            block = shapes[i][0] // nf
            core = lax.rem(lax.axis_index("fsdp"), 2)
            out = []
            for app in range(2):
                for n in range(nf):
                    f = 2 * n + core if n < nf // 2 else 2 * (n - nf // 2) + 1 - core
                    features = pl.ds(pl.multiple_of(f * block + r0, rn), rn)
                    if rn % 128 == 0:
                        out.append((lefts[i][app].at[:, features], lhs.at[s, app, n]))
                    else:
                        out.append((lefts[i][app].at[features], lhs.at[s, app, n]))
            return out

        return item

    groups = list(dict.fromkeys((c[0], c[1], c[3]) for c in chunks if c[0] < 4))
    left = Loads(l_sem, 2, [left_item(*g) for g in groups])
    rights = (
        lambda app, at: r_down[app, :, at],
        lambda app, at: r_up[app, :, at],
        lambda app, at: r_out[app, :, at],
        lambda app, at: joined[app][:, at],
    )

    def source(engine, j):
        i, r0, c0, rn, cn, _ = chunks[j]
        slot, s = engine.slot(j), j % STAGED
        engine.sent(("staged", s))
        half = nf // 2
        if i < 4:
            if c0 == 0:
                buffer = left.wait(groups.index((i, r0, rn)))
                for app in range(2):
                    for n in range(nf):
                        block = lhs[buffer, app, n]
                        turned[pl.ds(n * rn, rn), pl.ds(app * tokens, tokens)] = block.T if rn % 128 == 0 else block
                left.start()

            def tile(at):
                right = pl.ds(c0 + at, TILE)
                total = nn(turned[:, :tokens], rights[i](0, right)) + nn(turned[:, tokens:], rights[i](1, right))
                total = total.astype(BF).reshape(nf, rn, TILE)
                engine.held[slot, :, :, pl.ds(at, TILE)] = total[:half]
                staged[s, :, :, pl.ds(at, TILE)] = total[half:]

            tiles(cn // TILE, tile, 1)
        else:
            block = sums[pl.ds(r0, rn), pl.ds(c0, cn)].astype(BF)
            for b in range(half):
                engine.held[slot, b, :rn, :cn] = block
                staged[s, b, :rn, :cn] = block
        src = staged.at[s, :, pl.ds(0, rn), pl.ds(0, cn)]
        dst = engine.from_core.at[j % engine.core_slots, :, pl.ds(0, rn), pl.ds(0, cn)]
        return [], [engine.push(src, dst, engine.sibling, ("staged", s))]

    def target(j):
        i, r0, c0, rn, cn, _ = chunks[j]
        return outs[i].at[pl.ds(r0, rn), pl.ds(c0, cn)]

    total = lambda t: jnp.sum(t.astype(F32), axis=0, keepdims=True)

    def norm_back(app, n, g_of, low, gain_row, rows_at):
        s = units.wait(2 * (1 - app) + n)

        def tile(at):
            rows = pl.ds(at, TILE)
            g, u = g_of(rows), unit_v[s, rows, :].astype(F32)
            gg = g * vec[gain_row : gain_row + 1, :]
            m1 = jnp.mean(gg, axis=1, keepdims=True)
            m2 = jnp.mean(gg * u, axis=1, keepdims=True)
            d = (gg - m1 - u * m2) * inverse[app][1 - n][rows, :]
            gh[rows, :] = d
            rounded = d.astype(BF)
            low[app, rows, :] = rounded
            for row, value in zip(rows_at, (rounded, g * u, g)):
                sums[row : row + 1, :] += total(value)

        tiles(tokens // TILE, tile)
        units.start()

    def tasks(app):
        base, unroll = turn * (1 - app), True if app else 1

        def du(t):
            s = weights.wait(base + t)
            k = slopes.wait(parts * (1 - app) + t)

            def tile(at):
                d = nt(r_down[app], weight[s, pl.ds(at, TILE), :])
                value = (d * slope_v[k, :, pl.ds(at, TILE)].astype(F32)).astype(BF)
                r_up[app, :, pl.ds(t * part + at, TILE)] = value
                sums[5 + t : 6 + t, pl.ds(at, TILE)] += total(value)

            tiles(part // TILE, tile, unroll)
            weights.start()
            slopes.start()

        def add(t, left_part, index):
            s = weights.wait(index)

            def tile(at):
                gh[:, pl.ds(at, TILE)] += nt(left_part(t), weight[s, pl.ds(at, TILE), :])

            tiles(width // TILE, tile, unroll)
            weights.start()

        def mixed():
            s = weights.wait(base + 2 * parts)

            def tile(at):
                do[:, pl.ds(at, TILE)] = nt(r_out[app], weight[s, pl.ds(at, TILE), :]).astype(BF)

            tiles(width // TILE, tile, unroll)
            weights.start()

        def one_pair(p):
            s = heads.wait(pairs * (1 - app) + p)
            at = lambda t: slice(t * width + p * pair, t * width + (p + 1) * pair)
            dq, dk, dv = attend_back_math(
                pair_v[s, 0], pair_v[s, 1], pair_v[s, 2], pair_v[s, 3], do[:, at(0)], lambda h: probs_v[s, h], scale
            )
            for t, value in enumerate((dq, dk, dv)):
                joined[app][:, at(t)] = value
            sums[0:1, at(0)] += total(dq)
            sums[1:2, at(0)] += total(dv)
            heads.start()

        early = [functools.partial(du, t) for t in range(parts)]
        early += [
            functools.partial(add, t, lambda t: r_up[app, :, t * part : (t + 1) * part], base + parts + t)
            for t in range(parts)
        ]
        middle = [lambda: norm_back(app, 1, lambda rows: gh[rows, :], r_out, 3, (2, 3, 4)), mixed]
        middle += [functools.partial(one_pair, p) for p in range(pairs)]
        late = [
            functools.partial(
                add, t, lambda t: joined[app][:, t * part : (t + 1) * part], base + 2 * parts + 1 + t
            )
            for t in range(n_mid)
        ]
        return early, middle, late

    def task_table():
        def tile(at):
            g = gh[:, pl.ds(at, TILE)]
            high = g.astype(BF)
            rest = (g - high.astype(F32)).astype(BF)
            sums[16:48, pl.ds(at, TILE)] += nn(entry_hot[...], high) + nn(entry_hot[...], rest)

        tiles(width // TILE, tile, 1)
        result.start()

    result = pltpu.make_async_copy(gh, g0, m_sem.at[1])
    for _ in range(2):
        weights.start()
        slopes.start()
        units.start()
        heads.start()
        left.start()
    engine = Engine(ndp, nf, chunks, refs[34:], source, target)
    sums[...] = jnp.zeros_like(sums)
    first_g.wait()
    last_rows = (5 + parts, 6 + parts, 7 + parts)
    norm_back(1, 0, lambda rows: r_out[0, rows, :].astype(F32), r_down, 6 + parts, last_rows)
    for group in tasks(1):
        for task in group:
            task()
    norm_back(0, 0, lambda rows: gh[rows, :], r_down, 6 + parts, last_rows)
    counts = [sum(c[0] == i for c in chunks) for i in range(5)]
    first = [sum(counts[:i]) for i in range(5)]
    early, middle, late = tasks(0)
    plan = {}

    def spread(group, begin, end):
        for n, task in enumerate(group):
            plan.setdefault(begin + n * (end - begin) // len(group), []).append(task)

    spread(early, 0, first[1])
    spread(middle, first[1], first[3] - 1)
    spread(late + [task_table], first[3], first[4])
    for t in range(engine.steps):
        engine.step(t)
        for task in plan.get(t, ()):
            task()
    engine.finish()
    result.wait()


SAVED = ("slope", "unit2", "unit1", "q", "k", "v", "o", "probs")


def tail(ndp, nf, collective_id, scale, full, cotangent, kept, vec, entry_hot):
    w_down, w_up, w_out, w_qkv = full
    tokens, width = cotangent.shape
    ff, extra = w_down.shape[0], 64
    shapes = (w_down.shape, w_up.shape, w_out.shape, w_qkv.shape, (nf * extra, width))
    chunks = chunk_list(ndp, nf, shapes, KINDS)
    half = nf // 2
    part = min(1024, width)
    pair = 2 * (width // HEADS)
    rn = chunks[0][3]
    lefts = [kept[app][name] for name in ("active", "hidden", "mixed", "low") for app in range(2)]
    if rn % 128:
        lefts = [t.T for t in lefts]
    big = list(full) + [cotangent] + lefts
    for app in range(2):
        big += [kept[app]["mixed" if name == "o" else name] for name in SAVED]
    little = [kept[app][name] for app in range(2) for name in ("inv1", "inv2")] + [vec, entry_hot]
    any_space = pl.BlockSpec(memory_space=pl.ANY)
    vmem = pl.BlockSpec(memory_space=pltpu.VMEM)
    return pl.pallas_call(
        functools.partial(tail_kernel, ndp, nf, shapes, chunks, scale),
        out_shape=[jax.ShapeDtypeStruct((r // nf, c), BF) for r, c in shapes]
        + [jax.ShapeDtypeStruct((tokens, width), F32)],
        in_specs=[any_space] * len(big) + [vmem] * len(little),
        out_specs=[any_space] * 6,
        scratch_shapes=[
            pltpu.VMEM((2, tokens, width), BF),
            pltpu.VMEM((2, tokens, ff), BF),
            pltpu.VMEM((2, tokens, width), BF),
            pltpu.VMEM((tokens, 3 * width), BF),
            pltpu.VMEM((tokens, 3 * width), BF),
            pltpu.VMEM((2, 2, nf, tokens, rn) if rn % 128 == 0 else (2, 2, nf, rn, tokens), BF),
            pltpu.VMEM((nf * rn, 2 * tokens), BF),
            pltpu.VMEM((STAGED, half, rn, chunks[0][4]), BF),
            pltpu.VMEM((tokens, width), F32),
            pltpu.VMEM((2, tokens, width), BF),
            pltpu.VMEM((2, part, width), BF),
            pltpu.VMEM((2, tokens, part), BF),
            pltpu.VMEM((2, 4, tokens, pair), BF),
            pltpu.VMEM((tokens, width), BF),
            pltpu.VMEM((2, 2, tokens, tokens), BF),
            pltpu.VMEM((extra, width), F32),
            pltpu.SemaphoreType.DMA((2, 1)),
            pltpu.SemaphoreType.DMA((2, 1)),
            pltpu.SemaphoreType.DMA((2, 5)),
            pltpu.SemaphoreType.DMA((2, 2 * nf)),
            pltpu.SemaphoreType.DMA((2, 1)),
            pltpu.SemaphoreType.DMA((2,)),
        ]
        + engine_scratch(ndp, nf, chunks),
        compiler_params=pltpu.CompilerParams(
            collective_id=collective_id, has_side_effects=True, vmem_limit_bytes=63 * 1024 * 1024
        ),
        name="tail",
    )(*big, *little)


def widen_kernel(*refs):
    keep, g0 = refs[:2]
    ins, token_grad, outs = refs[2:6], refs[6], refs[7:]
    token_grad[...] = g0[...] * keep[...]
    for source, target in zip(ins, outs):
        target[...] = source[...].astype(F32)


def widen(keep, g0, grads):
    arrays = [keep, g0, *grads]
    blocks = [pl.BlockSpec((t.shape[0] // 4, t.shape[1]), lambda n: (n, 0)) for t in arrays]
    return pl.pallas_call(
        widen_kernel,
        grid=(4,),
        in_specs=blocks,
        out_specs=blocks[1:],
        out_shape=[jax.ShapeDtypeStruct(t.shape, F32) for t in arrays[1:]],
        compiler_params=pltpu.CompilerParams(vmem_limit_bytes=60 * 1024 * 1024),
        name="widen",
    )(*arrays)


LAYER = ("low", "q", "k", "v", "mixed", "probs", "unit1", "inv1", "hidden", "active", "slope", "unit2", "inv2")


def head_kernel(ndp, nf, shapes, scale, *refs):
    n = len(shapes)
    ins, small = refs[:n], refs[n]
    tokens_ref, positions, counts, ids, table = refs[n + 1 : n + 6]
    refs = refs[n + 6 :]
    full_out, vec_out, final_out, keep_out, entry_out = refs[:n], refs[n], refs[n + 1], refs[n + 2], refs[n + 3]
    kept = [dict(zip(LAYER, refs[n + 4 + k * len(LAYER) :])) for k in range(2)]
    refs = refs[n + 4 + 2 * len(LAYER) :]
    full, refs = refs[:n], refs[n:]
    (
        small_all, vec, entries, keep, entry_hot, x, low, joined, mixed, hidden, active, slope, probs, unit, inv,
        send, recv, local, save_sem,
    ) = refs
    outs = full
    dp, me = lax.axis_index("dp"), lax.axis_index("fsdp")
    fbits = log2(nf)
    sibling = (dp, flip(me, 0))
    outer = [(dp, flip(me, b)) for b in range(1, fbits)]
    near = [(flip(dp, 0), me), (flip(dp, 1), me)]
    others = [(dp, lax.rem(me + d, nf)) for d in range(1, nf)]
    started, arrived, final_of = [], [], {i: [] for i in range(n)}
    own = []
    for i in range(n):
        r, c = shapes[i]
        copy = pltpu.make_async_copy(ins[i], full[i].at[pl.ds(pl.multiple_of(me * r, r), r)], local.at[i])
        copy.start()
        own.append(copy)
    own_small = pltpu.make_async_copy(small, small_all.at[me], local.at[n])
    own_small.start()
    entry_barrier(others + near)

    def push(src, dst, partner):
        k = len(started)
        copy = pltpu.make_async_remote_copy(src, dst, send.at[k], recv.at[k], device_id=partner, device_id_type=MESH)
        copy.start()
        started.append(copy)
        arrived.append(False)
        return k

    def arrive(k):
        if not arrived[k]:
            started[k].wait_recv()
            arrived[k] = True

    small_copies = [push(small, small_all.at[me], other) for other in others]

    def place(i, f, k, half, q):
        r, c = shapes[i]
        w = c // CUTS
        return full[i].at[pl.ds(pl.multiple_of(f * r + k * q, 16), q), pl.ds(half * w, w)]

    items = [(i, h) for i in range(n) for h in range(CUTS)]
    waits, known = {}, {}

    def share(i, where):
        final_of[i].append(push(where, where, sibling))

    def stage(t, s):
        i, half = items[t]
        r, c = shapes[i]
        w = c // CUTS
        lone = half % 4 == 3
        p1 = (half if half % 4 < 2 else i) % 2
        p2 = 1 - p1
        q, code = (r // 2, bit_of(dp, p1)) if lone else (r // 4, lax.rem(dp, 4))
        over = lambda k, bit: 1 - k if lone else flip(k, bit)
        src = ins[i].at[pl.ds(pl.multiple_of(code * q, 16), q), pl.ds(half * w, w)]
        at = lambda f, k: place(i, f, k, half, q)
        if s == 0:
            if fbits > 1:
                waits[t, "y", 1] = [(me, push(src, at(me, code), outer[0]))]
            whole = full[i].at[pl.ds(pl.multiple_of(me * r, r), r), pl.ds(half * w, w)]
            final_of[i].append(push(ins[i].at[:, pl.ds(half * w, w)], whole, sibling))
        elif s < fbits:
            got = []
            for f, copy in waits.pop((t, "y", s)):
                arrive(copy)
                got.append(flip(f, s))
            known.setdefault(t, []).extend(got)
            if s < fbits - 1:
                waits[t, "y", s + 1] = [(me, push(src, at(me, code), outer[s]))] + [
                    (f, push(at(f, code), at(f, code), outer[s])) for f in known[t]
                ]
            else:
                waits[t, "p1"] = [(f, push(at(f, code), at(f, code), near[p1])) for f in known[t]]
                waits[t, "p2a"] = [(f, push(at(f, code), at(f, code), near[p2])) for f in known[t] if not lone]
            for f in got:
                share(i, at(f, code))
        elif s == fbits:
            k = over(code, p1)
            waits[t, "p2b"] = []
            for f, copy in waits.pop((t, "p1")):
                arrive(copy)
                if not lone:
                    waits[t, "p2b"].append((f, push(at(f, k), at(f, k), near[p2])))
                share(i, at(f, k))
        else:
            k = over(code, p2) if s == fbits + 1 else over(over(code, p2), p1)
            for f, copy in waits.pop((t, "p2a" if s == fbits + 1 else "p2b")):
                arrive(copy)
                share(i, at(f, k))

    saves, pending = [], {}

    def save(name, src, dst):
        copy = pltpu.make_async_copy(src, dst, save_sem.at[len(saves)])
        copy.start()
        saves.append(copy)
        pending.setdefault(name, []).append(copy)

    def free(name):
        for copy in pending.pop(name, []):
            copy.wait()

    ready = set()

    def need(i):
        if i not in ready:
            ready.add(i)
            own[i].wait()
            for k in final_of[i]:
                arrive(k)
            save("full", full[i], full_out[i])

    tokens, width = x.shape
    part = min(1024, width)
    parts = shapes[2][1] // part
    pairs = HEADS // 2
    pair = width // pairs
    mine = width // nf

    def task_start():
        own_small.wait()
        for k in small_copies:
            arrive(k)
        row = 0
        for count in (2, 1, 1, 1, parts, 1, 1, 1):
            for f in range(nf):
                for i in range(count):
                    at = (f * count + i) * mine
                    vec[row + at // width : row + at // width + 1, at % width : at % width + mine] = small_all[
                        f, row + i : row + i + 1, :
                    ].astype(F32)
            row += count
        save("vec", vec, vec_out)
        entries[...] = jnp.zeros_like(entries)
        entries[: table.shape[0], :] = table[...]

        slots = positions.shape[1]
        used = (lax.broadcasted_iota(jnp.int32, (1, slots), 1) < counts[...]).astype(F32)
        places = lax.broadcasted_iota(jnp.int32, (tokens, slots), 0)
        hot = (places == positions[...]).astype(F32) * used
        hot_low = hot.astype(BF)
        entry_of = (lax.broadcasted_iota(jnp.int32, (32, slots), 0) == ids[...]).astype(F32).astype(BF)
        row_hot = nt(hot_low, entry_of).astype(BF)
        keep[...] = 1.0 - jnp.sum(hot, axis=1, keepdims=True)
        entry_hot[...] = nt(entry_of, hot_low).astype(BF)
        save("masks", keep, keep_out)
        save("masks", entry_hot, entry_out)
        x[...] = nn(row_hot, entries[...])

        def tile(at):
            rows = pl.ds(at, TILE)
            x0 = tokens_ref[rows, :].astype(F32) * keep[rows, :] + x[rows, :]
            x[rows, :] = x0
            low[rows, :] = x0.astype(BF)

        tiles(tokens // TILE, tile)
        save("low", low, kept[0]["low"])

    def task_joined(app, t):
        def run():
            need(0)
            free("qkv"[t])

            def tile(at):
                cols = pl.ds(t * width + at, TILE)
                value = nn(low[...], full[0][:, cols])
                if t == 0:
                    value = (value + vec[0:1, pl.ds(at, TILE)]) * scale
                if t == 2:
                    value = value + vec[1:2, pl.ds(at, TILE)]
                joined[:, cols] = value.astype(BF)

            tiles(width // TILE, tile)
            save("qkv"[t], joined.at[:, pl.ds(t * width, width)], kept[app]["qkv"[t]])
        return run

    def task_heads(app, p):
        def run():
            if p == 0:
                free("mixed")
            free(("probs", p % 2))
            at = lambda t: slice(t * width + p * pair, t * width + (p + 1) * pair)
            mixed[:, at(0)] = attend_math(joined[:, at(0)], joined[:, at(1)], joined[:, at(2)], probs.at[p % 2])
            save(("probs", p % 2), probs.at[p % 2], kept[app]["probs"].at[pl.ds(2 * p, 2)])
            if p == pairs - 1:
                save("mixed", mixed, kept[app]["mixed"])
        return run

    def norm(t, gain, shift):
        mean = jnp.mean(t, axis=1, keepdims=True)
        centred = t - mean
        spread = jnp.mean(centred * centred, axis=1, keepdims=True)
        inverse = lax.rsqrt(spread + EPSILON)
        normal = centred * inverse
        return normal * vec[gain : gain + 1, :] + vec[shift : shift + 1, :], normal.astype(BF), inverse

    def task_out(app):
        def run():
            need(1)
            free("hidden")
            free("unit1")
            free("inv1")

            def tile(at):
                rows = pl.ds(at, TILE)
                t = x[rows, :] + nn(mixed[rows, :], full[1][...]) + vec[2:3, :]
                h, unit[0, rows, :], inv[0, rows, :] = norm(t, 3, 4)
                x[rows, :] = h
                hidden[rows, :] = h.astype(BF)

            tiles(tokens // TILE, tile)
            save("unit1", unit.at[0], kept[app]["unit1"])
            save("inv1", inv.at[0], kept[app]["inv1"])
            save("hidden", hidden, kept[app]["hidden"])
        return run

    def task_up(app, t):
        def run():
            need(2)
            free(("active", t))
            free(("slope", t % 2))

            def tile(at):
                cols = pl.ds(t * part + at, TILE)
                u = nn(hidden[...], full[2][:, cols]) + vec[5 + t : 6 + t, pl.ds(at, TILE)]
                below = 0.5 + 0.5 * lax.erf(u * math.sqrt(0.5))
                active[:, cols] = (u * below).astype(BF)
                bell = math.sqrt(0.5 / math.pi) * jnp.exp(-0.5 * u * u)
                slope[t % 2, :, pl.ds(at, TILE)] = (below + u * bell).astype(BF)

            tiles(part // TILE, tile)
            cols = pl.ds(t * part, part)
            save(("active", t), active.at[:, cols], kept[app]["active"].at[:, cols])
            save(("slope", t % 2), slope.at[t % 2], kept[app]["slope"].at[:, cols])
        return run

    def task_down(app):
        def run():
            need(3)
            free("low")
            free("unit2")
            free("inv2")

            def tile(at):
                rows = pl.ds(at, TILE)
                t = x[rows, :] + nn(active[rows, :], full[3][...]) + vec[5 + parts : 6 + parts, :]
                y, unit[1, rows, :], inv[1, rows, :] = norm(t, 6 + parts, 7 + parts)
                x[rows, :] = y
                low[rows, :] = y.astype(BF)

            tiles(tokens // TILE, tile)
            save("unit2", unit.at[1], kept[app]["unit2"])
            save("inv2", inv.at[1], kept[app]["inv2"])
            save("low", low, final_out if app else kept[1]["low"])
        return run

    first = lambda app: [task_joined(app, t) for t in range(3)] + [task_heads(app, p) for p in range(pairs)] + [task_out(app)]
    second = lambda app: [task_up(app, t) for t in range(parts)]
    stages = fbits + 3
    ahead = 2
    steps = len(items) + SKEW * (stages - 1)
    done_at = lambda i: CUTS * (i + 1) - 1 + SKEW * (stages - 1)
    plan = {}

    def spread(tasks, begin, end):
        for k, task in enumerate(tasks):
            plan.setdefault(min(begin + k * (end - begin) // len(tasks), steps), []).append(task)

    spread([task_start], 0, 1)
    spread(first(0), done_at(0) + 1, done_at(2) + 1)
    spread(second(0), done_at(2) + 1, steps)
    spread([task_down(0)] + first(1) + second(1) + [task_down(1)], steps, steps)
    for step in range(-ahead, steps):
        for s in range(stages - 1, -1, -1):
            t = step - SKEW * s if s else step + ahead
            if 0 <= t < len(items):
                stage(t, s)
        for task in plan.get(step, ()):
            task()
    for task in plan[steps]:
        task()
    for copy in started:
        copy.wait_send()
    for k in range(len(started)):
        arrive(k)
    for name in list(pending):
        free(name)


def head(ndp, nf, collective_id, scale, shards, small, tokens, positions, counts, ids, table):
    shapes = tuple(s.shape for s in shards)
    length, width = tokens.shape
    ff = shapes[2][1]
    part = min(1024, width)
    kinds = dict(
        low=((length, width), BF), q=((length, width), BF), k=((length, width), BF), v=((length, width), BF),
        mixed=((length, width), BF), probs=((HEADS, length, length), BF), unit1=((length, width), BF),
        inv1=((length, 1), F32), hidden=((length, width), BF), active=((length, ff), BF), slope=((length, ff), BF),
        unit2=((length, width), BF), inv2=((length, 1), F32),
    )
    full = [(nf * r, c) for r, c in shapes]
    out_shape = [jax.ShapeDtypeStruct(s, BF) for s in full]
    out_shape += [jax.ShapeDtypeStruct((small.shape[0], width), F32), jax.ShapeDtypeStruct((length, width), BF)]
    out_shape += [jax.ShapeDtypeStruct((length, 1), F32), jax.ShapeDtypeStruct((32, length), BF)]
    out_shape += [jax.ShapeDtypeStruct(*kinds[name]) for _ in range(2) for name in LAYER]
    per_item = (nf // 2 - 1) * 8 + 1
    copies = nf - 1 + CUTS * len(shards) * per_item
    any_space = pl.BlockSpec(memory_space=pl.ANY)
    vmem = pl.BlockSpec(memory_space=pltpu.VMEM)
    outs = pl.pallas_call(
        functools.partial(head_kernel, ndp, nf, shapes, scale),
        out_shape=out_shape,
        in_specs=[any_space] * (len(shards) + 1) + [vmem] * 5,
        out_specs=[any_space] * len(out_shape),
        scratch_shapes=[pltpu.VMEM(s, BF) for s in full]
        + [
            pltpu.VMEM((nf,) + small.shape, BF),
            pltpu.VMEM((small.shape[0], width), F32),
            pltpu.VMEM((32, width), BF),
            pltpu.VMEM((length, 1), F32),
            pltpu.VMEM((32, length), BF),
            pltpu.VMEM((length, width), F32),
            pltpu.VMEM((length, width), BF),
            pltpu.VMEM((length, 3 * width), BF),
            pltpu.VMEM((length, width), BF),
            pltpu.VMEM((length, width), BF),
            pltpu.VMEM((length, ff), BF),
            pltpu.VMEM((2, length, part), BF),
            pltpu.VMEM((2, 2, length, length), BF),
            pltpu.VMEM((2, length, width), BF),
            pltpu.VMEM((2, length, 1), F32),
            pltpu.SemaphoreType.DMA((copies,)),
            pltpu.SemaphoreType.DMA((copies,)),
            pltpu.SemaphoreType.DMA((len(shards) + 1,)),
            pltpu.SemaphoreType.DMA((96,)),
        ],
        compiler_params=pltpu.CompilerParams(
            collective_id=collective_id, has_side_effects=True, vmem_limit_bytes=61 * 1024 * 1024
        ),
        name="head",
    )(*shards, small, tokens, positions, counts, ids, table)
    n = len(shards)
    kept = [dict(zip(LAYER, outs[n + 4 + k * len(LAYER) :])) for k in range(2)]
    return outs[:n], *outs[n : n + 4], kept


def shards(ndp, nf, tokens, mask_positions, mask_counts, replace_ids, cotangent, replace_table,
           w_qkv, b_qv, w_out, b_out, norm1_gain, norm1_bias, w_up, b_up, w_down, b_down, norm2_gain, norm2_bias):
    length, width = tokens.shape
    entries = replace_table.shape[0]
    mine = width // nf
    small = jnp.zeros((16 * mine,), BF)
    at = 0
    for vector in (b_qv, b_out, norm1_gain, norm1_bias, b_up, b_down, norm2_gain, norm2_bias):
        small = small + jnp.pad(vector, (at, 16 * mine - at - vector.shape[0]))
        at += vector.shape[0]
    small = small.reshape(16, mine)
    scale = 1.0 / math.sqrt(width // HEADS)
    (qkv, out, up, down), vec, final, keep, entry_hot, (kept_one, kept_two) = head(
        ndp, nf, 0, scale, [w_qkv, w_out, w_up, w_down], small, tokens,
        mask_positions, mask_counts.reshape(1, 1), replace_ids, replace_table,
    )
    grown = w_up.shape[1] // width
    g_down, g_up, g_out, g_qkv, extra, d_start = tail(
        ndp, nf, 1, scale, (down, up, out, qkv), cotangent, (kept_one, kept_two), vec, entry_hot
    )
    token_grad, g_down, g_up, g_out, g_qkv = widen(keep, d_start, (g_down, g_up, g_out, g_qkv))
    extra = extra.astype(F32)
    table_grad = extra[16 : 16 + entries]
    place = lax.axis_index("fsdp")
    mine = lambda t: lax.dynamic_slice_in_dim(t, place * (t.shape[0] // nf), t.shape[0] // nf)
    v = [mine(extra[:2].reshape(-1))] + [mine(extra[n]) for n in (2, 3, 4)]
    v += [mine(extra[5 : 5 + grown].reshape(-1))] + [mine(extra[n + grown]) for n in (5, 6, 7)]
    return (
        final, token_grad, table_grad, g_qkv, v[0], g_out, v[1], v[2], v[3],
        g_up, v[4], g_down, v[5], v[6], v[7],
    )


def solution(mesh):
    both = P(("dp", "fsdp"))
    rows = P("fsdp")
    in_specs = (both,) * 5 + (P(),) + (rows,) * 12
    out_specs = (both, both, P()) + (rows,) * 12
    body = functools.partial(shards, mesh.shape["dp"], mesh.shape["fsdp"])
    return jax.shard_map(body, mesh=mesh, in_specs=in_specs, out_specs=out_specs, check_vma=False)
```
